32 devices in a mesh: pair: 2 (over core), batch: 4 (over y, x), vocab: 4 (over z).
Axes of the slice: x: 2, y: 2, z: 4, core: 2. Of those that a mesh axis runs over, the one named last changes fastest.
Arguments:
- hidden: bfloat16 [2, 512, 8192], P('pair', 'batch', 'vocab'), may hold values from -120 to 120
- norm_gain: bfloat16 [8192], P('vocab'), may hold values from 0.099609375 to 1.8984375
- head_weight: bfloat16 [8192, 16384], P(('pair', 'batch'), 'vocab'), may hold values from -1 to 1
Outputs:
- guided_logprobs: float32 [512, 16384], P(('pair', 'batch'), 'vocab')
- cond_logprobs: float32 [512, 16384], P(('pair', 'batch'), 'vocab')
The draws below stay inside these ranges and needn't reach their ends.
All inputs are finite; a program needn't handle non-finite values.
Results may differ from the reference program's by a relative error of at most 0.007.
Values may be sent and summed in bfloat16 or wider, within the bound.
No kernel may reach another device: no remote copies, remote signals or barrier semaphores. Data moves between devices by JAX's collectives and lax.ppermute only.
A program may use at most 128 MiB of HBM per device.

```python
import math
import jax
import jax.numpy as jnp
from jax import lax

D = 8192
B = 512
V = 16384


def shared_pattern(key):
    return jnp.clip(jax.random.normal(jax.random.fold_in(key, 4242), (D,), jnp.float32), -4.0, 4.0)


def draw_hidden(key, part):
    first, second, third = jax.random.split(jax.random.fold_in(key, 11), 3)
    base = jnp.clip(jax.random.normal(first, (2, B, D), jnp.float32), -4.0, 4.0)
    top_ramp = 3.0
    row_scale = jnp.exp(jax.random.uniform(second, (2, B, 1), jnp.float32, math.log(0.3), math.log(3.0)))
    ramp = jnp.exp(math.log(top_ramp) * jnp.arange(D, dtype=jnp.float32) / (D - 1))
    col_scale = ramp * jnp.exp(jax.random.uniform(third, (D,), jnp.float32, 0.0, math.log(3.3)))
    values = base * row_scale * col_scale
    pattern = shared_pattern(key)
    chosen = jnp.array([0, B // 3, 2 * B // 3], jnp.int32)
    values = values.at[0, chosen, :].set(jnp.broadcast_to(2.0 * pattern, (3, D)))
    return values.astype(jnp.bfloat16)


def draw_head_weight(key, part):
    scale = 3.0 / math.sqrt(D)
    first = jax.random.fold_in(key, 23)
    values = jnp.clip(jax.random.normal(first, (D, V), jnp.float32), -4.0, 4.0) * scale
    pattern = shared_pattern(key) * (80.0 / D)
    strengths = [2.5, 1.8, 1.3]
    for place in range(3):
        column = place * (V // 3) + 5
        values = values.at[:, column].set(strengths[place] * pattern)
        values = values.at[:, column + 1].set((strengths[place] - 0.02) * pattern)
    return values.astype(jnp.bfloat16)


def setup_inputs(seed: int = 0) -> dict:
    keys = jax.random.split(jax.random.key(seed), 4)
    return {
        "hidden": draw_hidden(jax.random.fold_in(keys[3], 71), 0),
        "norm_gain": jnp.clip(1.0 + 0.18 * jax.random.normal(keys[1], (D,), jnp.float32), 0.099609375, 1.8984375).astype(jnp.bfloat16),
        "head_weight": draw_head_weight(jax.random.fold_in(keys[3], 71), 0),
    }


EPS = 1e-05
GUIDE = 1.5

def normalized(scores):
    peak = lax.optimization_barrier(jnp.max(scores, axis=1, keepdims=True))
    total = lax.optimization_barrier(jnp.sum(jnp.exp(scores - peak), axis=1, keepdims=True))
    return scores - (peak + jnp.log(total))

def reference(hidden, norm_gain, head_weight):
    wide = hidden.astype(jnp.float32)
    meansq = lax.optimization_barrier(jnp.mean(wide * wide, axis=2, keepdims=True))
    features = (wide * lax.rsqrt(meansq + EPS) * norm_gain.astype(jnp.float32)).astype(jnp.bfloat16)
    cond = jnp.dot(features[0], head_weight, preferred_element_type=jnp.float32)
    uncond = jnp.dot(features[1], head_weight, preferred_element_type=jnp.float32)
    guided = GUIDE * cond + (1.0 - GUIDE) * uncond
    return (normalized(guided), normalized(cond))
```

```python
import jax
import jax.numpy as jnp
from jax import lax
from jax.sharding import PartitionSpec as P

EPS = 1e-05
GUIDE = 1.5
CHUNKS = 4
SUM_TYPE = jnp.float16

X_SWAP = [(0, 1), (1, 0), (2, 3), (3, 2)]
Y_SWAP = [(0, 2), (2, 0), (1, 3), (3, 1)]
CORE_SWAP = [(0, 1), (1, 0)]


def pick(array, index, axis):
    return lax.dynamic_index_in_dim(array, index, axis, keepdims=False)


def in_order(mine, other, index, axis):
    first = jnp.where(index == 0, mine, other)
    second = jnp.where(index == 0, other, mine)
    return jnp.stack([first, second], axis=axis)


def on_device(hidden, norm_gain, head_weight):
    core = lax.axis_index("pair")
    place = lax.axis_index("batch")
    y, x = place // 2, place % 2
    vocab = lax.axis_size("vocab")
    rows = hidden[0]
    seg = rows.shape[0] // 2
    depth = rows.shape[1]
    block, columns = head_weight.shape
    width = columns // 2
    model = depth * vocab
    step = seg // CHUNKS

    halves = head_weight.reshape(block, 2, width)
    weight = in_order(
        pick(halves, core, 1),
        lax.ppermute(pick(halves, 1 - core, 1), "pair", CORE_SWAP),
        core,
        0,
    ).reshape(2 * block, width)

    wide = rows.astype(jnp.float32)
    gained = (wide * norm_gain.astype(jnp.float32)[None, :]).astype(jnp.bfloat16)
    squares = lax.all_gather(jnp.sum(wide * wide, axis=1), ("pair", "batch", "vocab"))
    total_sq = squares.reshape(2, 4, vocab, 2, seg).sum(axis=2)
    scale = lax.rsqrt(total_sq / model + EPS).reshape(2, 2, 2, 2, seg)

    if depth == 2 * block:
        parts = gained.reshape(2, seg, 2, block)
        mine = pick(parts, x, 2)
        other = lax.ppermute(pick(parts, 1 - x, 2), "batch", X_SWAP)
        shard = in_order(mine, other, x, 0)

    def features(c):
        if depth == 2 * block:
            piece = shard[:, :, c * step : (c + 1) * step]
            whole = lax.all_gather(piece, "vocab").reshape(2, 2, 2, 2, step, block)
            mine = pick(whole, y, 1)
            other = lax.ppermute(pick(whole, 1 - y, 1), "batch", Y_SWAP)
            branch = in_order(mine, other, y, 1)
        else:
            piece = gained.reshape(2, seg, depth)[:, c * step : (c + 1) * step]
            whole = lax.all_gather(piece, "vocab", axis=2, tiled=True)
            whole = whole.reshape(2, step, 2, 4, block).transpose(3, 2, 0, 1, 4)
            branch = lax.all_to_all(whole, "batch", split_axis=0, concat_axis=0)
            branch = branch.reshape(2, 2, 2, 2, step, block).transpose(2, 0, 1, 3, 4, 5)
        return in_order(branch, lax.ppermute(branch, "pair", CORE_SWAP), core, 0)

    def partial(feats, gain, j):
        left = pick(feats, j, 4).transpose(0, 2, 3, 4, 1, 5).reshape(-1, 2 * block)
        out = jnp.dot(left, weight, preferred_element_type=jnp.float32)
        return out.reshape(2, 2, 2, step, width) * pick(gain, j, 3)[..., None]

    def chunk(c):
        feats = features(c)
        gain = scale[..., c * step : (c + 1) * step]
        away = lax.ppermute(partial(feats, gain, 1 - x).astype(SUM_TYPE), "batch", X_SWAP)
        half = partial(feats, gain, x) + away.astype(jnp.float32)
        away = lax.ppermute(pick(half, 1 - y, 2).astype(SUM_TYPE), "batch", Y_SWAP)
        whole = pick(half, y, 2) + away.astype(jnp.float32)
        mine = pick(whole, core, 1).astype(SUM_TYPE)
        other = lax.ppermute(pick(whole, 1 - core, 1).astype(SUM_TYPE), "pair", CORE_SWAP)
        return in_order(mine, other, core, 2).reshape(2, step, columns)

    logits = jnp.concatenate([chunk(c) for c in range(CHUNKS)], axis=1).astype(jnp.float32)
    cond, uncond = logits[0], logits[1]
    guided = GUIDE * cond + (1.0 - GUIDE) * uncond

    def stats(values):
        peak = jnp.max(values, axis=1)
        return peak, jnp.sum(jnp.exp(values - peak[:, None]), axis=1)

    peak_c, sum_c = stats(cond)
    peak_g, sum_g = stats(guided)
    every = lax.all_gather(jnp.stack([peak_c, peak_g, sum_c, sum_g]), "vocab")
    top = jnp.max(every[:, :2], axis=0)
    total = jnp.sum(every[:, 2:] * jnp.exp(every[:, :2] - top[None]), axis=0)
    norm = top + jnp.log(total)
    return (guided - norm[1][:, None], cond - norm[0][:, None])


def solution(mesh):
    in_specs = (P("pair", "batch", "vocab"), P("vocab"), P(("pair", "batch"), "vocab"))
    out_specs = (P(("pair", "batch"), "vocab"), P(("pair", "batch"), "vocab"))
    return jax.shard_map(
        on_device, mesh=mesh, in_specs=in_specs, out_specs=out_specs, check_vma=False
    )
```

```python
import jax
import jax.numpy as jnp
from jax import lax
from jax.sharding import PartitionSpec as P

EPS = 1e-05
GUIDE = 1.5
CHUNKS = 4
SHRINK = 1.0 / 32.0
SUM_TYPE = jnp.float16

X_SWAP = [(0, 1), (1, 0), (2, 3), (3, 2)]
Y_SWAP = [(0, 2), (2, 0), (1, 3), (3, 1)]
CORE_SWAP = [(0, 1), (1, 0)]


def pick(array, index, axis):
    return lax.dynamic_index_in_dim(array, index, axis, keepdims=False)


def relative(array, index, axis):
    return jnp.where(index == 0, array, jnp.flip(array, axis))


def line_pairs(vocab, moves, hop=False):
    pairs = []
    for b in range(4):
        y = b // 2
        for start, end in moves:
            z = start if y == 0 else vocab - 1 - start
            if hop:
                pairs.append((b * vocab + z, (b ^ 2) * vocab + z))
            else:
                w = end if y == 0 else vocab - 1 - end
                pairs.append((b * vocab + z, b * vocab + w))
    return pairs


def on_device(hidden, norm_gain, head_weight):
    core = lax.axis_index("pair")
    place = lax.axis_index("batch")
    level = lax.axis_index("vocab")
    vocab = lax.axis_size("vocab")
    y, x = place // 2, place % 2
    rows = hidden[0]
    seg = rows.shape[0] // 2
    depth = rows.shape[1]
    block, columns = head_weight.shape
    width = columns // 2
    model = depth * vocab
    step = seg // CHUNKS

    wide = rows.astype(jnp.float32)
    gained = (wide * norm_gain.astype(jnp.float32)[None, :]).astype(jnp.bfloat16)

    keep = lax.dynamic_slice_in_dim(head_weight, core * width, width, 1)
    give = lax.dynamic_slice_in_dim(head_weight, (1 - core) * width, width, 1)
    take = lax.ppermute(give, "pair", CORE_SWAP)
    weight = jnp.concatenate([jnp.where(core == y, keep, take), jnp.where(core == y, take, keep)])

    squares = jnp.sum(wide * wide, axis=1)
    reach = 1
    while reach < vocab:
        squares += lax.ppermute(squares, "vocab", [(i, i ^ reach) for i in range(vocab)])
        reach *= 2
    squares = squares.reshape(2, seg)
    sent = [
        lax.ppermute(
            pick(squares, core ^ k, 0),
            ("pair", "batch"),
            [(4 * s + b, 2 * b + (s ^ k)) for s in range(2) for b in range(4)],
        )
        for k in range(2)
    ]
    total_sq = jnp.stack([jnp.where(x == 0, sent[0], sent[1]), jnp.where(x == 0, sent[1], sent[0])])
    scale = lax.rsqrt(total_sq / model + EPS) / SHRINK

    u = jnp.where(y == 0, level, vocab - 1 - level)

    def line(value, moves, hop=False):
        return lax.ppermute(value, ("batch", "vocab"), line_pairs(vocab, moves, hop))

    def line_features(c):
        piece = gained[:, :].reshape(2, seg, depth)[:, c * step : (c + 1) * step]
        mine = lax.dynamic_slice_in_dim(piece, x * block, block, 2)
        other = lax.ppermute(
            lax.dynamic_slice_in_dim(piece, (1 - x) * block, block, 2), "batch", X_SWAP
        )
        own = jnp.stack([mine, other])
        ahead = line(own, [(0, 1), (2, 3)])
        back = line(own, [(2, 1), (1, 0)])
        beside = line(own, [(1, 1), (3, 3)], hop=True)
        ahead_b = line(beside, [(0, 1)])
        back_b = line(beside, [(2, 1)])
        detour = line(back, [(0, 0)], hop=True)
        second = line(jnp.stack([ahead, ahead_b]), [(1, 2)])
        first = line(jnp.stack([back, back_b]), [(1, 0)])
        last = line(second, [(2, 3)])
        home = jnp.stack([own, beside])
        from_0 = jnp.where(
            u == 0, home, jnp.where(u == 1, jnp.stack([ahead, ahead_b]), jnp.where(u == 2, second, last))
        )
        from_2 = jnp.where(
            u == 2,
            home,
            jnp.where(u == 1, jnp.stack([back, back_b]), jnp.where(u == 0, first, jnp.stack([ahead, detour]))),
        )
        return jnp.stack([from_0, from_2], axis=4)

    def gathered_features(c):
        piece = gained.reshape(2, seg, depth)[:, c * step : (c + 1) * step]
        whole = lax.all_gather(piece, "vocab", axis=2, tiled=True)
        whole = whole.reshape(2, step, 2, 4, block).transpose(3, 0, 1, 2, 4)
        whole = lax.all_to_all(whole, "batch", split_axis=0, concat_axis=0)
        whole = whole.reshape(2, 2, 2, step, 2, block)
        return relative(relative(relative(whole, y, 0), x, 1), y, 4)

    features = line_features if depth == 2 * block and vocab == 4 else gathered_features

    def partial(left, low, high):
        lead = left.shape[:-2]
        out = jnp.dot(
            left.reshape(-1, 2 * block), weight[:, low:high], preferred_element_type=jnp.float32
        )
        return (out * SHRINK).reshape(*lead, high - low)

    def chunk(c):
        branch = features(c)
        branch = relative(relative(branch, x ^ y, 1), x, 2).transpose(1, 2, 0, 3, 4, 5)
        left = jnp.stack([branch, lax.ppermute(branch, "pair", CORE_SWAP)], axis=2)
        middle = width // 2
        away_x = lax.ppermute(partial(left[:, 1], 0, middle).astype(SUM_TYPE), "batch", X_SWAP)
        away_y = lax.ppermute(partial(left[1], middle, width).astype(SUM_TYPE), "batch", Y_SWAP)
        sum_x = partial(left[:, 0], 0, middle) + away_x.astype(jnp.float32)
        sum_y = partial(left[0], middle, width) + jnp.flip(away_y, 2).astype(jnp.float32)
        next_y = lax.ppermute(sum_x[1].astype(SUM_TYPE), "batch", Y_SWAP)
        next_x = lax.ppermute(sum_y[1].astype(SUM_TYPE), "batch", X_SWAP)
        whole = jnp.concatenate(
            [
                sum_x[0] + jnp.flip(next_y, 1).astype(jnp.float32),
                sum_y[0] + next_x.astype(jnp.float32),
            ],
            axis=-1,
        ).astype(SUM_TYPE)
        mine = pick(whole, core ^ y, 1)
        other = jnp.flip(lax.ppermute(pick(whole, 1 - (core ^ y), 1), "pair", CORE_SWAP), 0)
        return mine, other

    pieces = [chunk(c) for c in range(CHUNKS)]
    mine = jnp.concatenate([piece[0] for piece in pieces], axis=1)
    other = jnp.concatenate([piece[1] for piece in pieces], axis=1)
    logits = jnp.concatenate(
        [jnp.where(core == 0, mine, other), jnp.where(core == 0, other, mine)], axis=2
    )
    logits = relative(logits, core, 0).astype(jnp.float32) * scale[..., None]
    cond, uncond = logits[0], logits[1]
    guided = GUIDE * cond + (1.0 - GUIDE) * uncond

    def stats(values):
        peak = jnp.max(values, axis=1)
        return peak, jnp.sum(jnp.exp(values - peak[:, None]), axis=1)

    peak_c, sum_c = stats(cond)
    peak_g, sum_g = stats(guided)
    own = jnp.stack([peak_c, peak_g, sum_c, sum_g])
    every = jnp.stack(
        [own]
        + [
            lax.ppermute(own, "vocab", [(i, (i + k) % vocab) for i in range(vocab)])
            for k in range(1, vocab)
        ]
    )
    top = jnp.max(every[:, :2], axis=0)
    total = jnp.sum(every[:, 2:] * jnp.exp(every[:, :2] - top[None]), axis=0)
    norm = top + jnp.log(total)
    return (guided - norm[1][:, None], cond - norm[0][:, None])


def solution(mesh):
    in_specs = (P("pair", "batch", "vocab"), P("vocab"), P(("pair", "batch"), "vocab"))
    out_specs = (P(("pair", "batch"), "vocab"), P(("pair", "batch"), "vocab"))
    return jax.shard_map(
        on_device, mesh=mesh, in_specs=in_specs, out_specs=out_specs, check_vma=False
    )
```

```python
import jax
import jax.numpy as jnp
from jax import lax
from jax.sharding import PartitionSpec as P

EPS = 1e-05
GUIDE = 1.5
CHUNKS = 2
SHRINK = 1.0 / 32.0
SUM_TYPE = jnp.float16

X_SWAP = [(0, 1), (1, 0), (2, 3), (3, 2)]
Y_SWAP = [(0, 2), (2, 0), (1, 3), (3, 1)]
CORE_SWAP = [(0, 1), (1, 0)]


def pick(array, index, axis):
    return lax.dynamic_index_in_dim(array, index, axis, keepdims=False)


def after(value, *others):
    return lax.optimization_barrier((value, *others))[0]


def on_device(hidden, norm_gain, head_weight):
    core = lax.axis_index("pair")
    place = lax.axis_index("batch")
    level = lax.axis_index("vocab")
    vocab = lax.axis_size("vocab")
    y, x = place // 2, place % 2
    rows = hidden[0]
    seg = rows.shape[0] // 2
    depth = rows.shape[1]
    block, columns = head_weight.shape
    width = columns // 2
    model = depth * vocab
    step = seg // CHUNKS

    wide = rows.astype(jnp.float32)
    gained = (wide * norm_gain.astype(jnp.float32)[None, :]).astype(jnp.bfloat16)
    gained = gained.reshape(2, seg, depth)

    diagonal = [
        pair
        for b in range(2)
        for z in range(1, vocab, 2)
        for pair in (
            (b * vocab + z, (b + 2) * vocab + z - 1),
            ((b + 2) * vocab + z - 1, b * vocab + z),
        )
    ]

    def line_features(c):
        piece = gained[:, c * step : (c + 1) * step]
        mine = lax.dynamic_slice_in_dim(piece, x * block, block, 2)
        other = lax.ppermute(
            lax.dynamic_slice_in_dim(piece, (1 - x) * block, block, 2), "batch", X_SWAP
        )
        own = jnp.stack([jnp.where(x == 0, mine, other), jnp.where(x == 0, other, mine)])
        moved = lax.ppermute(own, ("batch", "vocab"), diagonal)
        held = jnp.where((level + y) % 2 == 1, moved, own)
        whole = lax.all_gather(held.reshape(-1, block), "vocab", axis=0, tiled=True)
        return whole.reshape(2, 2, 2, 2, step, block), other, held

    def gathered_features(c):
        piece = gained[:, c * step : (c + 1) * step]
        whole = lax.all_gather(piece, "vocab", axis=2, tiled=True)
        whole = whole.reshape(2, step, 2, 4, block).transpose(3, 2, 0, 1, 4)
        whole = lax.all_to_all(whole, "batch", split_axis=0, concat_axis=0)
        whole = whole.reshape(2, 2, 2, 2, step, block).transpose(2, 0, 1, 3, 4, 5)
        return whole, piece, piece

    features = line_features if depth == 2 * block and vocab == 4 else gathered_features
    found = [features(c) for c in range(CHUNKS)]

    side = after(core, found[0][1])
    give = lax.dynamic_slice_in_dim(head_weight, (1 - side) * width, width, 1)
    take = lax.ppermute(give, "pair", CORE_SWAP)
    keep = lax.dynamic_slice_in_dim(head_weight, side * width, width, 1)

    squares = jnp.sum(wide * wide, axis=1)
    reach = 1
    while reach < vocab:
        squares += lax.ppermute(squares, "vocab", [(i, i ^ reach) for i in range(vocab)])
        reach *= 2
    squares = squares.reshape(2, seg)
    sent = [
        lax.ppermute(
            pick(squares, core ^ k, 0),
            ("pair", "batch"),
            [(4 * s + b, 2 * b + (s ^ k)) for s in range(2) for b in range(4)],
        )
        for k in range(2)
    ]
    total_sq = jnp.stack([jnp.where(x == 0, sent[0], sent[1]), jnp.where(x == 0, sent[1], sent[0])])
    scale = lax.rsqrt(total_sq / model + EPS) / SHRINK

    def partial(left, low, high):
        lead = left.shape[1:-1]
        out = jnp.dot(
            pick(left, core, 0).reshape(-1, block),
            keep[:, low:high],
            preferred_element_type=jnp.float32,
        ) + jnp.dot(
            pick(left, 1 - core, 0).reshape(-1, block),
            take[:, low:high],
            preferred_element_type=jnp.float32,
        )
        return (out * SHRINK).reshape(*lead, high - low)

    def reduced(left):
        middle = width // 2
        away_x = lax.ppermute(
            partial(pick(left, 1 - x, 3), 0, middle).astype(SUM_TYPE), "batch", X_SWAP
        )
        away_y = lax.ppermute(
            partial(pick(left, 1 - y, 2), middle, width).astype(SUM_TYPE), "batch", Y_SWAP
        )
        sum_x = partial(pick(left, x, 3), 0, middle) + away_x.astype(jnp.float32)
        sum_y = partial(pick(left, y, 2), middle, width) + away_y.astype(jnp.float32)
        next_y = lax.ppermute(pick(sum_x, 1 - y, 1).astype(SUM_TYPE), "batch", Y_SWAP)
        next_x = lax.ppermute(pick(sum_y, 1 - x, 1).astype(SUM_TYPE), "batch", X_SWAP)
        return jnp.concatenate(
            [
                pick(sum_x, y, 1) + next_y.astype(jnp.float32),
                pick(sum_y, x, 1) + next_x.astype(jnp.float32),
            ],
            axis=-1,
        ).astype(SUM_TYPE)

    def chunk(c, *earlier):
        ready = [found[c + 1][2]] if c + 1 < CHUNKS else []
        own = after(found[c][0], *earlier, *ready)
        other = lax.ppermute(own, "pair", CORE_SWAP)
        sums = jnp.stack([reduced(own), reduced(other)])
        return pick(sums, core, 1), lax.ppermute(pick(sums, 1 - core, 1), "pair", CORE_SWAP)

    pieces = [chunk(0)]
    for c in range(1, CHUNKS):
        pieces.append(chunk(c, *pieces[-1]))
    mine = jnp.concatenate([piece[0] for piece in pieces], axis=1)
    theirs = jnp.concatenate([piece[1] for piece in pieces], axis=1)

    def scores(own, other, got_own, got_other, gain):
        low = jnp.where(core == 0, own, got_own)
        high = jnp.where(core == 0, got_other, other)
        return jnp.concatenate([low, high], axis=1).astype(jnp.float32) * gain[:, None]

    cond = scores(mine[0], mine[1], theirs[0], theirs[1], scale[0])
    uncond = scores(mine[1], mine[0], theirs[1], theirs[0], scale[1])
    guided = GUIDE * cond + (1.0 - GUIDE) * uncond

    def stats(values):
        peak = jnp.max(values, axis=1)
        return peak, jnp.sum(jnp.exp(values - peak[:, None]), axis=1)

    peak_c, sum_c = stats(cond)
    peak_g, sum_g = stats(guided)
    own = jnp.stack([peak_c, peak_g, sum_c, sum_g])
    every = jnp.stack(
        [own]
        + [
            lax.ppermute(own, "vocab", [(i, (i + k) % vocab) for i in range(vocab)])
            for k in range(1, vocab)
        ]
    )
    top = jnp.max(every[:, :2], axis=0)
    total = jnp.sum(every[:, 2:] * jnp.exp(every[:, :2] - top[None]), axis=0)
    norm = top + jnp.log(total)
    return (guided - norm[1][:, None], cond - norm[0][:, None])


def solution(mesh):
    in_specs = (P("pair", "batch", "vocab"), P("vocab"), P(("pair", "batch"), "vocab"))
    out_specs = (P(("pair", "batch"), "vocab"), P(("pair", "batch"), "vocab"))
    return jax.shard_map(
        on_device, mesh=mesh, in_specs=in_specs, out_specs=out_specs, check_vma=False
    )
```

```python
import jax
import jax.numpy as jnp
from jax import lax
from jax.sharding import PartitionSpec as P

EPS = 1e-05
GUIDE = 1.5
CHUNKS = 2
SHRINK = 1.0 / 32.0
SUM_TYPE = jnp.float16

X_SWAP = [(0, 1), (1, 0), (2, 3), (3, 2)]
Y_SWAP = [(0, 2), (2, 0), (1, 3), (3, 1)]
CORE_SWAP = [(0, 1), (1, 0)]


def pick(array, index, axis):
    return lax.dynamic_index_in_dim(array, index, axis, keepdims=False)


def after(value, *others):
    return lax.optimization_barrier((value, *others))[0]


def on_device(hidden, norm_gain, head_weight):
    core = lax.axis_index("pair")
    place = lax.axis_index("batch")
    level = lax.axis_index("vocab")
    vocab = lax.axis_size("vocab")
    y, x = place // 2, place % 2
    rows = hidden[0]
    seg = rows.shape[0] // 2
    depth = rows.shape[1]
    block, columns = head_weight.shape
    width = columns // 2
    model = depth * vocab
    step = seg // CHUNKS

    wide = rows.astype(jnp.float32)
    gained = (wide * norm_gain.astype(jnp.float32)[None, :]).astype(jnp.bfloat16)
    gained = gained.reshape(2, seg, depth)

    diagonal = [
        pair
        for b in range(2)
        for z in range(1, vocab, 2)
        for pair in (
            (b * vocab + z, (b + 2) * vocab + z - 1),
            ((b + 2) * vocab + z - 1, b * vocab + z),
        )
    ]

    def line_features():
        pieces = [gained[:, c * step : (c + 1) * step] for c in range(CHUNKS)]
        sides = [lax.dynamic_slice_in_dim(piece, (1 - x) * block, block, 2) for piece in pieces]
        sides = [lax.ppermute(side, "batch", X_SWAP) for side in sides]
        held = []
        for piece, other in zip(pieces, sides):
            mine = lax.dynamic_slice_in_dim(piece, x * block, block, 2)
            own = jnp.stack([jnp.where(x == 0, mine, other), jnp.where(x == 0, other, mine)])
            moved = lax.ppermute(own, ("batch", "vocab"), diagonal)
            held.append(jnp.where((level + y) % 2 == 1, moved, own))

        wholes = []
        for own in held:
            below, above = [own], [own]
            for k in range(1, vocab):
                below.append(
                    lax.ppermute(below[-1], "vocab", [(z, z + 1) for z in range(k - 1, vocab - 1)])
                )
                above.append(
                    lax.ppermute(above[-1], "vocab", [(z + 1, z) for z in range(vocab - k)])
                )
            ordered = []
            for z in range(vocab):
                part = own
                for k in range(1, vocab):
                    if z + k < vocab:
                        part = jnp.where(level == z + k, below[k], part)
                    if z - k >= 0:
                        part = jnp.where(level == z - k, above[k], part)
                ordered.append(part)
            wholes.append(jnp.stack(ordered).reshape(2, 2, 2, 2, step, block))
        return wholes, held, sides[0]

    def gathered_features():
        wholes = []
        for c in range(CHUNKS):
            piece = gained[:, c * step : (c + 1) * step]
            whole = lax.all_gather(piece, "vocab", axis=2, tiled=True)
            whole = whole.reshape(2, step, 2, 4, block).transpose(3, 2, 0, 1, 4)
            whole = lax.all_to_all(whole, "batch", split_axis=0, concat_axis=0)
            wholes.append(whole.reshape(2, 2, 2, 2, step, block).transpose(2, 0, 1, 3, 4, 5))
        return wholes, wholes, gained

    lined = depth == 2 * block and vocab == 4
    found, held, begun = line_features() if lined else gathered_features()

    give = lax.dynamic_slice_in_dim(head_weight, (1 - core) * width, width, 1)
    take = lax.ppermute(give, "pair", CORE_SWAP)
    side = after(core, begun)
    keep = lax.optimization_barrier(lax.dynamic_slice_in_dim(head_weight, side * width, width, 1))

    squares = jnp.sum(wide * wide, axis=1)
    squares = after(squares, begun)
    reach = 1
    while reach < vocab:
        squares += lax.ppermute(squares, "vocab", [(i, i ^ reach) for i in range(vocab)])
        reach *= 2
    squares = squares.reshape(2, seg)
    sent = [
        lax.ppermute(
            pick(squares, core ^ k, 0),
            ("pair", "batch"),
            [(4 * s + b, 2 * b + (s ^ k)) for s in range(2) for b in range(4)],
        )
        for k in range(2)
    ]
    total_sq = jnp.stack([jnp.where(x == 0, sent[0], sent[1]), jnp.where(x == 0, sent[1], sent[0])])
    scale = lax.rsqrt(total_sq / model + EPS) / SHRINK

    def partial(left, low, high):
        lead = left.shape[1:-1]
        out = jnp.dot(
            pick(left, core, 0).reshape(-1, block),
            keep[:, low:high],
            preferred_element_type=jnp.float32,
        ) + jnp.dot(
            pick(left, 1 - core, 0).reshape(-1, block),
            take[:, low:high],
            preferred_element_type=jnp.float32,
        )
        return (out * SHRINK).reshape(*lead, high - low)

    def reduced(left):
        middle = width // 2
        away_x = lax.ppermute(
            partial(pick(left, 1 - x, 3), 0, middle).astype(SUM_TYPE), "batch", X_SWAP
        )
        away_y = lax.ppermute(
            partial(pick(left, 1 - y, 2), middle, width).astype(SUM_TYPE), "batch", Y_SWAP
        )
        sum_x = partial(pick(left, x, 3), 0, middle) + away_x.astype(jnp.float32)
        sum_y = partial(pick(left, y, 2), middle, width) + away_y.astype(jnp.float32)
        next_y = lax.ppermute(pick(sum_x, 1 - y, 1).astype(SUM_TYPE), "batch", Y_SWAP)
        next_x = lax.ppermute(pick(sum_y, 1 - x, 1).astype(SUM_TYPE), "batch", X_SWAP)
        return jnp.concatenate(
            [
                pick(sum_x, y, 1) + next_y.astype(jnp.float32),
                pick(sum_y, x, 1) + next_x.astype(jnp.float32),
            ],
            axis=-1,
        ).astype(SUM_TYPE)

    def chunk(c, *earlier):
        own = after(found[c], *earlier)
        other = lax.ppermute(own, "pair", CORE_SWAP)
        sums = jnp.stack([reduced(own), reduced(other)])
        return pick(sums, core, 1), lax.ppermute(pick(sums, 1 - core, 1), "pair", CORE_SWAP)

    pieces = [chunk(0)]
    for c in range(1, CHUNKS):
        pieces.append(chunk(c, *pieces[-1]))
    mine = jnp.concatenate([piece[0] for piece in pieces], axis=1)
    theirs = jnp.concatenate([piece[1] for piece in pieces], axis=1)

    def scores(own, other, got_own, got_other, gain):
        low = jnp.where(core == 0, own, got_own)
        high = jnp.where(core == 0, got_other, other)
        return jnp.concatenate([low, high], axis=1).astype(jnp.float32) * gain[:, None]

    cond = scores(mine[0], mine[1], theirs[0], theirs[1], scale[0])
    uncond = scores(mine[1], mine[0], theirs[1], theirs[0], scale[1])
    guided = GUIDE * cond + (1.0 - GUIDE) * uncond

    def stats(values):
        peak = jnp.max(values, axis=1)
        return peak, jnp.sum(jnp.exp(values - peak[:, None]), axis=1)

    peak_c, sum_c = stats(cond)
    peak_g, sum_g = stats(guided)
    own = jnp.stack([peak_c, peak_g, sum_c, sum_g])
    every = jnp.stack(
        [own]
        + [
            lax.ppermute(own, "vocab", [(i, (i + k) % vocab) for i in range(vocab)])
            for k in range(1, vocab)
        ]
    )
    top = jnp.max(every[:, :2], axis=0)
    total = jnp.sum(every[:, 2:] * jnp.exp(every[:, :2] - top[None]), axis=0)
    norm = top + jnp.log(total)
    return (guided - norm[1][:, None], cond - norm[0][:, None])


def solution(mesh):
    in_specs = (P("pair", "batch", "vocab"), P("vocab"), P(("pair", "batch"), "vocab"))
    out_specs = (P(("pair", "batch"), "vocab"), P(("pair", "batch"), "vocab"))
    return jax.shard_map(
        on_device, mesh=mesh, in_specs=in_specs, out_specs=out_specs, check_vma=False
    )
```

```python
import jax
import jax.numpy as jnp
from jax import lax
from jax.experimental import pallas as pl
from jax.experimental.pallas import tpu as pltpu
from jax.sharding import PartitionSpec as P

EPS = 1e-05
GUIDE = 1.5
CHUNKS = 2
SHRINK = 1.0 / 32.0
SUM_TYPE = jnp.float16
TILE = 512

X_SWAP = [(0, 1), (1, 0), (2, 3), (3, 2)]
Y_SWAP = [(0, 2), (2, 0), (1, 3), (3, 1)]
CORE_SWAP = [(0, 1), (1, 0)]


def pick(array, index, axis):
    return lax.dynamic_index_in_dim(array, index, axis, keepdims=False)


def after(value, *others):
    return lax.optimization_barrier((value, *others))[0]


def logits_kernel(core_ref, left_ref, keep_ref, take_ref, out_ref):
    core = core_ref[0]
    out = jnp.dot(left_ref[core], keep_ref[...], preferred_element_type=jnp.float32)
    out += jnp.dot(left_ref[1 - core], take_ref[...], preferred_element_type=jnp.float32)
    out_ref[...] = out * SHRINK


def partial_logits(core, left, head_weight, take):
    _, rows, block = left.shape
    width = take.shape[1]
    tile = min(TILE, width)
    tiles = width // tile
    return pl.pallas_call(
        logits_kernel,
        grid_spec=pltpu.PrefetchScalarGridSpec(
            num_scalar_prefetch=1,
            grid=(tiles,),
            in_specs=[
                pl.BlockSpec((2, rows, block), lambda t, core: (0, 0, 0)),
                pl.BlockSpec((block, tile), lambda t, core: (0, core[0] * tiles + t)),
                pl.BlockSpec((block, tile), lambda t, core: (0, t)),
            ],
            out_specs=pl.BlockSpec((rows, tile), lambda t, core: (0, t)),
        ),
        out_shape=jax.ShapeDtypeStruct((rows, width), jnp.float32),
        compiler_params=pltpu.CompilerParams(vmem_limit_bytes=24 * 1024 * 1024),
        cost_estimate=pl.CostEstimate(
            flops=4 * rows * block * width,
            bytes_accessed=4 * block * width + 4 * rows * block + 4 * rows * width,
            transcendentals=0,
        ),
    )(core.reshape(1).astype(jnp.int32), left, head_weight, take)


def on_device(hidden, norm_gain, head_weight):
    core = lax.axis_index("pair")
    place = lax.axis_index("batch")
    level = lax.axis_index("vocab")
    vocab = lax.axis_size("vocab")
    y, x = place // 2, place % 2
    rows = hidden[0]
    seg = rows.shape[0] // 2
    depth = rows.shape[1]
    block, columns = head_weight.shape
    width = columns // 2
    model = depth * vocab
    step = seg // CHUNKS

    wide = rows.astype(jnp.float32)
    gained = (wide * norm_gain.astype(jnp.float32)[None, :]).astype(jnp.bfloat16)
    gained = gained.reshape(2, seg, depth)

    diagonal = [
        pair
        for b in range(2)
        for z in range(1, vocab, 2)
        for pair in (
            (b * vocab + z, (b + 2) * vocab + z - 1),
            ((b + 2) * vocab + z - 1, b * vocab + z),
        )
    ]

    def line_features():
        pieces = [gained[:, c * step : (c + 1) * step] for c in range(CHUNKS)]
        sides = [lax.dynamic_slice_in_dim(piece, (1 - x) * block, block, 2) for piece in pieces]
        sides = [lax.ppermute(side, "batch", X_SWAP) for side in sides]
        held = []
        for piece, other in zip(pieces, sides):
            mine = lax.dynamic_slice_in_dim(piece, x * block, block, 2)
            own = jnp.stack([jnp.where(x == 0, mine, other), jnp.where(x == 0, other, mine)])
            if held:
                own = after(own, held[-1])
            else:
                begun = own
            moved = lax.ppermute(own, ("batch", "vocab"), diagonal)
            held.append(jnp.where((level + y) % 2 == 1, moved, own))

        wholes = []
        for own in held:
            below, above = [own], [own]
            for k in range(1, vocab):
                below.append(
                    lax.ppermute(below[-1], "vocab", [(z, z + 1) for z in range(k - 1, vocab - 1)])
                )
                above.append(
                    lax.ppermute(above[-1], "vocab", [(z + 1, z) for z in range(vocab - k)])
                )
            ordered = []
            for z in range(vocab):
                part = own
                for k in range(1, vocab):
                    if z + k < vocab:
                        part = jnp.where(level == z + k, below[k], part)
                    if z - k >= 0:
                        part = jnp.where(level == z - k, above[k], part)
                ordered.append(part)
            wholes.append(jnp.stack(ordered).reshape(2, 2, 2, 2, step, block))
        return wholes, held, begun

    def gathered_features():
        wholes = []
        for c in range(CHUNKS):
            piece = gained[:, c * step : (c + 1) * step]
            whole = lax.all_gather(piece, "vocab", axis=2, tiled=True)
            whole = whole.reshape(2, step, 2, 4, block).transpose(3, 2, 0, 1, 4)
            whole = lax.all_to_all(whole, "batch", split_axis=0, concat_axis=0)
            wholes.append(whole.reshape(2, 2, 2, 2, step, block).transpose(2, 0, 1, 3, 4, 5))
        return wholes, wholes, gained

    lined = depth == 2 * block and vocab == 4
    found, held, begun = line_features() if lined else gathered_features()

    side = after(core, begun)
    give = lax.dynamic_slice_in_dim(head_weight, (1 - side) * width, width, 1)
    take = lax.ppermute(give, "pair", CORE_SWAP)

    squares = jnp.sum(wide * wide, axis=1)
    squares = after(squares, held[-1])
    reach = 1
    while reach < vocab:
        squares += lax.ppermute(squares, "vocab", [(i, i ^ reach) for i in range(vocab)])
        reach *= 2
    squares = squares.reshape(2, seg)
    sent = [
        lax.ppermute(
            pick(squares, core ^ k, 0),
            ("pair", "batch"),
            [(4 * s + b, 2 * b + (s ^ k)) for s in range(2) for b in range(4)],
        )
        for k in range(2)
    ]
    total_sq = jnp.stack([jnp.where(x == 0, sent[0], sent[1]), jnp.where(x == 0, sent[1], sent[0])])
    scale = lax.rsqrt(total_sq / model + EPS) / SHRINK

    def reduced(left):
        middle = width // 2
        parts = partial_logits(core, left.reshape(2, -1, block), head_weight, take)
        parts = parts.reshape(2, 2, 2, step, width)
        low, high = parts[..., :middle], parts[..., middle:]
        away_x = lax.ppermute(pick(low, 1 - x, 2).astype(SUM_TYPE), "batch", X_SWAP)
        away_y = lax.ppermute(pick(high, 1 - y, 1).astype(SUM_TYPE), "batch", Y_SWAP)
        sum_x = pick(low, x, 2) + away_x.astype(jnp.float32)
        sum_y = pick(high, y, 1) + away_y.astype(jnp.float32)
        next_y = lax.ppermute(pick(sum_x, 1 - y, 1).astype(SUM_TYPE), "batch", Y_SWAP)
        next_x = lax.ppermute(pick(sum_y, 1 - x, 1).astype(SUM_TYPE), "batch", X_SWAP)
        return jnp.concatenate(
            [
                pick(sum_x, y, 1) + next_y.astype(jnp.float32),
                pick(sum_y, x, 1) + next_x.astype(jnp.float32),
            ],
            axis=-1,
        ).astype(SUM_TYPE)

    def chunk(c, *earlier):
        own = after(found[c], *earlier)
        other = lax.ppermute(own, "pair", CORE_SWAP)
        sums = jnp.stack([reduced(own), reduced(other)])
        return pick(sums, core, 1), lax.ppermute(pick(sums, 1 - core, 1), "pair", CORE_SWAP)

    pieces = [chunk(0)]
    for c in range(1, CHUNKS):
        pieces.append(chunk(c, *pieces[-1]))
    mine = jnp.concatenate([piece[0] for piece in pieces], axis=1)
    theirs = jnp.concatenate([piece[1] for piece in pieces], axis=1)

    def scores(own, other, got_own, got_other, gain):
        low = jnp.where(core == 0, own, got_own)
        high = jnp.where(core == 0, got_other, other)
        return jnp.concatenate([low, high], axis=1).astype(jnp.float32) * gain[:, None]

    cond = scores(mine[0], mine[1], theirs[0], theirs[1], scale[0])
    uncond = scores(mine[1], mine[0], theirs[1], theirs[0], scale[1])
    guided = GUIDE * cond + (1.0 - GUIDE) * uncond

    def stats(values):
        peak = jnp.max(values, axis=1)
        return peak, jnp.sum(jnp.exp(values - peak[:, None]), axis=1)

    peak_c, sum_c = stats(cond)
    peak_g, sum_g = stats(guided)
    own = jnp.stack([peak_c, peak_g, sum_c, sum_g])
    every = jnp.stack(
        [own]
        + [
            lax.ppermute(own, "vocab", [(i, (i + k) % vocab) for i in range(vocab)])
            for k in range(1, vocab)
        ]
    )
    top = jnp.max(every[:, :2], axis=0)
    total = jnp.sum(every[:, 2:] * jnp.exp(every[:, :2] - top[None]), axis=0)
    norm = top + jnp.log(total)
    return (guided - norm[1][:, None], cond - norm[0][:, None])


def solution(mesh):
    in_specs = (P("pair", "batch", "vocab"), P("vocab"), P(("pair", "batch"), "vocab"))
    out_specs = (P(("pair", "batch"), "vocab"), P(("pair", "batch"), "vocab"))
    return jax.shard_map(
        on_device, mesh=mesh, in_specs=in_specs, out_specs=out_specs, check_vma=False
    )
```

```python
import jax
import jax.numpy as jnp
from jax import lax
from jax.experimental import pallas as pl
from jax.experimental.pallas import tpu as pltpu
from jax.sharding import PartitionSpec as P

EPS = 1e-05
GUIDE = 1.5
CHUNKS = 2
SHRINK = 1.0 / 32.0
SUM_TYPE = jnp.float16
TILE = 512

X_SWAP = [(0, 1), (1, 0), (2, 3), (3, 2)]
Y_SWAP = [(0, 2), (2, 0), (1, 3), (3, 1)]
CORE_SWAP = [(0, 1), (1, 0)]


def pick(array, index, axis):
    return lax.dynamic_index_in_dim(array, index, axis, keepdims=False)


def after(value, *others):
    return lax.optimization_barrier((value, *others))[0]


def logits_kernel(place_ref, left_ref, weight_ref, take_ref, out_ref):
    side, own = place_ref[0], place_ref[1]
    width = out_ref.shape[1]
    tile = min(TILE, width)

    @pl.loop(0, width // tile)
    def _(t):
        here = pl.ds(pl.multiple_of(t * tile, tile), tile)
        there = pl.ds(pl.multiple_of(side * width + t * tile, tile), tile)
        out = jnp.dot(left_ref[own], weight_ref[:, there], preferred_element_type=jnp.float32)
        out += jnp.dot(left_ref[1 - own], take_ref[:, there], preferred_element_type=jnp.float32)
        out_ref[:, here] = out * SHRINK


def partial_logits(core, own, left, head_weight, take):
    _, rows, block = left.shape
    width = take.shape[1] // 2
    whole = pl.BlockSpec(memory_space=pltpu.VMEM)
    return pl.pallas_call(
        logits_kernel,
        in_specs=[pl.BlockSpec(memory_space=pltpu.SMEM), whole, whole, whole],
        out_specs=whole,
        out_shape=jax.ShapeDtypeStruct((rows, width), jnp.float32),
        compiler_params=pltpu.CompilerParams(vmem_limit_bytes=32 * 1024 * 1024),
        cost_estimate=pl.CostEstimate(
            flops=4 * rows * block * width,
            bytes_accessed=4 * block * width + 4 * rows * block + 4 * rows * width,
            transcendentals=0,
        ),
    )(jnp.stack([core, own]).astype(jnp.int32), left, head_weight, take)


def on_device(hidden, norm_gain, head_weight):
    core = lax.axis_index("pair")
    place = lax.axis_index("batch")
    level = lax.axis_index("vocab")
    vocab = lax.axis_size("vocab")
    y, x = place // 2, place % 2
    rows = hidden[0]
    seg = rows.shape[0] // 2
    depth = rows.shape[1]
    block, columns = head_weight.shape
    width = columns // 2
    model = depth * vocab
    step = seg // CHUNKS

    wide = rows.astype(jnp.float32)
    gained = (wide * norm_gain.astype(jnp.float32)[None, :]).astype(jnp.bfloat16)
    gained = gained.reshape(2, seg, depth)

    squares = jnp.sum(wide * wide, axis=1)
    reach = 1
    while reach < vocab:
        squares += lax.ppermute(squares, "vocab", [(i, i ^ reach) for i in range(vocab)])
        reach *= 2

    first = level // 2 if vocab == 4 else 0
    pieces = [gained[:, c * step : (c + 1) * step] for c in range(CHUNKS)]
    lined = depth == 2 * block and vocab == 4
    if lined:
        sides = [lax.dynamic_slice_in_dim(piece, (1 - x) * block, block, 2) for piece in pieces]
        sides = [lax.ppermute(side, "batch", X_SWAP) for side in sides]

    def line_features(c, held, *earlier):
        mine = lax.dynamic_slice_in_dim(pieces[c], x * block, block, 2)
        other = sides[c]
        own = jnp.stack([jnp.where(x == 0, mine, other), jnp.where(x == 0, other, mine)])
        own = after(own, squares, *held)
        below, above = [own], [own]
        for k in range(1, vocab):
            below.append(
                lax.ppermute(below[-1], "vocab", [(z, z + 1) for z in range(k - 1, vocab - 1)])
            )
            above.append(
                lax.ppermute(above[-1], "vocab", [(z + 1, z) for z in range(vocab - k)])
            )

        def quarter(place, reach):
            part = own
            for k in range(1, reach + 1):
                part = jnp.where(level - place == k, below[k], part)
                part = jnp.where(place - level == k, above[k], part)
            return part

        far = 1 - y + 2 * (1 - first)
        got_near = lax.ppermute(quarter(1 - y + 2 * first, 1), "batch", Y_SWAP)
        ends = [(0, 0), (1, vocab - 1)]
        pairs = [(b * vocab + z, (b ^ 2) * vocab + z) for b in range(4) for z in range(vocab)]
        late = [pair for pair in pairs if (pair[0] // vocab // 2, pair[0] % vocab) in ends]
        early = [pair for pair in pairs if pair not in late]
        got_early = after(lax.ppermute(quarter(far, 2), ("batch", "vocab"), early), *earlier)
        below[-1], above[-1] = after(below[-1], *earlier), after(above[-1], *earlier)
        last = jnp.where(level == 0, above[-1], below[-1])
        got_late = lax.ppermute(last, ("batch", "vocab"), late)
        is_late = (level == 0) & (y == 1) | (level == vocab - 1) & (y == 0)
        got_far = jnp.where(is_late, got_late, got_early)
        halves = []
        for mine, other in (
            (quarter(y + 2 * first, 1), got_near),
            (quarter(y + 2 * (1 - first), vocab - 1), got_far),
        ):
            halves.append(
                jnp.stack([jnp.where(y == 0, mine, other), jnp.where(y == 0, other, mine)])
            )
        return jnp.stack(halves), (below[-1], above[-1], got_near, got_early)

    def gathered_features(c, held, *earlier):
        whole = lax.all_gather(pieces[c], "vocab", axis=2, tiled=True)
        whole = whole.reshape(2, step, 2, 4, block).transpose(3, 2, 0, 1, 4)
        whole = lax.all_to_all(whole, "batch", split_axis=0, concat_axis=0)
        whole = whole.reshape(2, 2, 2, 2, step, block).transpose(2, 0, 1, 3, 4, 5)
        return after(whole, *earlier), (gained,)

    features = line_features if lined else gathered_features
    own_half = core ^ first if lined else core
    found, begun = features(0, ())

    take = lax.ppermute(head_weight, "pair", CORE_SWAP)

    squares = squares.reshape(2, seg)
    sent = [
        lax.ppermute(
            pick(squares, core ^ k, 0),
            ("pair", "batch"),
            [(4 * s + b, 2 * b + (s ^ k)) for s in range(2) for b in range(4)],
        )
        for k in range(2)
    ]
    total_sq = jnp.stack([jnp.where(x == 0, sent[0], sent[1]), jnp.where(x == 0, sent[1], sent[0])])
    scale = lax.rsqrt(total_sq / model + EPS) / SHRINK

    def reduced(left):
        middle = width // 2
        parts = partial_logits(core, own_half, left.reshape(2, -1, block), head_weight, take)
        parts = parts.reshape(2, 2, 2, step, width)
        low, high = parts[..., :middle], parts[..., middle:]
        away_x = lax.ppermute(pick(low, 1 - x, 2).astype(SUM_TYPE), "batch", X_SWAP)
        away_y = lax.ppermute(pick(high, 1 - y, 1).astype(SUM_TYPE), "batch", Y_SWAP)
        sum_x = pick(low, x, 2) + away_x.astype(jnp.float32)
        sum_y = pick(high, y, 1) + away_y.astype(jnp.float32)
        next_y = lax.ppermute(pick(sum_x, 1 - y, 1).astype(SUM_TYPE), "batch", Y_SWAP)
        next_x = lax.ppermute(pick(sum_y, 1 - x, 1).astype(SUM_TYPE), "batch", X_SWAP)
        sums = jnp.concatenate(
            [
                pick(sum_x, y, 1) + next_y.astype(jnp.float32),
                pick(sum_y, x, 1) + next_x.astype(jnp.float32),
            ],
            axis=-1,
        ).astype(SUM_TYPE)
        return sums, parts, sum_y

    done = []
    for c in range(CHUNKS):
        other = lax.ppermute(found, "pair", CORE_SWAP)
        own_sums, parts, _ = reduced(found)
        other_sums, _, halfway = reduced(other)
        if c + 1 < CHUNKS:
            found = after(features(c + 1, begun, parts)[0], halfway)
        sums = jnp.stack([own_sums, other_sums])
        theirs = lax.ppermute(pick(sums, 1 - core, 1), "pair", CORE_SWAP)
        done.append((pick(sums, core, 1), theirs))

    mine = jnp.concatenate([part[0] for part in done], axis=1)
    theirs = jnp.concatenate([part[1] for part in done], axis=1)

    def scores(own, other, got_own, got_other, gain):
        low = jnp.where(core == 0, own, got_own)
        high = jnp.where(core == 0, got_other, other)
        return jnp.concatenate([low, high], axis=1).astype(jnp.float32) * gain[:, None]

    cond = scores(mine[0], mine[1], theirs[0], theirs[1], scale[0])
    uncond = scores(mine[1], mine[0], theirs[1], theirs[0], scale[1])
    guided = GUIDE * cond + (1.0 - GUIDE) * uncond

    def stats(values):
        peak = jnp.max(values, axis=1)
        return peak, jnp.sum(jnp.exp(values - peak[:, None]), axis=1)

    peak_c, sum_c = stats(cond)
    peak_g, sum_g = stats(guided)
    own = jnp.stack([peak_c, peak_g, sum_c, sum_g])
    every = jnp.stack(
        [own]
        + [
            lax.ppermute(own, "vocab", [(i, (i + k) % vocab) for i in range(vocab)])
            for k in range(1, vocab)
        ]
    )
    top = jnp.max(every[:, :2], axis=0)
    total = jnp.sum(every[:, 2:] * jnp.exp(every[:, :2] - top[None]), axis=0)
    norm = top + jnp.log(total)
    return (guided - norm[1][:, None], cond - norm[0][:, None])


def solution(mesh):
    in_specs = (P("pair", "batch", "vocab"), P("vocab"), P(("pair", "batch"), "vocab"))
    out_specs = (P(("pair", "batch"), "vocab"), P(("pair", "batch"), "vocab"))
    return jax.shard_map(
        on_device, mesh=mesh, in_specs=in_specs, out_specs=out_specs, check_vma=False
    )
```

```python
import jax
import jax.numpy as jnp
from jax import lax
from jax.experimental import pallas as pl
from jax.experimental.pallas import tpu as pltpu
from jax.sharding import PartitionSpec as P

EPS = 1e-05
GUIDE = 1.5
CHUNKS = 2
SHRINK = 1.0 / 32.0
SUM_TYPE = jnp.float16

X_SWAP = [(0, 1), (1, 0), (2, 3), (3, 2)]
Y_SWAP = [(0, 2), (2, 0), (1, 3), (3, 1)]
CORE_SWAP = [(0, 1), (1, 0)]


def pick(array, index, axis):
    return lax.dynamic_index_in_dim(array, index, axis, keepdims=False)


def after(value, *others):
    return lax.optimization_barrier((value, *others))[0]


def columns_kernel(start_ref, weight_ref, out_ref, done):
    width = out_ref.shape[1]
    start = pl.multiple_of(start_ref[0] * width, width)
    copy = pltpu.make_async_copy(weight_ref.at[:, pl.ds(start, width)], out_ref, done)
    copy.start()
    copy.wait()


def half_columns(weight, side):
    block, columns = weight.shape
    return pl.pallas_call(
        columns_kernel,
        in_specs=[
            pl.BlockSpec(memory_space=pltpu.SMEM),
            pl.BlockSpec(memory_space=pl.ANY),
        ],
        out_specs=pl.BlockSpec(memory_space=pltpu.VMEM),
        out_shape=jax.ShapeDtypeStruct((block, columns // 2), weight.dtype),
        scratch_shapes=[pltpu.SemaphoreType.DMA],
        cost_estimate=pl.CostEstimate(
            flops=0, bytes_accessed=2 * block * columns, transcendentals=0
        ),
        compiler_params=pltpu.CompilerParams(vmem_limit_bytes=16 * 1024 * 1024),
    )(side.reshape(1).astype(jnp.int32), weight)


def on_device(hidden, norm_gain, head_weight):
    core = lax.axis_index("pair")
    place = lax.axis_index("batch")
    level = lax.axis_index("vocab")
    vocab = lax.axis_size("vocab")
    y, x = place // 2, place % 2
    rows = hidden[0]
    seg = rows.shape[0] // 2
    depth = rows.shape[1]
    block, columns = head_weight.shape
    width = columns // 2
    model = depth * vocab
    step = seg // CHUNKS

    wide = rows.astype(jnp.float32)
    gained = (wide * norm_gain.astype(jnp.float32)[None, :]).astype(jnp.bfloat16)
    gained = gained.reshape(2, seg, depth)

    def paired(value, reach):
        return lax.ppermute(value, "vocab", [(i, i ^ reach) for i in range(vocab)])

    squares = jnp.sum(wide * wide, axis=1)
    reach = 1
    while 2 * reach < vocab:
        squares += paired(squares, reach)
        reach *= 2

    first = level // 2 if vocab == 4 else 0
    pieces = [gained[:, c * step : (c + 1) * step] for c in range(CHUNKS)]
    lined = depth == 2 * block and vocab == 4
    if lined:
        sides = [lax.dynamic_slice_in_dim(piece, (1 - x) * block, block, 2) for piece in pieces]
        sides = [lax.ppermute(side, "batch", X_SWAP) for side in sides]

    def line_features(c):
        mine = lax.dynamic_slice_in_dim(pieces[c], x * block, block, 2)
        other = sides[c]
        own = jnp.stack([jnp.where(x == 0, mine, other), jnp.where(x == 0, other, mine)])
        own = after(own, squares)
        below, above = [own], [own]
        for k in range(1, vocab):
            below.append(
                lax.ppermute(below[-1], "vocab", [(z, z + 1) for z in range(k - 1, vocab - 1)])
            )
            above.append(
                lax.ppermute(above[-1], "vocab", [(z + 1, z) for z in range(vocab - k)])
            )
            if c == 0 and k == 2:
                below[2], above[2] = after(below[2], *sides), after(above[2], *sides)

        def quarter(place, reach):
            part = own
            for k in range(1, reach + 1):
                part = jnp.where(level - place == k, below[k], part)
                part = jnp.where(place - level == k, above[k], part)
            return part

        far = 1 - y + 2 * (1 - first)
        got_near = lax.ppermute(quarter(1 - y + 2 * first, 1), "batch", Y_SWAP)
        ends = [(0, 0), (1, vocab - 1)]
        pairs = [(b * vocab + z, (b ^ 2) * vocab + z) for b in range(4) for z in range(vocab)]
        late = [pair for pair in pairs if (pair[0] // vocab // 2, pair[0] % vocab) in ends]
        early = [pair for pair in pairs if pair not in late]
        earlier = yield below[1], above[1]
        got_early = after(lax.ppermute(quarter(far, 2), ("batch", "vocab"), early), *earlier)
        below[-1], above[-1] = after(below[-1], *earlier), after(above[-1], *earlier)
        last = jnp.where(level == 0, above[-1], below[-1])
        got_late = lax.ppermute(last, ("batch", "vocab"), late)
        is_late = (level == 0) & (y == 1) | (level == vocab - 1) & (y == 0)
        got_far = jnp.where(is_late, got_late, got_early)
        halves = []
        for mine, other in (
            (quarter(y + 2 * first, 1), got_near),
            (quarter(y + 2 * (1 - first), vocab - 1), got_far),
        ):
            halves.append(
                jnp.stack([jnp.where(y == 0, mine, other), jnp.where(y == 0, other, mine)])
            )
        yield jnp.stack(halves)

    def gathered_features(c):
        earlier = yield (gained,)
        whole = lax.all_gather(pieces[c], "vocab", axis=2, tiled=True)
        whole = whole.reshape(2, step, 2, 4, block).transpose(3, 2, 0, 1, 4)
        whole = lax.all_to_all(whole, "batch", split_axis=0, concat_axis=0)
        whole = whole.reshape(2, 2, 2, 2, step, block).transpose(2, 0, 1, 3, 4, 5)
        yield after(whole, *earlier)

    features = line_features if lined else gathered_features
    own_half = core ^ first if lined else core
    gathers = [features(c) for c in range(CHUNKS)]
    begun = [next(gather) for gather in gathers]
    found = gathers[0].send(())
    for parts in begun[1:]:
        found = after(found, *parts)

    take = lax.ppermute(head_weight, "pair", CORE_SWAP)
    keep = half_columns(after(head_weight, *begun[0]), core)
    take = half_columns(take, core)

    more_squares = paired(after(squares, *begun[0]), reach)

    def row_scale(*earlier):
        total = (squares + after(more_squares, *earlier)).reshape(2, seg)
        sent = [
            lax.ppermute(
                pick(total, core ^ k, 0),
                ("pair", "batch"),
                [(4 * s + b, 2 * b + (s ^ k)) for s in range(2) for b in range(4)],
            )
            for k in range(2)
        ]
        total = jnp.stack(
            [jnp.where(x == 0, sent[0], sent[1]), jnp.where(x == 0, sent[1], sent[0])]
        )
        return lax.rsqrt(total / model + EPS) / SHRINK

    def partial(left):
        out = jnp.dot(pick(left, own_half, 0), keep, preferred_element_type=jnp.float32)
        out += jnp.dot(pick(left, 1 - own_half, 0), take, preferred_element_type=jnp.float32)
        return out * SHRINK

    def reduced(left):
        middle = width // 2
        parts = partial(left.reshape(2, -1, block))
        parts = parts.reshape(2, 2, 2, step, width)
        low, high = parts[..., :middle], parts[..., middle:]
        away_x = lax.ppermute(pick(low, 1 - x, 2).astype(SUM_TYPE), "batch", X_SWAP)
        away_y = lax.ppermute(pick(high, 1 - y, 1).astype(SUM_TYPE), "batch", Y_SWAP)
        sum_x = pick(low, x, 2) + away_x.astype(jnp.float32)
        sum_y = pick(high, y, 1) + away_y.astype(jnp.float32)
        next_y = lax.ppermute(pick(sum_x, 1 - y, 1).astype(SUM_TYPE), "batch", Y_SWAP)
        next_x = lax.ppermute(pick(sum_y, 1 - x, 1).astype(SUM_TYPE), "batch", X_SWAP)
        sums = jnp.concatenate(
            [
                pick(sum_x, y, 1) + next_y.astype(jnp.float32),
                pick(sum_y, x, 1) + next_x.astype(jnp.float32),
            ],
            axis=-1,
        ).astype(SUM_TYPE)
        return sums, parts, sum_y

    done = []
    for c in range(CHUNKS):
        found, other = lax.optimization_barrier(
            (found, lax.ppermute(found, "pair", CORE_SWAP))
        )
        own_sums, parts, _ = reduced(found)
        other_sums, more_parts, halfway = reduced(other)
        if c == 0:
            scale = row_scale(more_parts)
        if c + 1 < CHUNKS:
            found = after(gathers[c + 1].send((parts,)), halfway)
        sums = jnp.stack([own_sums, other_sums])
        theirs = lax.ppermute(pick(sums, 1 - core, 1), "pair", CORE_SWAP)
        done.append((pick(sums, core, 1), theirs))

    mine = jnp.concatenate([part[0] for part in done], axis=1)
    theirs = jnp.concatenate([part[1] for part in done], axis=1)

    def scores(own, other, got_own, got_other, gain):
        low = jnp.where(core == 0, own, got_own)
        high = jnp.where(core == 0, got_other, other)
        return jnp.concatenate([low, high], axis=1).astype(jnp.float32) * gain[:, None]

    cond = scores(mine[0], mine[1], theirs[0], theirs[1], scale[0])
    uncond = scores(mine[1], mine[0], theirs[1], theirs[0], scale[1])
    guided = GUIDE * cond + (1.0 - GUIDE) * uncond

    def stats(values):
        peak = jnp.max(values, axis=1)
        return peak, jnp.sum(jnp.exp(values - peak[:, None]), axis=1)

    peak_c, sum_c = stats(cond)
    peak_g, sum_g = stats(guided)
    own = jnp.stack([peak_c, peak_g, sum_c, sum_g])
    every = jnp.stack(
        [own]
        + [
            lax.ppermute(own, "vocab", [(i, (i + k) % vocab) for i in range(vocab)])
            for k in range(1, vocab)
        ]
    )
    top = jnp.max(every[:, :2], axis=0)
    total = jnp.sum(every[:, 2:] * jnp.exp(every[:, :2] - top[None]), axis=0)
    norm = top + jnp.log(total)
    return (guided - norm[1][:, None], cond - norm[0][:, None])


def solution(mesh):
    in_specs = (P("pair", "batch", "vocab"), P("vocab"), P(("pair", "batch"), "vocab"))
    out_specs = (P(("pair", "batch"), "vocab"), P(("pair", "batch"), "vocab"))
    return jax.shard_map(
        on_device, mesh=mesh, in_specs=in_specs, out_specs=out_specs, check_vma=False
    )
```

```python
import jax
import jax.numpy as jnp
from jax import lax
from jax.experimental import pallas as pl
from jax.experimental.pallas import tpu as pltpu
from jax.sharding import PartitionSpec as P

EPS = 1e-05
GUIDE = 1.5
CHUNKS = 2
SHRINK = 1.0 / 32.0
SUM_TYPE = jnp.float16

X_SWAP = [(0, 1), (1, 0), (2, 3), (3, 2)]
Y_SWAP = [(0, 2), (2, 0), (1, 3), (3, 1)]
CORE_SWAP = [(0, 1), (1, 0)]


def pick(array, index, axis):
    return lax.dynamic_index_in_dim(array, index, axis, keepdims=False)


def after(value, *others):
    return lax.optimization_barrier((value, *others))[0]


def columns_kernel(start_ref, weight_ref, out_ref, done):
    width = out_ref.shape[1]
    start = pl.multiple_of(start_ref[0] * width, width)
    copy = pltpu.make_async_copy(weight_ref.at[:, pl.ds(start, width)], out_ref, done)
    copy.start()
    copy.wait()


def half_columns(weight, side):
    block, columns = weight.shape
    return pl.pallas_call(
        columns_kernel,
        in_specs=[
            pl.BlockSpec(memory_space=pltpu.SMEM),
            pl.BlockSpec(memory_space=pltpu.HBM),
        ],
        out_specs=pl.BlockSpec(memory_space=pltpu.VMEM),
        out_shape=jax.ShapeDtypeStruct((block, columns // 2), weight.dtype),
        scratch_shapes=[pltpu.SemaphoreType.DMA],
        cost_estimate=pl.CostEstimate(
            flops=0, bytes_accessed=2 * block * columns, transcendentals=0
        ),
        compiler_params=pltpu.CompilerParams(vmem_limit_bytes=16 * 1024 * 1024),
    )(side.reshape(1).astype(jnp.int32), weight)


def on_device(hidden, norm_gain, head_weight):
    core = lax.axis_index("pair")
    place = lax.axis_index("batch")
    level = lax.axis_index("vocab")
    vocab = lax.axis_size("vocab")
    y, x = place // 2, place % 2
    rows = hidden[0]
    seg = rows.shape[0] // 2
    depth = rows.shape[1]
    block, columns = head_weight.shape
    width = columns // 2
    model = depth * vocab
    step = seg // CHUNKS

    wide = rows.astype(jnp.float32)
    gained = (wide * norm_gain.astype(jnp.float32)[None, :]).astype(jnp.bfloat16)
    gained = gained.reshape(2, seg, depth)

    def paired(value, reach):
        return lax.ppermute(value, "vocab", [(i, i ^ reach) for i in range(vocab)])

    near_squares = jnp.sum(wide * wide, axis=1)
    reach = 1
    while 2 * reach < vocab:
        near_squares += paired(near_squares, reach)
        reach *= 2
    squares = near_squares + paired(near_squares, reach)

    first = level // 2 if vocab == 4 else 0
    pieces = [gained[:, c * step : (c + 1) * step] for c in range(CHUNKS)]
    lined = depth == 2 * block and vocab == 4
    if lined:
        sides = [lax.dynamic_slice_in_dim(piece, (1 - x) * block, block, 2) for piece in pieces]
        sides = [lax.ppermute(side, "batch", X_SWAP) for side in sides]

    def line_features(c, *held):
        mine = lax.dynamic_slice_in_dim(pieces[c], x * block, block, 2)
        other = sides[c]
        own = jnp.stack([jnp.where(x == 0, mine, other), jnp.where(x == 0, other, mine)])
        own = after(own, near_squares, *held)
        below, above = [own], [own]
        for k in range(1, vocab):
            below.append(
                lax.ppermute(below[-1], "vocab", [(z, z + 1) for z in range(k - 1, vocab - 1)])
            )
            above.append(
                lax.ppermute(above[-1], "vocab", [(z + 1, z) for z in range(vocab - k)])
            )
            if c == 0 and k == 1:
                side = after(core, below[1], above[1])
                weights.append(half_columns(head_weight, side))
                weights.append(half_columns(take, side))
            if c == 0 and k == 2:
                ready = (*sides, *weights, squares)
                below[2], above[2] = after(below[2], *ready), after(above[2], *ready)
            if k == 2:
                earlier = yield (below[1], above[1]), (below[2], above[2])
                below[2], above[2] = after(below[2], *earlier), after(above[2], *earlier)

        def quarter(place, reach):
            part = own
            for k in range(1, reach + 1):
                part = jnp.where(level - place == k, below[k], part)
                part = jnp.where(place - level == k, above[k], part)
            return part

        far = 1 - y + 2 * (1 - first)
        got_near = lax.ppermute(quarter(1 - y + 2 * first, 1), "batch", Y_SWAP)
        ends = [(0, 0), (1, vocab - 1)]
        pairs = [(b * vocab + z, (b ^ 2) * vocab + z) for b in range(4) for z in range(vocab)]
        late = [pair for pair in pairs if (pair[0] // vocab // 2, pair[0] % vocab) in ends]
        early = [pair for pair in pairs if pair not in late]
        got_early = lax.ppermute(quarter(far, 2), ("batch", "vocab"), early)
        last = jnp.where(level == 0, above[-1], below[-1])
        got_late = lax.ppermute(last, ("batch", "vocab"), late)
        is_late = (level == 0) & (y == 1) | (level == vocab - 1) & (y == 0)
        got_far = jnp.where(is_late, got_late, got_early)
        halves = []
        for mine, other in (
            (quarter(y + 2 * first, 1), got_near),
            (quarter(y + 2 * (1 - first), vocab - 1), got_far),
        ):
            halves.append(
                jnp.stack([jnp.where(y == 0, mine, other), jnp.where(y == 0, other, mine)])
            )
        yield jnp.stack(halves)

    def gathered_features(c, *held):
        if c == 0:
            weights.append(half_columns(head_weight, core))
            weights.append(half_columns(take, core))
        earlier = yield (gained,), (gained,)
        whole = lax.all_gather(pieces[c], "vocab", axis=2, tiled=True)
        whole = whole.reshape(2, step, 2, 4, block).transpose(3, 2, 0, 1, 4)
        whole = lax.all_to_all(whole, "batch", split_axis=0, concat_axis=0)
        whole = whole.reshape(2, 2, 2, 2, step, block).transpose(2, 0, 1, 3, 4, 5)
        yield after(whole, *earlier)

    take = lax.ppermute(head_weight, "pair", CORE_SWAP)
    weights = []

    features = line_features if lined else gathered_features
    own_half = core ^ first if lined else core
    gathers = [features(0)]
    begun = next(gathers[0])[1]
    for c in range(1, CHUNKS):
        gathers.append(features(c, *begun))
        first_step = next(gathers[c])[0]
    squares = after(squares, *begun).reshape(2, seg)
    sent = [
        lax.ppermute(
            pick(squares, core ^ k, 0),
            ("pair", "batch"),
            [(4 * s + b, 2 * b + (s ^ k)) for s in range(2) for b in range(4)],
        )
        for k in range(2)
    ]
    total_sq = jnp.stack([jnp.where(x == 0, sent[0], sent[1]), jnp.where(x == 0, sent[1], sent[0])])
    scale = lax.rsqrt(total_sq / model + EPS) / SHRINK

    found = after(gathers[0].send(()), scale, *first_step)
    keep, take = weights

    def partial(left):
        out = jnp.dot(pick(left, own_half, 0), keep, preferred_element_type=jnp.float32)
        out += jnp.dot(pick(left, 1 - own_half, 0), take, preferred_element_type=jnp.float32)
        return out * SHRINK

    def reduced(lefts):
        middle = width // 2
        parts = [partial(left.reshape(2, -1, block)) for left in lefts]
        whole = jnp.stack([part.reshape(2, 2, 2, step, width) for part in parts])
        low, high = whole[..., :middle], whole[..., middle:]
        away_x = lax.ppermute(pick(low, 1 - x, 3).astype(SUM_TYPE), "batch", X_SWAP)
        away_y = lax.ppermute(pick(high, 1 - y, 2).astype(SUM_TYPE), "batch", Y_SWAP)
        sum_x = pick(low, x, 3) + away_x.astype(jnp.float32)
        sum_y = pick(high, y, 2) + away_y.astype(jnp.float32)
        next_y = lax.ppermute(pick(sum_x, 1 - y, 2).astype(SUM_TYPE), "batch", Y_SWAP)
        next_x = lax.ppermute(pick(sum_y, 1 - x, 2).astype(SUM_TYPE), "batch", X_SWAP)
        sums = jnp.concatenate(
            [
                pick(sum_x, y, 2) + next_y.astype(jnp.float32),
                pick(sum_y, x, 2) + next_x.astype(jnp.float32),
            ],
            axis=-1,
        ).astype(SUM_TYPE)
        return sums, parts, (sum_x, sum_y)

    done = []
    for c in range(CHUNKS):
        lefts = lax.optimization_barrier((found, lax.ppermute(found, "pair", CORE_SWAP)))
        sums, parts, halfway = reduced(lefts)
        if c + 1 < CHUNKS:
            found = after(gathers[c + 1].send(parts), *halfway)
        theirs = lax.ppermute(pick(sums, 1 - core, 1), "pair", CORE_SWAP)
        done.append((pick(sums, core, 1), theirs))

    mine = jnp.concatenate([part[0] for part in done], axis=1)
    theirs = jnp.concatenate([part[1] for part in done], axis=1)

    def scores(own, other, got_own, got_other, gain):
        low = jnp.where(core == 0, own, got_own)
        high = jnp.where(core == 0, got_other, other)
        return jnp.concatenate([low, high], axis=1).astype(jnp.float32) * gain[:, None]

    cond = scores(mine[0], mine[1], theirs[0], theirs[1], scale[0])
    uncond = scores(mine[1], mine[0], theirs[1], theirs[0], scale[1])
    guided = GUIDE * cond + (1.0 - GUIDE) * uncond

    def stats(values):
        peak = jnp.max(values, axis=1)
        return peak, jnp.sum(jnp.exp(values - peak[:, None]), axis=1)

    peak_c, sum_c = stats(cond)
    peak_g, sum_g = stats(guided)
    own = jnp.stack([peak_c, peak_g, sum_c, sum_g])
    every = jnp.stack(
        [own]
        + [
            lax.ppermute(own, "vocab", [(i, (i + k) % vocab) for i in range(vocab)])
            for k in range(1, vocab)
        ]
    )
    top = jnp.max(every[:, :2], axis=0)
    total = jnp.sum(every[:, 2:] * jnp.exp(every[:, :2] - top[None]), axis=0)
    norm = top + jnp.log(total)
    return (guided - norm[1][:, None], cond - norm[0][:, None])


def solution(mesh):
    in_specs = (P("pair", "batch", "vocab"), P("vocab"), P(("pair", "batch"), "vocab"))
    out_specs = (P(("pair", "batch"), "vocab"), P(("pair", "batch"), "vocab"))
    return jax.shard_map(
        on_device, mesh=mesh, in_specs=in_specs, out_specs=out_specs, check_vma=False
    )
```

```python
import jax
import jax.numpy as jnp
from jax import lax
from jax.experimental import pallas as pl
from jax.experimental.pallas import tpu as pltpu
from jax.sharding import PartitionSpec as P

EPS = 1e-05
GUIDE = 1.5
CHUNKS = 2
SHRINK = 1.0 / 32.0
SUM_TYPE = jnp.float16

X_SWAP = [(0, 1), (1, 0), (2, 3), (3, 2)]
Y_SWAP = [(0, 2), (2, 0), (1, 3), (3, 1)]
CORE_SWAP = [(0, 1), (1, 0)]


def pick(array, index, axis):
    return lax.dynamic_index_in_dim(array, index, axis, keepdims=False)


def after(value, *others):
    return lax.optimization_barrier((value, *others))[0]


def columns_kernel(place_ref, own_ref, other_ref, near_ref, far_ref, done):
    width = near_ref.shape[1]
    start = pl.multiple_of(place_ref[0] * width, width)
    columns = pl.ds(start, width)

    def fetch(near, far):
        copies = [
            pltpu.make_async_copy(near.at[:, columns], near_ref, done.at[0]),
            pltpu.make_async_copy(far.at[:, columns], far_ref, done.at[1]),
        ]
        for copy in copies:
            copy.start()
        for copy in copies:
            copy.wait()

    @pl.when(place_ref[1] == 0)
    def _():
        fetch(own_ref, other_ref)

    @pl.when(place_ref[1] != 0)
    def _():
        fetch(other_ref, own_ref)


def half_columns(core, own_half, own, other):
    block, columns = own.shape
    shape = jax.ShapeDtypeStruct((block, columns // 2), own.dtype)
    return pl.pallas_call(
        columns_kernel,
        in_specs=[
            pl.BlockSpec(memory_space=pltpu.SMEM),
            pl.BlockSpec(memory_space=pltpu.HBM),
            pl.BlockSpec(memory_space=pltpu.HBM),
        ],
        out_specs=[pl.BlockSpec(memory_space=pltpu.VMEM)] * 2,
        out_shape=[shape, shape],
        scratch_shapes=[pltpu.SemaphoreType.DMA((2,))],
        cost_estimate=pl.CostEstimate(
            flops=0, bytes_accessed=4 * block * columns, transcendentals=0
        ),
        compiler_params=pltpu.CompilerParams(vmem_limit_bytes=24 * 1024 * 1024),
    )(jnp.stack([core, own_half]).astype(jnp.int32), own, other)


def on_device(hidden, norm_gain, head_weight):
    core = lax.axis_index("pair")
    place = lax.axis_index("batch")
    level = lax.axis_index("vocab")
    vocab = lax.axis_size("vocab")
    y, x = place // 2, place % 2
    rows = hidden[0]
    seg = rows.shape[0] // 2
    depth = rows.shape[1]
    block, columns = head_weight.shape
    width = columns // 2
    model = depth * vocab
    step = seg // CHUNKS

    wide = rows.astype(jnp.float32)
    gained = (wide * norm_gain.astype(jnp.float32)[None, :]).astype(jnp.bfloat16)
    gained = gained.reshape(2, CHUNKS, step, depth).transpose(1, 0, 2, 3)

    take = lax.ppermute(head_weight, "pair", CORE_SWAP)

    def paired(value, reach):
        return lax.ppermute(value, "vocab", [(i, i ^ reach) for i in range(vocab)])

    squares = jnp.sum(wide * wide, axis=1)
    reach = 1
    while reach < vocab:
        squares += paired(squares, reach)
        reach *= 2
    squares = squares.reshape(2, seg)

    def row_scale(*earlier):
        sent = [
            lax.ppermute(
                pick(after(squares, *earlier), core ^ k, 0),
                ("pair", "batch"),
                [(4 * s + b, 2 * b + (s ^ k)) for s in range(2) for b in range(4)],
            )
            for k in range(2)
        ]
        total = jnp.stack([jnp.where(x == 0, sent[0], sent[1]), jnp.where(x == 0, sent[1], sent[0])])
        return lax.rsqrt(total / model + EPS) / SHRINK

    def by_y(mine, other, axis):
        return jnp.stack([jnp.where(y == 0, mine, other), jnp.where(y == 0, other, mine)], axis)

    def swapped(value):
        return lax.ppermute(value, "pair", CORE_SWAP)

    def dots(lefts, weight):
        return [
            jnp.dot(left.reshape(-1, block), weight, preferred_element_type=jnp.float32)
            for left in lefts
        ]

    def line_parts():
        mine = lax.dynamic_slice_in_dim(gained, x * block, block, 3)
        other = lax.ppermute(
            lax.dynamic_slice_in_dim(gained, (1 - x) * block, block, 3), "batch", X_SWAP
        )
        own = jnp.stack([jnp.where(x == 0, mine, other), jnp.where(x == 0, other, mine)], axis=1)
        own = after(own, squares)

        def up(value, k):
            return lax.ppermute(value, "vocab", [(z, z + 1) for z in range(k - 1, vocab - 1)])

        def down(value, k):
            return lax.ppermute(value, "vocab", [(z + 1, z) for z in range(vocab - k)])

        below, above = [own, up(own, 1)], [own, down(own, 1)]

        def quarter(place, reach):
            part = own
            for k in range(1, reach + 1):
                part = jnp.where(level - place == k, below[k], part)
                part = jnp.where(place - level == k, above[k], part)
            return part

        first = level // 2
        got_near = lax.ppermute(quarter(1 - y + 2 * first, 1), "batch", Y_SWAP)
        below.append(up(below[1], 2))
        above.append(down(above[1], 2))
        weights = half_columns(after(core, below[1], above[1]), core ^ first, head_weight, take)
        scale = row_scale(*weights)
        near = by_y(quarter(y + 2 * first, 1), got_near, 1)
        ready = (near, scale, *weights)
        below[2], above[2] = after(below[2], *ready), after(above[2], *ready)
        nears = (near, swapped(near))

        far = 1 - y + 2 * (1 - first)
        tips = [(0, 0), (1, vocab - 1)]
        pairs = [(b * vocab + z, (b ^ 2) * vocab + z) for b in range(4) for z in range(vocab)]
        late = [pair for pair in pairs if (pair[0] // vocab // 2, pair[0] % vocab) in tips]
        early = [pair for pair in pairs if pair not in late]
        got_early = lax.ppermute(quarter(far, 2), ("batch", "vocab"), early)
        mine_early = quarter(y + 2 * (1 - first), 2)
        near_parts = [part.reshape(CHUNKS, -1, width) for part in dots(nears, weights[0])]
        is_late = (level == 0) & (y == 1) | (level == vocab - 1) & (y == 0)
        is_far = (level == 0) & (y == 1) | (level == vocab - 1) & (y == 0)
        ends = [(up(below[2][c], 3), down(above[2][c], 3)) for c in range(CHUNKS)]
        parts = []
        for c in range(CHUNKS):
            last = jnp.where(level == 0, ends[c][1], ends[c][0])
            earlier = parts[-1] if parts else sum(ends[1:], ())
            got_late = after(lax.ppermute(last, ("batch", "vocab"), late), *earlier)
            got = jnp.where(is_late, got_late, got_early[c])
            mine = jnp.where(is_far, last, mine_early[c])
            both = by_y(mine, got, 0)
            fars = lax.optimization_barrier((both, swapped(both)))
            parts.append(
                [
                    near_part[c] + far_part
                    for near_part, far_part in zip(near_parts, dots(fars, weights[1]))
                ]
            )
        return parts, scale

    def gathered_parts():
        weights = half_columns(core, core, head_weight, take)
        parts = []
        for c in range(CHUNKS):
            whole = lax.all_gather(gained[c], "vocab", axis=2, tiled=True)
            whole = whole.reshape(2, step, 2, 4, block).transpose(3, 2, 0, 1, 4)
            whole = lax.all_to_all(whole, "batch", split_axis=0, concat_axis=0)
            whole = whole.reshape(2, 2, 2, 2, step, block).transpose(2, 0, 1, 3, 4, 5)
            lefts = (whole, swapped(whole))
            parts.append(
                [
                    near + far
                    for near, far in zip(
                        dots([left[0] for left in lefts], weights[0]),
                        dots([left[1] for left in lefts], weights[1]),
                    )
                ]
            )
        return parts, row_scale()

    def reduced(parts):
        middle = width // 2
        whole = jnp.stack([(part * SHRINK).reshape(2, 2, 2, step, width) for part in parts])
        low, high = whole[..., :middle], whole[..., middle:]
        away_x = lax.ppermute(pick(low, 1 - x, 3).astype(SUM_TYPE), "batch", X_SWAP)
        away_y = lax.ppermute(pick(high, 1 - y, 2).astype(SUM_TYPE), "batch", Y_SWAP)
        sum_x = pick(low, x, 3) + away_x.astype(jnp.float32)
        sum_y = pick(high, y, 2) + away_y.astype(jnp.float32)
        next_y = lax.ppermute(pick(sum_x, 1 - y, 2).astype(SUM_TYPE), "batch", Y_SWAP)
        next_x = lax.ppermute(pick(sum_y, 1 - x, 2).astype(SUM_TYPE), "batch", X_SWAP)
        return jnp.concatenate(
            [
                pick(sum_x, y, 2) + next_y.astype(jnp.float32),
                pick(sum_y, x, 2) + next_x.astype(jnp.float32),
            ],
            axis=-1,
        ).astype(SUM_TYPE)

    lined = depth == 2 * block and vocab == 4
    parts, scale = line_parts() if lined else gathered_parts()
    done = []
    for c in range(CHUNKS):
        sums = reduced(parts[c])
        theirs = lax.ppermute(pick(sums, 1 - core, 1), "pair", CORE_SWAP)
        done.append((pick(sums, core, 1), theirs))

    mine = jnp.concatenate([part[0] for part in done], axis=1)
    theirs = jnp.concatenate([part[1] for part in done], axis=1)

    def scores(own, other, got_own, got_other, gain):
        low = jnp.where(core == 0, own, got_own)
        high = jnp.where(core == 0, got_other, other)
        return jnp.concatenate([low, high], axis=1).astype(jnp.float32) * gain[:, None]

    cond = scores(mine[0], mine[1], theirs[0], theirs[1], scale[0])
    uncond = scores(mine[1], mine[0], theirs[1], theirs[0], scale[1])
    guided = GUIDE * cond + (1.0 - GUIDE) * uncond

    def stats(values):
        peak = jnp.max(values, axis=1)
        return peak, jnp.sum(jnp.exp(values - peak[:, None]), axis=1)

    peak_c, sum_c = stats(cond)
    peak_g, sum_g = stats(guided)
    own = jnp.stack([peak_c, peak_g, sum_c, sum_g])
    every = jnp.stack(
        [own]
        + [
            lax.ppermute(own, "vocab", [(i, (i + k) % vocab) for i in range(vocab)])
            for k in range(1, vocab)
        ]
    )
    top = jnp.max(every[:, :2], axis=0)
    total = jnp.sum(every[:, 2:] * jnp.exp(every[:, :2] - top[None]), axis=0)
    norm = top + jnp.log(total)
    return (guided - norm[1][:, None], cond - norm[0][:, None])


def solution(mesh):
    in_specs = (P("pair", "batch", "vocab"), P("vocab"), P(("pair", "batch"), "vocab"))
    out_specs = (P(("pair", "batch"), "vocab"), P(("pair", "batch"), "vocab"))
    return jax.shard_map(
        on_device, mesh=mesh, in_specs=in_specs, out_specs=out_specs, check_vma=False
    )
```

```python
import jax
import jax.numpy as jnp
from jax import lax
from jax.experimental import pallas as pl
from jax.experimental.pallas import tpu as pltpu
from jax.sharding import PartitionSpec as P

EPS = 1e-05
GUIDE = 1.5
CHUNKS = 2
SHRINK = 1.0 / 32.0
SUM_TYPE = jnp.float16

X_SWAP = [(0, 1), (1, 0), (2, 3), (3, 2)]
Y_SWAP = [(0, 2), (2, 0), (1, 3), (3, 1)]
CORE_SWAP = [(0, 1), (1, 0)]


def pick(array, index, axis):
    return lax.dynamic_index_in_dim(array, index, axis, keepdims=False)


def after(value, *others):
    return lax.optimization_barrier((value, *others))[0]


def columns_kernel(place_ref, own_ref, other_ref, near_ref, far_ref, done):
    width = near_ref.shape[1]
    start = pl.multiple_of(place_ref[0] * width, width)
    columns = pl.ds(start, width)

    def fetch(near, far):
        copies = [
            pltpu.make_async_copy(near.at[:, columns], near_ref, done.at[0]),
            pltpu.make_async_copy(far.at[:, columns], far_ref, done.at[1]),
        ]
        for copy in copies:
            copy.start()
        for copy in copies:
            copy.wait()

    @pl.when(place_ref[1] == 0)
    def _():
        fetch(own_ref, other_ref)

    @pl.when(place_ref[1] != 0)
    def _():
        fetch(other_ref, own_ref)


def half_columns(core, own_half, own, other):
    block, columns = own.shape
    shape = jax.ShapeDtypeStruct((block, columns // 2), own.dtype)
    return pl.pallas_call(
        columns_kernel,
        in_specs=[
            pl.BlockSpec(memory_space=pltpu.SMEM),
            pl.BlockSpec(memory_space=pltpu.HBM),
            pl.BlockSpec(memory_space=pltpu.HBM),
        ],
        out_specs=[pl.BlockSpec(memory_space=pltpu.VMEM)] * 2,
        out_shape=[shape, shape],
        scratch_shapes=[pltpu.SemaphoreType.DMA((2,))],
        cost_estimate=pl.CostEstimate(
            flops=0, bytes_accessed=4 * block * columns, transcendentals=0
        ),
        compiler_params=pltpu.CompilerParams(vmem_limit_bytes=48 * 1024 * 1024),
    )(jnp.stack([core, own_half]).astype(jnp.int32), own, other)


def on_device(hidden, norm_gain, head_weight):
    core = lax.axis_index("pair")
    place = lax.axis_index("batch")
    level = lax.axis_index("vocab")
    vocab = lax.axis_size("vocab")
    y, x = place // 2, place % 2
    rows = hidden[0]
    seg = rows.shape[0] // 2
    depth = rows.shape[1]
    block, columns = head_weight.shape
    width = columns // 2
    model = depth * vocab
    step = seg // CHUNKS

    wide = rows.astype(jnp.float32)
    gained = (wide * norm_gain.astype(jnp.float32)[None, :]).astype(jnp.bfloat16)
    gained = gained.reshape(2, CHUNKS, step, depth).transpose(1, 0, 2, 3)

    take = lax.ppermute(head_weight, "pair", CORE_SWAP)

    def paired(value, reach):
        return lax.ppermute(value, "vocab", [(i, i ^ reach) for i in range(vocab)])

    squares = jnp.sum(wide * wide, axis=1)
    reach = 1
    while reach < vocab:
        squares += paired(squares, reach)
        reach *= 2
    squares = squares.reshape(2, seg)

    def row_scale(*earlier):
        sent = [
            lax.ppermute(
                pick(after(squares, *earlier), core ^ k, 0),
                ("pair", "batch"),
                [(4 * s + b, 2 * b + (s ^ k)) for s in range(2) for b in range(4)],
            )
            for k in range(2)
        ]
        total = jnp.stack([jnp.where(x == 0, sent[0], sent[1]), jnp.where(x == 0, sent[1], sent[0])])
        return lax.rsqrt(total / model + EPS) / SHRINK

    def by_y(mine, other, axis):
        return jnp.stack([jnp.where(y == 0, mine, other), jnp.where(y == 0, other, mine)], axis)

    def swapped(value):
        return lax.ppermute(value, "pair", CORE_SWAP)

    def dots(lefts, weight):
        return [
            jnp.dot(left.reshape(-1, block), weight, preferred_element_type=jnp.float32)
            for left in lefts
        ]

    def line_parts():
        mine = lax.dynamic_slice_in_dim(gained, x * block, block, 3)
        other = lax.ppermute(
            lax.dynamic_slice_in_dim(gained, (1 - x) * block, block, 3), "batch", X_SWAP
        )
        own = jnp.stack([jnp.where(x == 0, mine, other), jnp.where(x == 0, other, mine)], axis=1)
        own = after(own, squares)

        def up(value, k):
            return lax.ppermute(value, "vocab", [(z, z + 1) for z in range(k - 1, vocab - 1)])

        def down(value, k):
            return lax.ppermute(value, "vocab", [(z + 1, z) for z in range(vocab - k)])

        below, above = [own, up(own, 1)], [own, down(own, 1)]

        def quarter(place, reach):
            part = own
            for k in range(1, reach + 1):
                part = jnp.where(level - place == k, below[k], part)
                part = jnp.where(place - level == k, above[k], part)
            return part

        first = level // 2
        weights = half_columns(after(core, own), core ^ first, head_weight, take)
        scale = row_scale(*weights)
        below[1], above[1] = after(below[1], scale, *weights), after(above[1], scale, *weights)
        got_near = lax.ppermute(quarter(1 - y + 2 * first, 1), "batch", Y_SWAP)
        below.append(up(below[1], 2))
        above.append(down(above[1], 2))
        near = by_y(quarter(y + 2 * first, 1), after(got_near, below[2], above[2]), 1)
        nears = (near, swapped(near))

        far = 1 - y + 2 * (1 - first)
        tips = [(0, 0), (1, vocab - 1)]
        pairs = [(b * vocab + z, (b ^ 2) * vocab + z) for b in range(4) for z in range(vocab)]
        late = [pair for pair in pairs if (pair[0] // vocab // 2, pair[0] % vocab) in tips]
        early = [pair for pair in pairs if pair not in late]
        got_early = lax.ppermute(quarter(far, 2), ("batch", "vocab"), early)
        mine_early = quarter(y + 2 * (1 - first), 2)
        near_parts = [part.reshape(CHUNKS, -1, width) for part in dots(nears, weights[0])]
        is_late = (level == 0) & (y == 1) | (level == vocab - 1) & (y == 0)
        ends = [
            (
                up(after(below[2][c], *([near] if c else [])), 3),
                down(after(above[2][c], *([near] if c else [])), 3),
            )
            for c in range(CHUNKS)
        ]

        lasts = [jnp.where(level == 0, above_3, below_3) for below_3, above_3 in ends]
        lates = [lax.ppermute(last, ("batch", "vocab"), late) for last in lasts]

        def parts(c, *earlier):
            got_late = after(lates[c], *(earlier or lasts[1:]))
            got = jnp.where(is_late, got_late, got_early[c])
            mine = jnp.where(is_late, lasts[c], mine_early[c])
            both = by_y(mine, got, 0)
            fars = lax.optimization_barrier((both, swapped(both)))
            found = [
                near_part[c] + far_part
                for near_part, far_part in zip(near_parts, dots(fars, weights[1]))
            ]
            return [after(part, *lates[c + 1 :]) for part in found]

        return parts, scale

    def gathered_parts():
        weights = half_columns(core, core, head_weight, take)

        def parts(c, *earlier):
            whole = lax.all_gather(gained[c], "vocab", axis=2, tiled=True)
            whole = whole.reshape(2, step, 2, 4, block).transpose(3, 2, 0, 1, 4)
            whole = lax.all_to_all(whole, "batch", split_axis=0, concat_axis=0)
            whole = whole.reshape(2, 2, 2, 2, step, block).transpose(2, 0, 1, 3, 4, 5)
            whole = after(whole, *earlier)
            lefts = (whole, swapped(whole))
            return [
                near + far
                for near, far in zip(
                    dots([left[0] for left in lefts], weights[0]),
                    dots([left[1] for left in lefts], weights[1]),
                )
            ]

        return parts, row_scale()

    lined = depth == 2 * block and vocab == 4
    parts, scale = line_parts() if lined else gathered_parts()
    halfway, more_sends = [], []
    for c in range(CHUNKS):
        whole = [part * SHRINK for part in parts(c, *(more_sends[-1] if c else ()))]
        whole = jnp.stack([part.reshape(2, 2, 2, step, width) for part in whole])
        low, high = whole[..., : width // 2], whole[..., width // 2 :]
        away_x = lax.ppermute(pick(low, 1 - x, 3).astype(SUM_TYPE), "batch", X_SWAP)
        away_y = lax.ppermute(pick(high, 1 - y, 2).astype(SUM_TYPE), "batch", Y_SWAP)
        sum_x = pick(low, x, 3) + away_x.astype(jnp.float32)
        sum_y = pick(high, y, 2) + away_y.astype(jnp.float32)
        halfway.append((pick(sum_x, y, 2), pick(sum_y, x, 2)))
        more_sends.append(
            (pick(sum_x, 1 - y, 2).astype(SUM_TYPE), pick(sum_y, 1 - x, 2).astype(SUM_TYPE))
        )
    done = []
    for c in range(CHUNKS):
        next_y = lax.ppermute(more_sends[c][0], "batch", Y_SWAP)
        next_x = lax.ppermute(more_sends[c][1], "batch", X_SWAP)
        sums = jnp.concatenate(
            [
                halfway[c][0] + next_y.astype(jnp.float32),
                halfway[c][1] + next_x.astype(jnp.float32),
            ],
            axis=-1,
        ).astype(SUM_TYPE)
        theirs = lax.ppermute(pick(sums, 1 - core, 1), "pair", CORE_SWAP)
        done.append((pick(sums, core, 1), theirs))

    mine = jnp.concatenate([part[0] for part in done], axis=1)
    theirs = jnp.concatenate([part[1] for part in done], axis=1)

    def scores(own, other, got_own, got_other, gain):
        low = jnp.where(core == 0, own, got_own)
        high = jnp.where(core == 0, got_other, other)
        return jnp.concatenate([low, high], axis=1).astype(jnp.float32) * gain[:, None]

    cond = scores(mine[0], mine[1], theirs[0], theirs[1], scale[0])
    uncond = scores(mine[1], mine[0], theirs[1], theirs[0], scale[1])
    guided = GUIDE * cond + (1.0 - GUIDE) * uncond

    def stats(values):
        peak = jnp.max(values, axis=1)
        return peak, jnp.sum(jnp.exp(values - peak[:, None]), axis=1)

    peak_c, sum_c = stats(cond)
    peak_g, sum_g = stats(guided)
    own = jnp.stack([peak_c, peak_g, sum_c, sum_g])
    every = jnp.stack(
        [own]
        + [
            lax.ppermute(own, "vocab", [(i, (i + k) % vocab) for i in range(vocab)])
            for k in range(1, vocab)
        ]
    )
    top = jnp.max(every[:, :2], axis=0)
    total = jnp.sum(every[:, 2:] * jnp.exp(every[:, :2] - top[None]), axis=0)
    norm = top + jnp.log(total)
    return (guided - norm[1][:, None], cond - norm[0][:, None])


def solution(mesh):
    in_specs = (P("pair", "batch", "vocab"), P("vocab"), P(("pair", "batch"), "vocab"))
    out_specs = (P(("pair", "batch"), "vocab"), P(("pair", "batch"), "vocab"))
    return jax.shard_map(
        on_device, mesh=mesh, in_specs=in_specs, out_specs=out_specs, check_vma=False
    )
```

```python
import jax
import jax.numpy as jnp
from jax import lax
from jax.sharding import PartitionSpec as P

EPS = 1e-05
GUIDE = 1.5
CHUNKS = 2
SHRINK = 1.0 / 32.0
SUM_TYPE = jnp.float16

X_SWAP = [(0, 1), (1, 0), (2, 3), (3, 2)]
Y_SWAP = [(0, 2), (2, 0), (1, 3), (3, 1)]
CORE_SWAP = [(0, 1), (1, 0)]


def pick(array, index, axis):
    return lax.dynamic_index_in_dim(array, index, axis, keepdims=False)


def after(value, *others):
    return lax.optimization_barrier((value, *others))[0]


def on_device(hidden, norm_gain, head_weight):
    core = lax.axis_index("pair")
    place = lax.axis_index("batch")
    level = lax.axis_index("vocab")
    vocab = lax.axis_size("vocab")
    y, x = place // 2, place % 2
    rows = hidden[0]
    seg = rows.shape[0] // 2
    depth = rows.shape[1]
    block, columns = head_weight.shape
    width = columns // 2
    model = depth * vocab
    step = seg // CHUNKS

    wide = rows.astype(jnp.float32)
    gained = (wide * norm_gain.astype(jnp.float32)[None, :]).astype(jnp.bfloat16)
    gained = gained.reshape(2, CHUNKS, step, depth).transpose(1, 0, 2, 3)

    take = lax.ppermute(head_weight, "pair", CORE_SWAP)

    def paired(value, reach):
        return lax.ppermute(value, "vocab", [(i, i ^ reach) for i in range(vocab)])

    squares = jnp.sum(wide * wide, axis=1)
    reach = 1
    while reach < vocab:
        squares += paired(squares, reach)
        reach *= 2
    squares = squares.reshape(2, seg)

    def row_scale(*earlier):
        sent = [
            lax.ppermute(
                pick(after(squares, *earlier), core ^ k, 0),
                ("pair", "batch"),
                [(4 * s + b, 2 * b + (s ^ k)) for s in range(2) for b in range(4)],
            )
            for k in range(2)
        ]
        total = jnp.stack([jnp.where(x == 0, sent[0], sent[1]), jnp.where(x == 0, sent[1], sent[0])])
        return lax.rsqrt(total / model + EPS) / SHRINK

    def by_y(mine, other, axis):
        return jnp.stack([jnp.where(y == 0, mine, other), jnp.where(y == 0, other, mine)], axis)

    def swapped(value):
        return lax.ppermute(value, "pair", CORE_SWAP)

    def half_columns(weight, *earlier):
        return lax.dynamic_slice_in_dim(weight, after(core, *earlier) * width, width, 1)

    def dots(lefts, own_half, weights):
        return [
            jnp.dot(
                pick(left, own_half, 0).reshape(-1, block),
                weights[0],
                preferred_element_type=jnp.float32,
            )
            + jnp.dot(
                pick(left, 1 - own_half, 0).reshape(-1, block),
                weights[1],
                preferred_element_type=jnp.float32,
            )
            for left in lefts
        ]

    def line_parts():
        mine = lax.dynamic_slice_in_dim(gained, x * block, block, 3)
        other = lax.ppermute(
            lax.dynamic_slice_in_dim(gained, (1 - x) * block, block, 3), "batch", X_SWAP
        )
        own = jnp.stack([jnp.where(x == 0, mine, other), jnp.where(x == 0, other, mine)], axis=1)
        own = after(own, squares)

        def up(value, k):
            return lax.ppermute(value, "vocab", [(z, z + 1) for z in range(k - 1, vocab - 1)])

        def down(value, k):
            return lax.ppermute(value, "vocab", [(z + 1, z) for z in range(vocab - k)])

        below, above = [own, up(own, 1)], [own, down(own, 1)]

        def quarter(place, reach):
            part = own
            for k in range(1, reach + 1):
                part = jnp.where(level - place == k, below[k], part)
                part = jnp.where(place - level == k, above[k], part)
            return part

        first = level // 2
        weights = lax.optimization_barrier(
            (half_columns(head_weight, own), half_columns(take, own))
        )
        below[1], above[1] = after(below[1], *weights), after(above[1], *weights)
        got_near = lax.ppermute(quarter(1 - y + 2 * first, 1), "batch", Y_SWAP)
        below.append(up(below[1], 2))
        above.append(down(above[1], 2))
        below[2], above[2] = after(below[2], got_near), after(above[2], got_near)
        near = by_y(quarter(y + 2 * first, 1), after(got_near, below[2], above[2]), 1)
        nears = (near, swapped(near))

        far = 1 - y + 2 * (1 - first)
        tips = [(0, 0), (1, vocab - 1)]
        pairs = [(b * vocab + z, (b ^ 2) * vocab + z) for b in range(4) for z in range(vocab)]
        late = [pair for pair in pairs if (pair[0] // vocab // 2, pair[0] % vocab) in tips]
        early = [pair for pair in pairs if pair not in late]
        got_early = lax.ppermute(quarter(far, 2), ("batch", "vocab"), early)
        mine_early = quarter(y + 2 * (1 - first), 2)
        is_late = (level == 0) & (y == 1) | (level == vocab - 1) & (y == 0)
        below_3, above_3 = up(below[2], 3), down(above[2], 3)
        last = after(jnp.where(level == 0, above_3, below_3), got_early)
        lasts = [last[c] for c in range(CHUNKS)]
        lates = [lax.ppermute(last, ("batch", "vocab"), late) for last in lasts]

        def parts(c, *earlier):
            got_late = after(lates[c], *earlier)
            got = jnp.where(is_late, got_late, got_early[c])
            mine = jnp.where(is_late, lasts[c], mine_early[c])
            both = by_y(mine, got, 0)
            fars = lax.optimization_barrier((both, swapped(both)))
            lefts = [jnp.stack([near[c], far]) for near, far in zip(nears, fars)]
            return [after(part, *lates[c + 1 :]) for part in dots(lefts, core ^ first, weights)]

        return parts

    def gathered_parts():
        weights = (half_columns(head_weight), half_columns(take))

        def parts(c, *earlier):
            whole = lax.all_gather(gained[c], "vocab", axis=2, tiled=True)
            whole = whole.reshape(2, step, 2, 4, block).transpose(3, 2, 0, 1, 4)
            whole = lax.all_to_all(whole, "batch", split_axis=0, concat_axis=0)
            whole = whole.reshape(2, 2, 2, 2, step, block).transpose(2, 0, 1, 3, 4, 5)
            whole = after(whole, *earlier)
            return dots((whole, swapped(whole)), core, weights)

        return parts

    lined = depth == 2 * block and vocab == 4
    parts = line_parts() if lined else gathered_parts()
    kept, sends = [], []
    for c in range(CHUNKS):
        whole = [part * SHRINK for part in parts(c, *(sends[-1] if c else ()))]
        whole = jnp.stack([part.reshape(2, 2, 2, step, width) for part in whole])
        low, high = whole[..., : width // 2], whole[..., width // 2 :]
        kept.append((pick(low, x, 3), pick(high, y, 2)))
        sends.append(
            (pick(low, 1 - x, 3).astype(SUM_TYPE), pick(high, 1 - y, 2).astype(SUM_TYPE))
        )
    scale = row_scale(*sends[-1])
    halfway, more_sends = [], []
    for c in range(CHUNKS):
        away_x = lax.ppermute(sends[c][0], "batch", X_SWAP)
        away_y = lax.ppermute(sends[c][1], "batch", Y_SWAP)
        if c + 1 < CHUNKS:
            away_x, away_y = after(away_x, *sends[c + 1]), after(away_y, *sends[c + 1])
        sum_x = kept[c][0] + away_x.astype(jnp.float32)
        sum_y = kept[c][1] + away_y.astype(jnp.float32)
        halfway.append((pick(sum_x, y, 2), pick(sum_y, x, 2)))
        more_sends.append(
            (pick(sum_x, 1 - y, 2).astype(SUM_TYPE), pick(sum_y, 1 - x, 2).astype(SUM_TYPE))
        )
    done = []
    for c in range(CHUNKS):
        next_y = lax.ppermute(more_sends[c][0], "batch", Y_SWAP)
        next_x = lax.ppermute(more_sends[c][1], "batch", X_SWAP)
        sums = jnp.concatenate(
            [
                halfway[c][0] + next_y.astype(jnp.float32),
                halfway[c][1] + next_x.astype(jnp.float32),
            ],
            axis=-1,
        ).astype(SUM_TYPE)
        theirs = lax.ppermute(pick(sums, 1 - core, 1), "pair", CORE_SWAP)
        done.append((pick(sums, core, 1), theirs))

    mine = jnp.concatenate([part[0] for part in done], axis=1)
    theirs = jnp.concatenate([part[1] for part in done], axis=1)

    def scores(own, other, got_own, got_other, gain):
        low = jnp.where(core == 0, own, got_own)
        high = jnp.where(core == 0, got_other, other)
        return jnp.concatenate([low, high], axis=1).astype(jnp.float32) * gain[:, None]

    cond = scores(mine[0], mine[1], theirs[0], theirs[1], scale[0])
    uncond = scores(mine[1], mine[0], theirs[1], theirs[0], scale[1])
    guided = GUIDE * cond + (1.0 - GUIDE) * uncond

    def stats(values):
        peak = jnp.max(values, axis=1)
        return peak, jnp.sum(jnp.exp(values - peak[:, None]), axis=1)

    peak_c, sum_c = stats(cond)
    peak_g, sum_g = stats(guided)
    own = jnp.stack([peak_c, peak_g, sum_c, sum_g])
    every = jnp.stack(
        [own]
        + [
            lax.ppermute(own, "vocab", [(i, (i + k) % vocab) for i in range(vocab)])
            for k in range(1, vocab)
        ]
    )
    top = jnp.max(every[:, :2], axis=0)
    total = jnp.sum(every[:, 2:] * jnp.exp(every[:, :2] - top[None]), axis=0)
    norm = top + jnp.log(total)
    return (guided - norm[1][:, None], cond - norm[0][:, None])


def solution(mesh):
    in_specs = (P("pair", "batch", "vocab"), P("vocab"), P(("pair", "batch"), "vocab"))
    out_specs = (P(("pair", "batch"), "vocab"), P(("pair", "batch"), "vocab"))
    return jax.shard_map(
        on_device, mesh=mesh, in_specs=in_specs, out_specs=out_specs, check_vma=False
    )
```

```python
import jax
import jax.numpy as jnp
from jax import lax
from jax.sharding import PartitionSpec as P

EPS = 1e-05
GUIDE = 1.5
SHRINK = 1.0 / 32.0
SUM_TYPE = jnp.float16

X_SWAP = [(0, 1), (1, 0), (2, 3), (3, 2)]
Y_SWAP = [(0, 2), (2, 0), (1, 3), (3, 1)]
CORE_SWAP = [(0, 1), (1, 0)]


def pick(array, index, axis):
    return lax.dynamic_index_in_dim(array, index, axis, keepdims=False)


def after(value, *others):
    return lax.optimization_barrier((value, *others))[0]


def on_device(hidden, norm_gain, head_weight):
    core = lax.axis_index("pair")
    place = lax.axis_index("batch")
    level = lax.axis_index("vocab")
    vocab = lax.axis_size("vocab")
    y, x = place // 2, place % 2
    rows = hidden[0]
    seg = rows.shape[0] // 2
    depth = rows.shape[1]
    block, columns = head_weight.shape
    width = columns // 2
    model = depth * vocab

    wide = rows.astype(jnp.float32)
    gained = (wide * norm_gain.astype(jnp.float32)[None, :]).astype(jnp.bfloat16)
    gained = gained.reshape(2, seg, depth)

    take = lax.ppermute(head_weight, "pair", CORE_SWAP)

    def paired(value, reach):
        return lax.ppermute(value, "vocab", [(i, i ^ reach) for i in range(vocab)])

    squares = jnp.sum(wide * wide, axis=1)
    reach = 1
    while reach < vocab:
        squares += paired(squares, reach)
        reach *= 2
    squares = squares.reshape(2, seg)

    def row_scale(*earlier):
        sent = [
            lax.ppermute(
                pick(after(squares, *earlier), core ^ k, 0),
                ("pair", "batch"),
                [(4 * s + b, 2 * b + (s ^ k)) for s in range(2) for b in range(4)],
            )
            for k in range(2)
        ]
        total = jnp.stack([jnp.where(x == 0, sent[0], sent[1]), jnp.where(x == 0, sent[1], sent[0])])
        return lax.rsqrt(total / model + EPS) / SHRINK

    def by_y(mine, other, axis):
        return jnp.stack([jnp.where(y == 0, mine, other), jnp.where(y == 0, other, mine)], axis)

    def swapped(value):
        return lax.ppermute(value, "pair", CORE_SWAP)

    def half_columns(weight, *earlier):
        return lax.dynamic_slice_in_dim(weight, after(core, *earlier) * width, width, 1)

    def dot(left, weight):
        return jnp.dot(left.reshape(-1, block), weight, preferred_element_type=jnp.float32)

    def line_parts():
        mine = lax.dynamic_slice_in_dim(gained, x * block, block, 2)
        other = lax.ppermute(
            lax.dynamic_slice_in_dim(gained, (1 - x) * block, block, 2), "batch", X_SWAP
        )
        own = jnp.stack([jnp.where(x == 0, mine, other), jnp.where(x == 0, other, mine)])
        own = after(own, squares)

        def up(value, k):
            return lax.ppermute(value, "vocab", [(z, z + 1) for z in range(k - 1, vocab - 1)])

        def down(value, k):
            return lax.ppermute(value, "vocab", [(z + 1, z) for z in range(vocab - k)])

        below, above = [own, up(own, 1)], [own, down(own, 1)]

        def quarter(place, reach):
            part = own
            for k in range(1, reach + 1):
                part = jnp.where(level - place == k, below[k], part)
                part = jnp.where(place - level == k, above[k], part)
            return part

        first = level // 2
        scale = row_scale(own)
        below[1], above[1] = after(below[1], scale), after(above[1], scale)
        near_sent = quarter(1 - y + 2 * first, 1)
        got_near = lax.ppermute(near_sent, "batch", Y_SWAP)
        below.append(up(below[1], 2))
        above.append(down(above[1], 2))
        keep_near = (core ^ first) == 0
        kept, taken = half_columns(head_weight, near_sent), half_columns(take, near_sent)
        near_weight, far_weight = lax.optimization_barrier(
            (jnp.where(keep_near, kept, taken), jnp.where(keep_near, taken, kept))
        )
        ready = (got_near, near_weight, far_weight)
        below[2], above[2] = after(below[2], *ready), after(above[2], *ready)
        near = by_y(quarter(y + 2 * first, 1), after(got_near, below[2], above[2]), 0)
        swapped_near = swapped(near)

        far = 1 - y + 2 * (1 - first)
        tips = [(0, 0), (1, vocab - 1)]
        pairs = [(b * vocab + z, (b ^ 2) * vocab + z) for b in range(4) for z in range(vocab)]
        late = [pair for pair in pairs if (pair[0] // vocab // 2, pair[0] % vocab) in tips]
        early = [pair for pair in pairs if pair not in late]
        got_early = lax.ppermute(quarter(far, 2), ("batch", "vocab"), early)
        mine_early = quarter(y + 2 * (1 - first), 2)
        is_late = (level == 0) & (y == 1) | (level == vocab - 1) & (y == 0)
        below_3, above_3 = up(below[2], 3), down(above[2], 3)
        near_part = dot(near, near_weight)
        last = after(jnp.where(level == 0, above_3, below_3), got_early, near_part)
        got_late = lax.ppermute(last, ("batch", "vocab"), late)
        far = by_y(
            jnp.where(is_late, last, mine_early), jnp.where(is_late, got_late, got_early), 0
        )
        swapped_far = swapped(far)

        def own_part():
            return near_part + dot(far, far_weight)

        def other_part(*earlier):
            left = after(swapped_far, *earlier)
            return dot(swapped_near, near_weight) + dot(left, far_weight)

        return (own_part, other_part), scale

    def gathered_parts():
        near_weight, far_weight = half_columns(head_weight), half_columns(take)
        whole = lax.all_gather(gained, "vocab", axis=2, tiled=True)
        whole = whole.reshape(2, seg, 2, 4, block).transpose(3, 2, 0, 1, 4)
        whole = lax.all_to_all(whole, "batch", split_axis=0, concat_axis=0)
        whole = whole.reshape(2, 2, 2, 2, seg, block).transpose(2, 0, 1, 3, 4, 5)
        swapped_whole = swapped(whole)

        def part(left):
            return dot(pick(left, core, 0), near_weight) + dot(pick(left, 1 - core, 0), far_weight)

        return (lambda: part(whole), lambda *earlier: part(after(swapped_whole, *earlier))), row_scale()

    lined = depth == 2 * block and vocab == 4
    parts, scale = line_parts() if lined else gathered_parts()
    kept, sends = [], []
    for part in parts:
        whole = (part(*(sends[-1] if sends else ())) * SHRINK).reshape(2, 2, 2, seg, width)
        low, high = whole[..., : width // 2], whole[..., width // 2 :]
        kept.append((pick(low, x, 2), pick(high, y, 1)))
        sends.append(
            (pick(low, 1 - x, 2).astype(SUM_TYPE), pick(high, 1 - y, 1).astype(SUM_TYPE))
        )
    halfway, more_sends = [], []
    for i in range(2):
        away_x = lax.ppermute(sends[i][0], "batch", X_SWAP)
        away_y = lax.ppermute(sends[i][1], "batch", Y_SWAP)
        if i == 0:
            away_x, away_y = after(away_x, *sends[1]), after(away_y, *sends[1])
        sum_x = kept[i][0] + away_x.astype(jnp.float32)
        sum_y = kept[i][1] + away_y.astype(jnp.float32)
        halfway.append((pick(sum_x, y, 1), pick(sum_y, x, 1)))
        more_sends.append(
            (pick(sum_x, 1 - y, 1).astype(SUM_TYPE), pick(sum_y, 1 - x, 1).astype(SUM_TYPE))
        )
    mine, theirs = [], []
    for i in range(2):
        next_y = lax.ppermute(more_sends[i][0], "batch", Y_SWAP)
        next_x = lax.ppermute(more_sends[i][1], "batch", X_SWAP)
        if i == 0:
            next_y, next_x = after(next_y, *more_sends[1]), after(next_x, *more_sends[1])
        sums = jnp.concatenate(
            [
                halfway[i][0] + next_y.astype(jnp.float32),
                halfway[i][1] + next_x.astype(jnp.float32),
            ],
            axis=-1,
        ).astype(SUM_TYPE)
        mine.append(pick(sums, core, 0))
        theirs.append(swapped(pick(sums, 1 - core, 0)))

    def scores(own, other, got_own, got_other, gain):
        low = jnp.where(core == 0, own, got_own)
        high = jnp.where(core == 0, got_other, other)
        return jnp.concatenate([low, high], axis=1).astype(jnp.float32) * gain[:, None]

    cond = scores(mine[0], mine[1], theirs[0], theirs[1], scale[0])
    uncond = scores(mine[1], mine[0], theirs[1], theirs[0], scale[1])
    guided = GUIDE * cond + (1.0 - GUIDE) * uncond

    def stats(values):
        peak = jnp.max(values, axis=1)
        return peak, jnp.sum(jnp.exp(values - peak[:, None]), axis=1)

    peak_c, sum_c = stats(cond)
    peak_g, sum_g = stats(guided)
    own = jnp.stack([peak_c, peak_g, sum_c, sum_g])
    every = jnp.stack(
        [own]
        + [
            lax.ppermute(own, "vocab", [(i, (i + k) % vocab) for i in range(vocab)])
            for k in range(1, vocab)
        ]
    )
    top = jnp.max(every[:, :2], axis=0)
    total = jnp.sum(every[:, 2:] * jnp.exp(every[:, :2] - top[None]), axis=0)
    norm = top + jnp.log(total)
    return (guided - norm[1][:, None], cond - norm[0][:, None])


def solution(mesh):
    in_specs = (P("pair", "batch", "vocab"), P("vocab"), P(("pair", "batch"), "vocab"))
    out_specs = (P(("pair", "batch"), "vocab"), P(("pair", "batch"), "vocab"))
    return jax.shard_map(
        on_device, mesh=mesh, in_specs=in_specs, out_specs=out_specs, check_vma=False
    )
```

```python
import jax
import jax.numpy as jnp
from jax import lax
from jax.sharding import PartitionSpec as P

EPS = 1e-05
GUIDE = 1.5
SHRINK = 1.0 / 32.0
SUM_TYPE = jnp.float16
CHUNKS = 2

X_SWAP = [(0, 1), (1, 0), (2, 3), (3, 2)]
Y_SWAP = [(0, 2), (2, 0), (1, 3), (3, 1)]
CORE_SWAP = [(0, 1), (1, 0)]


def pick(array, index, axis):
    return lax.dynamic_index_in_dim(array, index, axis, keepdims=False)


def after(value, *others):
    return lax.optimization_barrier((value, *others))[0]


def on_device(hidden, norm_gain, head_weight):
    core = lax.axis_index("pair")
    place = lax.axis_index("batch")
    level = lax.axis_index("vocab")
    vocab = lax.axis_size("vocab")
    y, x = place // 2, place % 2
    rows = hidden[0]
    seg = rows.shape[0] // 2
    depth = rows.shape[1]
    block, columns = head_weight.shape
    width = columns // 2
    model = depth * vocab
    step = seg // CHUNKS

    wide = rows.astype(jnp.float32)
    gained = (wide * norm_gain.astype(jnp.float32)[None, :]).astype(jnp.bfloat16)
    gained = gained.reshape(2, CHUNKS, step, depth).transpose(1, 0, 2, 3)

    take = lax.ppermute(head_weight, "pair", CORE_SWAP)

    def paired(value, reach):
        return lax.ppermute(value, "vocab", [(i, i ^ reach) for i in range(vocab)])

    squares = jnp.sum(wide * wide, axis=1)
    reach = 1
    while reach < vocab:
        squares += paired(squares, reach)
        reach *= 2
    squares = squares.reshape(2, seg)

    def row_scale(*earlier):
        sent = [
            lax.ppermute(
                pick(after(squares, *earlier), core ^ k, 0),
                ("pair", "batch"),
                [(4 * s + b, 2 * b + (s ^ k)) for s in range(2) for b in range(4)],
            )
            for k in range(2)
        ]
        total = jnp.stack([jnp.where(x == 0, sent[0], sent[1]), jnp.where(x == 0, sent[1], sent[0])])
        return lax.rsqrt(total / model + EPS) / SHRINK

    def by_y(mine, other, axis):
        return jnp.stack([jnp.where(y == 0, mine, other), jnp.where(y == 0, other, mine)], axis)

    def swapped(value):
        return lax.ppermute(value, "pair", CORE_SWAP)

    def half_columns(weight, *earlier):
        return lax.dynamic_slice_in_dim(weight, after(core, *earlier) * width, width, 1)

    def dot(left, weight):
        return jnp.dot(left.reshape(-1, block), weight, preferred_element_type=jnp.float32)

    def line_parts():
        mine = lax.dynamic_slice_in_dim(gained, x * block, block, 3)
        other = lax.ppermute(
            lax.dynamic_slice_in_dim(gained, (1 - x) * block, block, 3), "batch", X_SWAP
        )
        own = jnp.stack([jnp.where(x == 0, mine, other), jnp.where(x == 0, other, mine)], axis=1)
        own = after(own, squares)

        def up(value, k):
            return lax.ppermute(value, "vocab", [(z, z + 1) for z in range(k - 1, vocab - 1)])

        def down(value, k):
            return lax.ppermute(value, "vocab", [(z + 1, z) for z in range(vocab - k)])

        first = level // 2
        keep_near = (core ^ first) == 0
        kept, taken = half_columns(head_weight, own), half_columns(take, own)
        near_weight, far_weight = lax.optimization_barrier(
            (jnp.where(keep_near, kept, taken), jnp.where(keep_near, taken, kept))
        )
        scale = row_scale(own)
        ready = (scale, near_weight, far_weight)
        below_1, above_1 = after(up(own, 1), *ready), after(down(own, 1), *ready)
        belows, aboves = [], []
        for c in range(CHUNKS):
            below = [own[c], below_1[c], up(below_1[c], 2)]
            above = [own[c], above_1[c], down(above_1[c], 2)]
            if c:
                below[2] = after(below[2], belows[-1][2], aboves[-1][2])
                above[2] = after(above[2], belows[-1][2], aboves[-1][2])
            belows.append(below)
            aboves.append(above)

        def quarter(c, place, reach):
            part = own[c]
            for k in range(1, reach + 1):
                part = jnp.where(level - place == k, belows[c][k], part)
                part = jnp.where(place - level == k, aboves[c][k], part)
            return part

        def quarters(place, reach):
            return jnp.stack([quarter(c, place, reach) for c in range(CHUNKS)])

        got_near = lax.ppermute(quarters(1 - y + 2 * first, 1), "batch", Y_SWAP)
        far = 1 - y + 2 * (1 - first)
        tips = [(0, 0), (1, vocab - 1)]
        pairs = [(b * vocab + z, (b ^ 2) * vocab + z) for b in range(4) for z in range(vocab)]
        late = [pair for pair in pairs if (pair[0] // vocab // 2, pair[0] % vocab) in tips]
        early = [pair for pair in pairs if pair not in late]
        far_sent = quarters(far, 2)
        got_early = lax.ppermute(far_sent, ("batch", "vocab"), early)
        is_late = (level == 0) & (y == 1) | (level == vocab - 1) & (y == 0)
        ends = []
        for c in range(CHUNKS):
            earlier = (got_near,) if c else ()
            below_3 = up(after(belows[c][2], *earlier), 3)
            above_3 = down(after(aboves[c][2], *earlier), 3)
            earlier = (belows[1][2], aboves[1][2]) if c == 0 else ends[-1:]
            ends.append(after(jnp.where(level == 0, above_3, below_3), got_near, *earlier))
        lates = [lax.ppermute(end, ("batch", "vocab"), late) for end in ends]
        near = by_y(quarters(y + 2 * first, 1), after(got_near, belows[1][2]), 1)
        nears = (near, swapped(near))
        near_parts = [dot(left, near_weight).reshape(CHUNKS, -1, width) for left in nears]

        def parts(c, *earlier):
            got_late = after(lates[c], *(earlier or ends[1:]))
            mine = jnp.where(is_late, ends[c], quarter(c, y + 2 * (1 - first), 2))
            far = by_y(mine, jnp.where(is_late, got_late, got_early[c]), 0)
            found = [
                near_part[c] + dot(left, far_weight)
                for near_part, left in zip(near_parts, (far, swapped(far)))
            ]
            return found

        return parts, scale

    def gathered_parts():
        near_weight, far_weight = half_columns(head_weight), half_columns(take)

        def part(left):
            return dot(pick(left, core, 0), near_weight) + dot(pick(left, 1 - core, 0), far_weight)

        def parts(c, *earlier):
            whole = lax.all_gather(gained[c], "vocab", axis=2, tiled=True)
            whole = whole.reshape(2, step, 2, 4, block).transpose(3, 2, 0, 1, 4)
            whole = lax.all_to_all(whole, "batch", split_axis=0, concat_axis=0)
            whole = whole.reshape(2, 2, 2, 2, step, block).transpose(2, 0, 1, 3, 4, 5)
            whole = after(whole, *earlier)
            return [part(whole), part(swapped(whole))]

        return parts, row_scale()

    lined = depth == 2 * block and vocab == 4
    parts, scale = line_parts() if lined else gathered_parts()
    kept, sends = [], []
    for c in range(CHUNKS):
        whole = [part * SHRINK for part in parts(c, *(sends[-1] if c else ()))]
        whole = jnp.stack([part.reshape(2, 2, 2, step, width) for part in whole])
        low, high = whole[..., : width // 2], whole[..., width // 2 :]
        kept.append((pick(low, x, 3), pick(high, y, 2)))
        sends.append(
            (pick(low, 1 - x, 3).astype(SUM_TYPE), pick(high, 1 - y, 2).astype(SUM_TYPE))
        )
    halfway, more_sends = [], []
    for c in range(CHUNKS):
        away_x = lax.ppermute(sends[c][0], "batch", X_SWAP)
        away_y = lax.ppermute(sends[c][1], "batch", Y_SWAP)
        if c + 1 < CHUNKS:
            away_x, away_y = after(away_x, *sends[c + 1]), after(away_y, *sends[c + 1])
        sum_x = kept[c][0] + away_x.astype(jnp.float32)
        sum_y = kept[c][1] + away_y.astype(jnp.float32)
        halfway.append((pick(sum_x, y, 2), pick(sum_y, x, 2)))
        more_sends.append(
            (pick(sum_x, 1 - y, 2).astype(SUM_TYPE), pick(sum_y, 1 - x, 2).astype(SUM_TYPE))
        )
    done = []
    for c in range(CHUNKS):
        next_y = lax.ppermute(more_sends[c][0], "batch", Y_SWAP)
        next_x = lax.ppermute(more_sends[c][1], "batch", X_SWAP)
        if c + 1 < CHUNKS:
            next_y, next_x = after(next_y, *more_sends[c + 1]), after(next_x, *more_sends[c + 1])
        sums = jnp.concatenate(
            [
                halfway[c][0] + next_y.astype(jnp.float32),
                halfway[c][1] + next_x.astype(jnp.float32),
            ],
            axis=-1,
        ).astype(SUM_TYPE)
        done.append((pick(sums, core, 1), swapped(pick(sums, 1 - core, 1))))
    mine = jnp.concatenate([part[0] for part in done], axis=1)
    theirs = jnp.concatenate([part[1] for part in done], axis=1)

    def scores(own, other, got_own, got_other, gain):
        low = jnp.where(core == 0, own, got_own)
        high = jnp.where(core == 0, got_other, other)
        return jnp.concatenate([low, high], axis=1).astype(jnp.float32) * gain[:, None]

    cond = scores(mine[0], mine[1], theirs[0], theirs[1], scale[0])
    uncond = scores(mine[1], mine[0], theirs[1], theirs[0], scale[1])
    guided = GUIDE * cond + (1.0 - GUIDE) * uncond

    def stats(values):
        peak = jnp.max(values, axis=1)
        return peak, jnp.sum(jnp.exp(values - peak[:, None]), axis=1)

    peak_c, sum_c = stats(cond)
    peak_g, sum_g = stats(guided)
    own = jnp.stack([peak_c, peak_g, sum_c, sum_g])
    every = jnp.stack(
        [own]
        + [
            lax.ppermute(own, "vocab", [(i, (i + k) % vocab) for i in range(vocab)])
            for k in range(1, vocab)
        ]
    )
    top = jnp.max(every[:, :2], axis=0)
    total = jnp.sum(every[:, 2:] * jnp.exp(every[:, :2] - top[None]), axis=0)
    norm = top + jnp.log(total)
    return (guided - norm[1][:, None], cond - norm[0][:, None])


def solution(mesh):
    in_specs = (P("pair", "batch", "vocab"), P("vocab"), P(("pair", "batch"), "vocab"))
    out_specs = (P(("pair", "batch"), "vocab"), P(("pair", "batch"), "vocab"))
    return jax.shard_map(
        on_device, mesh=mesh, in_specs=in_specs, out_specs=out_specs, check_vma=False
    )
```

```python
import jax
import jax.numpy as jnp
from jax import lax
from jax.sharding import PartitionSpec as P

EPS = 1e-05
GUIDE = 1.5
SHRINK = 1.0 / 32.0
SUM_TYPE = jnp.float16

X_SWAP = [(0, 1), (1, 0), (2, 3), (3, 2)]
Y_SWAP = [(0, 2), (2, 0), (1, 3), (3, 1)]
CORE_SWAP = [(0, 1), (1, 0)]


def pick(array, index, axis):
    return lax.dynamic_index_in_dim(array, index, axis, keepdims=False)


def after(value, *others):
    return lax.optimization_barrier((value, *others))[0]


def on_device(hidden, norm_gain, head_weight):
    core = lax.axis_index("pair")
    place = lax.axis_index("batch")
    level = lax.axis_index("vocab")
    vocab = lax.axis_size("vocab")
    y, x = place // 2, place % 2
    rows = hidden[0]
    seg = rows.shape[0] // 2
    depth = rows.shape[1]
    block, columns = head_weight.shape
    width = columns // 2
    model = depth * vocab

    wide = rows.astype(jnp.float32)
    gain = norm_gain.astype(jnp.float32)

    def gained(value, factor):
        return (value.astype(jnp.float32) * factor).astype(jnp.bfloat16)

    take = lax.ppermute(head_weight, "pair", CORE_SWAP)

    def paired(value, reach):
        return lax.ppermute(value, "vocab", [(i, i ^ reach) for i in range(vocab)])

    near_squares = jnp.sum(wide * wide, axis=1)
    reach = 1
    while 2 * reach < vocab:
        near_squares += paired(near_squares, reach)
        reach *= 2

    def far_squares(*earlier):
        return paired(after(near_squares, *earlier), reach)

    def row_scale(squares, *earlier):
        squares = squares.reshape(2, seg)
        sent = [
            lax.ppermute(
                pick(after(squares, *earlier), core ^ k, 0),
                ("pair", "batch"),
                [(4 * s + b, 2 * b + (s ^ k)) for s in range(2) for b in range(4)],
            )
            for k in range(2)
        ]
        total = jnp.stack([jnp.where(x == 0, sent[0], sent[1]), jnp.where(x == 0, sent[1], sent[0])])
        return lax.rsqrt(total / model + EPS) / SHRINK

    def by_y(mine, other, axis):
        return jnp.stack([jnp.where(y == 0, mine, other), jnp.where(y == 0, other, mine)], axis)

    def swapped(value):
        return lax.ppermute(value, "pair", CORE_SWAP)

    def half_columns(weight, *earlier):
        return lax.dynamic_slice_in_dim(weight, after(core, *earlier) * width, width, 1)

    def dot(left, weight):
        return jnp.dot(left.reshape(-1, block), weight, preferred_element_type=jnp.float32)

    def pieces(left, weight):
        low, high = weight[:, : width // 2], weight[:, width // 2 :]
        return [
            dot(pick(left, 1 - x, 2), low),
            dot(pick(left, 1 - y, 1), high),
            dot(pick(left, x, 2), low),
            dot(pick(left, y, 1), high),
        ]

    def line_parts():
        raw = rows.reshape(2, seg, depth)
        mine = lax.dynamic_slice_in_dim(raw, x * block, block, 2)
        other = lax.ppermute(
            lax.dynamic_slice_in_dim(raw, (1 - x) * block, block, 2), "batch", X_SWAP
        )
        own = jnp.stack([jnp.where(x == 0, mine, other), jnp.where(x == 0, other, mine)])
        own = gained(own, lax.dynamic_slice_in_dim(gain, x * block, block, 0))
        own = after(own, near_squares)

        def up(value, k):
            return lax.ppermute(value, "vocab", [(z, z + 1) for z in range(k - 1, vocab - 1)])

        def down(value, k):
            return lax.ppermute(value, "vocab", [(z + 1, z) for z in range(vocab - k)])

        below, above = [own, up(own, 1)], [own, down(own, 1)]

        def quarter(place, reach):
            part = own
            for k in range(1, reach + 1):
                part = jnp.where(level - place == k, below[k], part)
                part = jnp.where(place - level == k, above[k], part)
            return part

        first = level // 2
        more_squares = far_squares(own)
        keep_near = (core ^ first) == 0
        kept, taken = half_columns(head_weight, own), half_columns(take, own)
        near_weight, far_weight = lax.optimization_barrier(
            (jnp.where(keep_near, kept, taken), jnp.where(keep_near, taken, kept))
        )
        squares = near_squares + after(more_squares, near_weight, far_weight)
        ready = (near_weight, far_weight)
        below[1], above[1] = after(below[1], *ready), after(above[1], *ready)
        scale = row_scale(squares, below[1], above[1])
        got_near = lax.ppermute(quarter(1 - y + 2 * first, 1), "batch", Y_SWAP)
        below.append(up(below[1], 2))
        above.append(down(above[1], 2))
        ready = (got_near, scale)
        below[2], above[2] = after(below[2], *ready), after(above[2], *ready)
        near = by_y(quarter(y + 2 * first, 1), after(got_near, below[2], above[2]), 0)
        swapped_near = swapped(near)

        far = 1 - y + 2 * (1 - first)
        tips = [(0, 0), (1, vocab - 1)]
        pairs = [(b * vocab + z, (b ^ 2) * vocab + z) for b in range(4) for z in range(vocab)]
        late = [pair for pair in pairs if (pair[0] // vocab // 2, pair[0] % vocab) in tips]
        early = [pair for pair in pairs if pair not in late]
        got_early = lax.ppermute(quarter(far, 2), ("batch", "vocab"), early)
        mine_early = quarter(y + 2 * (1 - first), 2)
        is_late = (level == 0) & (y == 1) | (level == vocab - 1) & (y == 0)
        below_3, above_3 = up(below[2], 3), down(above[2], 3)
        near_pieces = pieces(near, near_weight)
        mine_early, last = after(mine_early, got_early), jnp.where(level == 0, above_3, below_3)
        last = after(last, got_early, mine_early, *near_pieces)
        got_late = lax.ppermute(last, ("batch", "vocab"), late)
        far = by_y(
            jnp.where(is_late, last, mine_early), jnp.where(is_late, got_late, got_early), 0
        )
        swapped_far = swapped(far)

        def own_pieces():
            return [a + b for a, b in zip(near_pieces, pieces(far, far_weight))]

        def other_pieces(*earlier):
            left = after(swapped_far, *earlier)
            return [
                a + b
                for a, b in zip(pieces(swapped_near, near_weight), pieces(left, far_weight))
            ]

        return (own_pieces, other_pieces), scale

    def gathered_parts():
        near_weight, far_weight = half_columns(head_weight), half_columns(take)
        whole = lax.all_gather(gained(rows, gain).reshape(2, seg, depth), "vocab", axis=2, tiled=True)
        whole = whole.reshape(2, seg, 2, 4, block).transpose(3, 2, 0, 1, 4)
        whole = lax.all_to_all(whole, "batch", split_axis=0, concat_axis=0)
        whole = whole.reshape(2, 2, 2, 2, seg, block).transpose(2, 0, 1, 3, 4, 5)
        swapped_whole = swapped(whole)

        def found(left):
            near, far = pick(left, core, 0), pick(left, 1 - core, 0)
            return [a + b for a, b in zip(pieces(near, near_weight), pieces(far, far_weight))]

        branches = (lambda: found(whole), lambda *earlier: found(after(swapped_whole, *earlier)))
        return branches, row_scale(near_squares + far_squares())

    lined = depth == 2 * block and vocab == 4
    branches, scale = line_parts() if lined else gathered_parts()
    kept, sends = [], []
    for branch in branches:
        found = branch(*(sends[-1] if sends else ()))
        found = [(piece * SHRINK).reshape(2, 2, seg, width // 2) for piece in found]
        sends.append((found[0].astype(SUM_TYPE), found[1].astype(SUM_TYPE)))
        kept.append((found[2], found[3]))
    halfway, more_sends = [], []
    for i in range(2):
        away_x = lax.ppermute(sends[i][0], "batch", X_SWAP)
        away_y = lax.ppermute(sends[i][1], "batch", Y_SWAP)
        if i == 0:
            away_x, away_y = after(away_x, *sends[1]), after(away_y, *sends[1])
        sum_x = kept[i][0] + away_x.astype(jnp.float32)
        sum_y = kept[i][1] + away_y.astype(jnp.float32)
        halfway.append((pick(sum_x, y, 1), pick(sum_y, x, 1)))
        more_sends.append(
            (pick(sum_x, 1 - y, 1).astype(SUM_TYPE), pick(sum_y, 1 - x, 1).astype(SUM_TYPE))
        )
    mine, theirs = [], []
    for i in range(2):
        next_y = lax.ppermute(more_sends[i][0], "batch", Y_SWAP)
        next_x = lax.ppermute(more_sends[i][1], "batch", X_SWAP)
        if i == 0:
            next_y, next_x = after(next_y, *more_sends[1]), after(next_x, *more_sends[1])
        sums = jnp.concatenate(
            [
                halfway[i][0] + next_y.astype(jnp.float32),
                halfway[i][1] + next_x.astype(jnp.float32),
            ],
            axis=-1,
        ).astype(SUM_TYPE)
        mine.append(pick(sums, core, 0))
        theirs.append(swapped(pick(sums, 1 - core, 0)))

    def scores(own, other, got_own, got_other, gain):
        low = jnp.where(core == 0, own, got_own)
        high = jnp.where(core == 0, got_other, other)
        return jnp.concatenate([low, high], axis=1).astype(jnp.float32) * gain[:, None]

    cond = scores(mine[0], mine[1], theirs[0], theirs[1], scale[0])
    uncond = scores(mine[1], mine[0], theirs[1], theirs[0], scale[1])
    guided = GUIDE * cond + (1.0 - GUIDE) * uncond

    def stats(values):
        peak = jnp.max(values, axis=1)
        return peak, jnp.sum(jnp.exp(values - peak[:, None]), axis=1)

    peak_c, sum_c = stats(cond)
    peak_g, sum_g = stats(guided)
    own = jnp.stack([peak_c, peak_g, sum_c, sum_g])
    every = jnp.stack(
        [own]
        + [
            lax.ppermute(own, "vocab", [(i, (i + k) % vocab) for i in range(vocab)])
            for k in range(1, vocab)
        ]
    )
    top = jnp.max(every[:, :2], axis=0)
    total = jnp.sum(every[:, 2:] * jnp.exp(every[:, :2] - top[None]), axis=0)
    norm = top + jnp.log(total)
    return (guided - norm[1][:, None], cond - norm[0][:, None])


def solution(mesh):
    in_specs = (P("pair", "batch", "vocab"), P("vocab"), P(("pair", "batch"), "vocab"))
    out_specs = (P(("pair", "batch"), "vocab"), P(("pair", "batch"), "vocab"))
    return jax.shard_map(
        on_device, mesh=mesh, in_specs=in_specs, out_specs=out_specs, check_vma=False
    )
```

```python
import jax
import jax.numpy as jnp
from jax import lax
from jax.sharding import PartitionSpec as P

EPS = 1e-05
GUIDE = 1.5
SHRINK = 1.0 / 32.0
SUM_TYPE = jnp.float16

X_SWAP = [(0, 1), (1, 0), (2, 3), (3, 2)]
Y_SWAP = [(0, 2), (2, 0), (1, 3), (3, 1)]
CORE_SWAP = [(0, 1), (1, 0)]


def pick(array, index, axis):
    return lax.dynamic_index_in_dim(array, index, axis, keepdims=False)


def after(value, *others):
    return lax.optimization_barrier((value, *others))[0]


def on_device(hidden, norm_gain, head_weight):
    core = lax.axis_index("pair")
    place = lax.axis_index("batch")
    level = lax.axis_index("vocab")
    vocab = lax.axis_size("vocab")
    y, x = place // 2, place % 2
    rows = hidden[0]
    seg = rows.shape[0] // 2
    depth = rows.shape[1]
    block, columns = head_weight.shape
    width = columns // 2
    model = depth * vocab

    wide = rows.astype(jnp.float32)
    gained = (wide * norm_gain.astype(jnp.float32)[None, :]).astype(jnp.bfloat16)
    gained = gained.reshape(2, seg, depth)

    take = lax.ppermute(head_weight, "pair", CORE_SWAP)

    def shifted(value, k):
        return lax.ppermute(value, "vocab", [(i, (i + k) % vocab) for i in range(vocab)])

    def paired(value, reach):
        return lax.ppermute(value, "vocab", [(i, i ^ reach) for i in range(vocab)])

    squares = jnp.sum(wide * wide, axis=1)
    if vocab == 4:
        squares += sum(shifted(squares, k) for k in range(1, vocab))
    else:
        reach = 1
        while reach < vocab:
            squares += paired(squares, reach)
            reach *= 2
    squares = squares.reshape(2, seg)

    def row_scale(*earlier):
        sent = [
            lax.ppermute(
                pick(after(squares, *earlier), core ^ k, 0),
                ("pair", "batch"),
                [(4 * s + b, 2 * b + (s ^ k)) for s in range(2) for b in range(4)],
            )
            for k in range(2)
        ]
        total = jnp.stack([jnp.where(x == 0, sent[0], sent[1]), jnp.where(x == 0, sent[1], sent[0])])
        return lax.rsqrt(total / model + EPS) / SHRINK

    def by_y(mine, other, axis):
        return jnp.stack([jnp.where(y == 0, mine, other), jnp.where(y == 0, other, mine)], axis)

    def swapped(value):
        return lax.ppermute(value, "pair", CORE_SWAP)

    def half_columns(weight, *earlier):
        return lax.dynamic_slice_in_dim(weight, after(core, *earlier) * width, width, 1)

    def dot(left, weight):
        return jnp.dot(left.reshape(-1, block), weight, preferred_element_type=jnp.float32)

    def line_parts():
        mine = lax.dynamic_slice_in_dim(gained, x * block, block, 2)
        other = lax.ppermute(
            lax.dynamic_slice_in_dim(gained, (1 - x) * block, block, 2), "batch", X_SWAP
        )
        own = jnp.stack([jnp.where(x == 0, mine, other), jnp.where(x == 0, other, mine)])
        own = after(own, squares)

        def up(value, k):
            return lax.ppermute(value, "vocab", [(z, z + 1) for z in range(k - 1, vocab - 1)])

        def down(value, k):
            return lax.ppermute(value, "vocab", [(z + 1, z) for z in range(vocab - k)])

        below, above = [own, up(own, 1)], [own, down(own, 1)]

        def quarter(place, reach):
            part = own
            for k in range(1, reach + 1):
                part = jnp.where(level - place == k, below[k], part)
                part = jnp.where(place - level == k, above[k], part)
            return part

        first = level // 2
        scale = row_scale(own)
        below[1], above[1] = after(below[1], scale), after(above[1], scale)
        near_sent = quarter(1 - y + 2 * first, 1)
        got_near = lax.ppermute(near_sent, "batch", Y_SWAP)
        below.append(up(below[1], 2))
        above.append(down(above[1], 2))
        keep_near = (core ^ first) == 0
        kept, taken = half_columns(head_weight, near_sent), half_columns(take, near_sent)
        near_weight, far_weight = lax.optimization_barrier(
            (jnp.where(keep_near, kept, taken), jnp.where(keep_near, taken, kept))
        )
        ready = (got_near, near_weight, far_weight)
        below[2], above[2] = after(below[2], *ready), after(above[2], *ready)
        near = by_y(quarter(y + 2 * first, 1), after(got_near, below[2], above[2]), 0)
        swapped_near = swapped(near)

        far = 1 - y + 2 * (1 - first)
        pairs = [(b * vocab + z, (b ^ 2) * vocab + z) for b in range(4) for z in range(vocab)]
        lone = [b * vocab + (vocab - 1) * (b // 2) for b in range(4)]
        early = [pair for pair in pairs if pair[0] not in lone]
        got_early = lax.ppermute(quarter(far, 2), ("batch", "vocab"), early)
        mine_early = lax.optimization_barrier(quarter(y + 2 * (1 - first), 2))
        is_late = (level == 0) & (y == 1) | (level == vocab - 1) & (y == 0)
        near_part = dot(near, near_weight)
        sent = after(own, below[2], above[2])
        ends = []
        for cross in (0, 2):
            moves = []
            for place in lone:
                b, z = divmod(place, vocab)
                moves.append(((b ^ cross) * vocab + z, b * vocab + vocab - 1 - z))
            ends.append(lax.ppermute(sent, ("batch", "vocab"), sorted(moves)))
        mine_late, got_late, got_early, _ = lax.optimization_barrier(
            (ends[0], ends[1], got_early, near_part)
        )
        far = by_y(
            jnp.where(is_late, mine_late, mine_early), jnp.where(is_late, got_late, got_early), 0
        )
        swapped_far = swapped(far)

        def own_part():
            return near_part + dot(far, far_weight)

        def other_part(*earlier):
            left = after(swapped_far, *earlier)
            return dot(swapped_near, near_weight) + dot(left, far_weight)

        return (own_part, other_part), scale

    def gathered_parts():
        near_weight, far_weight = half_columns(head_weight), half_columns(take)
        whole = lax.all_gather(gained, "vocab", axis=2, tiled=True)
        whole = whole.reshape(2, seg, 2, 4, block).transpose(3, 2, 0, 1, 4)
        whole = lax.all_to_all(whole, "batch", split_axis=0, concat_axis=0)
        whole = whole.reshape(2, 2, 2, 2, seg, block).transpose(2, 0, 1, 3, 4, 5)
        swapped_whole = swapped(whole)

        def part(left):
            return dot(pick(left, core, 0), near_weight) + dot(pick(left, 1 - core, 0), far_weight)

        return (lambda: part(whole), lambda *earlier: part(after(swapped_whole, *earlier))), row_scale()

    lined = depth == 2 * block and vocab == 4
    parts, scale = line_parts() if lined else gathered_parts()
    kept, sends = [], []
    for part in parts:
        whole = (part(*(sends[-1] if sends else ())) * SHRINK).reshape(2, 2, 2, seg, width)
        low, high = whole[..., : width // 2], whole[..., width // 2 :]
        kept.append((pick(low, x, 2), pick(high, y, 1)))
        sends.append(
            (pick(low, 1 - x, 2).astype(SUM_TYPE), pick(high, 1 - y, 1).astype(SUM_TYPE))
        )
    halfway, more_sends = [], []
    for i in range(2):
        away_x = lax.ppermute(sends[i][0], "batch", X_SWAP)
        away_y = lax.ppermute(sends[i][1], "batch", Y_SWAP)
        if i == 0:
            away_x, away_y = after(away_x, *sends[1]), after(away_y, *sends[1])
        sum_x = kept[i][0] + away_x.astype(jnp.float32)
        sum_y = kept[i][1] + away_y.astype(jnp.float32)
        halfway.append((pick(sum_x, y, 1), pick(sum_y, x, 1)))
        more_sends.append(
            (pick(sum_x, 1 - y, 1).astype(SUM_TYPE), pick(sum_y, 1 - x, 1).astype(SUM_TYPE))
        )
    mine, theirs = [], []
    for i in range(2):
        next_y = lax.ppermute(more_sends[i][0], "batch", Y_SWAP)
        next_x = lax.ppermute(more_sends[i][1], "batch", X_SWAP)
        if i == 0:
            next_y, next_x = after(next_y, *more_sends[1]), after(next_x, *more_sends[1])
        sums = jnp.concatenate(
            [
                halfway[i][0] + next_y.astype(jnp.float32),
                halfway[i][1] + next_x.astype(jnp.float32),
            ],
            axis=-1,
        ).astype(SUM_TYPE)
        mine.append(pick(sums, core, 0))
        theirs.append(swapped(pick(sums, 1 - core, 0)))

    def scores(own, other, got_own, got_other, gain):
        low = jnp.where(core == 0, own, got_own)
        high = jnp.where(core == 0, got_other, other)
        return jnp.concatenate([low, high], axis=1).astype(jnp.float32) * gain[:, None]

    cond = scores(mine[0], mine[1], theirs[0], theirs[1], scale[0])
    uncond = scores(mine[1], mine[0], theirs[1], theirs[0], scale[1])
    guided = GUIDE * cond + (1.0 - GUIDE) * uncond

    def stats(values):
        peak = jnp.max(values, axis=1)
        return peak, jnp.sum(jnp.exp(values - peak[:, None]), axis=1)

    peak_c, sum_c = stats(cond)
    peak_g, sum_g = stats(guided)
    own = jnp.stack([peak_c, peak_g, sum_c, sum_g])
    every = jnp.stack(
        [own]
        + [
            shifted(own, k) for k in range(1, vocab)
        ]
    )
    top = jnp.max(every[:, :2], axis=0)
    total = jnp.sum(every[:, 2:] * jnp.exp(every[:, :2] - top[None]), axis=0)
    norm = top + jnp.log(total)
    return (guided - norm[1][:, None], cond - norm[0][:, None])


def solution(mesh):
    in_specs = (P("pair", "batch", "vocab"), P("vocab"), P(("pair", "batch"), "vocab"))
    out_specs = (P(("pair", "batch"), "vocab"), P(("pair", "batch"), "vocab"))
    return jax.shard_map(
        on_device, mesh=mesh, in_specs=in_specs, out_specs=out_specs, check_vma=False
    )
```

```python
import jax
import jax.numpy as jnp
from jax import lax
from jax.sharding import PartitionSpec as P

EPS = 1e-05
GUIDE = 1.5
SHRINK = 1.0 / 32.0
SUM_TYPE = jnp.float16

X_SWAP = [(0, 1), (1, 0), (2, 3), (3, 2)]
Y_SWAP = [(0, 2), (2, 0), (1, 3), (3, 1)]
CORE_SWAP = [(0, 1), (1, 0)]


def pick(array, index, axis):
    return lax.dynamic_index_in_dim(array, index, axis, keepdims=False)


def after(value, *others):
    return lax.optimization_barrier((value, *others))[0]


def on_device(hidden, norm_gain, head_weight):
    core = lax.axis_index("pair")
    place = lax.axis_index("batch")
    level = lax.axis_index("vocab")
    vocab = lax.axis_size("vocab")
    y, x = place // 2, place % 2
    rows = hidden[0]
    seg = rows.shape[0] // 2
    depth = rows.shape[1]
    block, columns = head_weight.shape
    width = columns // 2
    model = depth * vocab

    wide = rows.astype(jnp.float32)
    gained = (wide * norm_gain.astype(jnp.float32)[None, :]).astype(jnp.bfloat16)
    gained = gained.reshape(2, seg, depth)

    take = lax.ppermute(head_weight, "pair", CORE_SWAP)

    def shifted(value, k):
        return lax.ppermute(value, "vocab", [(i, (i + k) % vocab) for i in range(vocab)])

    def paired(value, reach):
        return lax.ppermute(value, "vocab", [(i, i ^ reach) for i in range(vocab)])

    squares = jnp.sum(wide * wide, axis=1).reshape(2, seg)
    ending = [
        lax.ppermute(
            pick(squares, core ^ k, 0),
            ("pair", "batch"),
            [(4 * s + b, 2 * b + (s ^ k)) for s in range(2) for b in range(4)],
        )
        for k in range(2)
    ]

    def row_scale(*earlier):
        total = jnp.stack(
            [jnp.where(x == 0, ending[0], ending[1]), jnp.where(x == 0, ending[1], ending[0])]
        )
        if vocab == 4:
            total += sum(after(shifted(total, k), *earlier) for k in range(1, vocab))
        else:
            reach = 1
            while reach < vocab:
                total += paired(total, reach)
                reach *= 2
        return lax.rsqrt(total / model + EPS) / SHRINK

    def by_y(mine, other, axis):
        return jnp.stack([jnp.where(y == 0, mine, other), jnp.where(y == 0, other, mine)], axis)

    def swapped(value):
        return lax.ppermute(value, "pair", CORE_SWAP)

    def half_columns(weight, *earlier):
        return lax.dynamic_slice_in_dim(weight, after(core, *earlier) * width, width, 1)

    def dot(left, weight):
        return jnp.dot(left.reshape(-1, block), weight, preferred_element_type=jnp.float32)

    def line_parts():
        mine = lax.dynamic_slice_in_dim(gained, x * block, block, 2)

        def by_x(mine, other):
            return jnp.stack([jnp.where(x == 0, mine, other), jnp.where(x == 0, other, mine)])

        def up(value, k):
            return lax.ppermute(value, "vocab", [(z, z + 1) for z in range(k - 1, vocab - 1)])

        def down(value, k):
            return lax.ppermute(value, "vocab", [(z + 1, z) for z in range(vocab - k)])

        mine = after(mine, squares)
        mine_up, mine_down = up(mine, 1), down(mine, 1)
        other = lax.ppermute(
            lax.dynamic_slice_in_dim(gained, (1 - x) * block, block, 2), "batch", X_SWAP
        )
        other = after(other, mine_up, mine_down)
        own = by_x(mine, other)
        below = [own, by_x(mine_up, up(other, 1))]
        above = [own, by_x(mine_down, down(other, 1))]

        def quarter(place, reach):
            part = own
            for k in range(1, reach + 1):
                part = jnp.where(level - place == k, below[k], part)
                part = jnp.where(place - level == k, above[k], part)
            return part

        first = level // 2
        scale = row_scale(below[1], above[1])
        near_sent = quarter(1 - y + 2 * first, 1)
        got_near = lax.ppermute(near_sent, "batch", Y_SWAP)
        below.append(up(below[1], 2))
        above.append(down(above[1], 2))
        keep_near = (core ^ first) == 0
        kept, taken = half_columns(head_weight, near_sent), half_columns(take, near_sent)
        near_weight, far_weight = lax.optimization_barrier(
            (jnp.where(keep_near, kept, taken), jnp.where(keep_near, taken, kept))
        )
        ready = (got_near, near_weight, far_weight, scale)
        below[2], above[2] = after(below[2], *ready), after(above[2], *ready)
        near = by_y(quarter(y + 2 * first, 1), after(got_near, below[2], above[2]), 0)
        swapped_near = swapped(near)

        far = 1 - y + 2 * (1 - first)
        pairs = [(b * vocab + z, (b ^ 2) * vocab + z) for b in range(4) for z in range(vocab)]
        lone = [b * vocab + (vocab - 1) * (b // 2) for b in range(4)]
        early = [pair for pair in pairs if pair[0] not in lone]
        far_sent = quarter(far, 2)
        mine_early = lax.optimization_barrier(quarter(y + 2 * (1 - first), 2))
        is_late = (level == 0) & (y == 1) | (level == vocab - 1) & (y == 0)
        near_part = dot(near, near_weight)
        sent = after(own, below[2], above[2], far_sent, swapped_near)
        ends = []
        for cross in (0, 2):
            moves = []
            for place in lone:
                b, z = divmod(place, vocab)
                moves.append(((b ^ cross) * vocab + z, b * vocab + vocab - 1 - z))
            ends.append(lax.ppermute(sent, ("batch", "vocab"), sorted(moves)))
        got_early = lax.ppermute(far_sent, ("batch", "vocab"), early)
        mine_late, got_late, got_early, _ = lax.optimization_barrier(
            (ends[0], ends[1], got_early, near_part)
        )
        far = by_y(
            jnp.where(is_late, mine_late, mine_early), jnp.where(is_late, got_late, got_early), 0
        )
        swapped_far = swapped(far)

        def own_part():
            return near_part + dot(far, far_weight)

        def other_part(*earlier):
            left = after(swapped_far, *earlier)
            return dot(swapped_near, near_weight) + dot(left, far_weight)

        return (own_part, other_part), scale

    def gathered_parts():
        near_weight, far_weight = half_columns(head_weight), half_columns(take)
        whole = lax.all_gather(gained, "vocab", axis=2, tiled=True)
        whole = whole.reshape(2, seg, 2, 4, block).transpose(3, 2, 0, 1, 4)
        whole = lax.all_to_all(whole, "batch", split_axis=0, concat_axis=0)
        whole = whole.reshape(2, 2, 2, 2, seg, block).transpose(2, 0, 1, 3, 4, 5)
        swapped_whole = swapped(whole)

        def part(left):
            return dot(pick(left, core, 0), near_weight) + dot(pick(left, 1 - core, 0), far_weight)

        return (lambda: part(whole), lambda *earlier: part(after(swapped_whole, *earlier))), row_scale()

    lined = depth == 2 * block and vocab == 4
    parts, scale = line_parts() if lined else gathered_parts()
    kept, sends = [], []
    for part in parts:
        whole = (part(*(sends[-1] if sends else ())) * SHRINK).reshape(2, 2, 2, seg, width)
        low, high = whole[..., : width // 2], whole[..., width // 2 :]
        kept.append((pick(low, x, 2), pick(high, y, 1)))
        sends.append(
            (pick(low, 1 - x, 2).astype(SUM_TYPE), pick(high, 1 - y, 1).astype(SUM_TYPE))
        )
    halfway, more_sends = [], []
    for i in range(2):
        away_x = lax.ppermute(sends[i][0], "batch", X_SWAP)
        away_y = lax.ppermute(sends[i][1], "batch", Y_SWAP)
        if i == 0:
            away_x, away_y = after(away_x, *sends[1]), after(away_y, *sends[1])
        sum_x = kept[i][0] + away_x.astype(jnp.float32)
        sum_y = kept[i][1] + away_y.astype(jnp.float32)
        halfway.append((pick(sum_x, y, 1), pick(sum_y, x, 1)))
        more_sends.append(
            (pick(sum_x, 1 - y, 1).astype(SUM_TYPE), pick(sum_y, 1 - x, 1).astype(SUM_TYPE))
        )
    mine, theirs = [], []
    for i in range(2):
        next_y = lax.ppermute(more_sends[i][0], "batch", Y_SWAP)
        next_x = lax.ppermute(more_sends[i][1], "batch", X_SWAP)
        if i == 0:
            next_y, next_x = after(next_y, *more_sends[1]), after(next_x, *more_sends[1])
        sums = jnp.concatenate(
            [
                halfway[i][0] + next_y.astype(jnp.float32),
                halfway[i][1] + next_x.astype(jnp.float32),
            ],
            axis=-1,
        ).astype(SUM_TYPE)
        mine.append(pick(sums, core, 0))
        theirs.append(swapped(pick(sums, 1 - core, 0)))

    def scores(own, other, got_own, got_other, gain):
        low = jnp.where(core == 0, own, got_own)
        high = jnp.where(core == 0, got_other, other)
        return jnp.concatenate([low, high], axis=1).astype(jnp.float32) * gain[:, None]

    cond = scores(mine[0], mine[1], theirs[0], theirs[1], scale[0])
    uncond = scores(mine[1], mine[0], theirs[1], theirs[0], scale[1])
    guided = GUIDE * cond + (1.0 - GUIDE) * uncond

    def stats(values):
        peak = jnp.max(values, axis=1)
        return peak, jnp.sum(jnp.exp(values - peak[:, None]), axis=1)

    peak_c, sum_c = stats(cond)
    peak_g, sum_g = stats(guided)
    own = jnp.stack([peak_c, peak_g, sum_c, sum_g])
    every = jnp.stack(
        [own]
        + [
            shifted(own, k) for k in range(1, vocab)
        ]
    )
    top = jnp.max(every[:, :2], axis=0)
    total = jnp.sum(every[:, 2:] * jnp.exp(every[:, :2] - top[None]), axis=0)
    norm = top + jnp.log(total)
    return (guided - norm[1][:, None], cond - norm[0][:, None])


def solution(mesh):
    in_specs = (P("pair", "batch", "vocab"), P("vocab"), P(("pair", "batch"), "vocab"))
    out_specs = (P(("pair", "batch"), "vocab"), P(("pair", "batch"), "vocab"))
    return jax.shard_map(
        on_device, mesh=mesh, in_specs=in_specs, out_specs=out_specs, check_vma=False
    )
```

```python
import jax
import jax.numpy as jnp
from jax import lax
from jax.sharding import PartitionSpec as P

EPS = 1e-05
GUIDE = 1.5
SHRINK = 1.0 / 32.0
SUM_TYPE = jnp.float16

X_SWAP = [(0, 1), (1, 0), (2, 3), (3, 2)]
Y_SWAP = [(0, 2), (2, 0), (1, 3), (3, 1)]
CORE_SWAP = [(0, 1), (1, 0)]


def pick(array, index, axis):
    return lax.dynamic_index_in_dim(array, index, axis, keepdims=False)


def after(value, *others):
    return lax.optimization_barrier((value, *others))[0]


def on_device(hidden, norm_gain, head_weight):
    core = lax.axis_index("pair")
    place = lax.axis_index("batch")
    level = lax.axis_index("vocab")
    vocab = lax.axis_size("vocab")
    y, x = place // 2, place % 2
    rows = hidden[0]
    seg = rows.shape[0] // 2
    depth = rows.shape[1]
    block, columns = head_weight.shape
    width = columns // 2
    model = depth * vocab

    wide = rows.astype(jnp.float32)
    gained = (wide * norm_gain.astype(jnp.float32)[None, :]).astype(jnp.bfloat16)
    gained = gained.reshape(2, seg, depth)

    take = lax.ppermute(head_weight, "pair", CORE_SWAP)

    def shifted(value, k):
        return lax.ppermute(value, "vocab", [(i, (i + k) % vocab) for i in range(vocab)])

    def paired(value, reach):
        return lax.ppermute(value, "vocab", [(i, i ^ reach) for i in range(vocab)])

    squares = jnp.sum(wide * wide, axis=1)
    if vocab == 4:
        squares += sum(shifted(squares, k) for k in range(1, vocab))
    else:
        reach = 1
        while reach < vocab:
            squares += paired(squares, reach)
            reach *= 2
    squares = squares.reshape(2, seg)

    def row_scale(*earlier):
        sent = [
            lax.ppermute(
                pick(after(squares, *earlier), core ^ k, 0),
                ("pair", "batch"),
                [(4 * s + b, 2 * b + (s ^ k)) for s in range(2) for b in range(4)],
            )
            for k in range(2)
        ]
        total = jnp.stack([jnp.where(x == 0, sent[0], sent[1]), jnp.where(x == 0, sent[1], sent[0])])
        return lax.rsqrt(total / model + EPS) / SHRINK

    def by_y(mine, other, axis):
        return jnp.stack([jnp.where(y == 0, mine, other), jnp.where(y == 0, other, mine)], axis)

    def swapped(value):
        return lax.ppermute(value, "pair", CORE_SWAP)

    def half_columns(weight, *earlier):
        return lax.dynamic_slice_in_dim(weight, after(core, *earlier) * width, width, 1)

    def dot(left, weight):
        return jnp.dot(left.reshape(-1, block), weight, preferred_element_type=jnp.float32)

    def line_parts():
        mine = lax.dynamic_slice_in_dim(gained, x * block, block, 2)
        other = lax.ppermute(
            lax.dynamic_slice_in_dim(gained, (1 - x) * block, block, 2), "batch", X_SWAP
        )
        own = jnp.stack([jnp.where(x == 0, mine, other), jnp.where(x == 0, other, mine)])
        own = after(own, squares)

        def up(value, k):
            return lax.ppermute(value, "vocab", [(z, z + 1) for z in range(k - 1, vocab - 1)])

        def down(value, k):
            return lax.ppermute(value, "vocab", [(z + 1, z) for z in range(vocab - k)])

        below, above = [own, up(own, 1)], [own, down(own, 1)]

        def quarter(place, reach):
            part = own
            for k in range(1, reach + 1):
                part = jnp.where(level - place == k, below[k], part)
                part = jnp.where(place - level == k, above[k], part)
            return part

        first = level // 2
        scale = row_scale(own)
        below[1], above[1] = after(below[1], scale), after(above[1], scale)
        near_sent = quarter(1 - y + 2 * first, 1)
        got_near = lax.ppermute(near_sent, "batch", Y_SWAP)
        below.append(up(below[1], 2))
        above.append(down(above[1], 2))
        keep_near = (core ^ first) == 0
        kept, taken = half_columns(head_weight, near_sent), half_columns(take, near_sent)
        near_weight, far_weight = lax.optimization_barrier(
            (jnp.where(keep_near, kept, taken), jnp.where(keep_near, taken, kept))
        )
        ready = (got_near, near_weight, far_weight)
        below[2], above[2] = after(below[2], *ready), after(above[2], *ready)
        near = by_y(quarter(y + 2 * first, 1), after(got_near, below[2], above[2]), 0)
        swapped_near = swapped(near)

        far = 1 - y + 2 * (1 - first)
        pairs = [(b * vocab + z, (b ^ 2) * vocab + z) for b in range(4) for z in range(vocab)]
        lone = [b * vocab + (vocab - 1) * (b // 2) for b in range(4)]
        early = [pair for pair in pairs if pair[0] not in lone]
        got_early = lax.ppermute(quarter(far, 2), ("batch", "vocab"), early)
        mine_early = lax.optimization_barrier(quarter(y + 2 * (1 - first), 2))
        is_late = (level == 0) & (y == 1) | (level == vocab - 1) & (y == 0)
        near_part = dot(near, near_weight)
        sent = after(own, near_weight, far_weight)
        ends = []
        for cross in (0, 2):
            moves = []
            for place in lone:
                b, z = divmod(place, vocab)
                moves.append(((b ^ cross) * vocab + z, b * vocab + vocab - 1 - z))
            ends.append(lax.ppermute(sent, ("batch", "vocab"), sorted(moves)))
        mine_late, got_late, got_early, _ = lax.optimization_barrier(
            (ends[0], ends[1], got_early, near_part)
        )
        far = by_y(
            jnp.where(is_late, mine_late, mine_early), jnp.where(is_late, got_late, got_early), 0
        )
        swapped_far = swapped(far)

        def own_part():
            return near_part + dot(far, far_weight)

        def other_part(*earlier):
            left = after(swapped_far, *earlier)
            return dot(swapped_near, near_weight) + dot(left, far_weight)

        return (own_part, other_part), scale

    def gathered_parts():
        near_weight, far_weight = half_columns(head_weight), half_columns(take)
        whole = lax.all_gather(gained, "vocab", axis=2, tiled=True)
        whole = whole.reshape(2, seg, 2, 4, block).transpose(3, 2, 0, 1, 4)
        whole = lax.all_to_all(whole, "batch", split_axis=0, concat_axis=0)
        whole = whole.reshape(2, 2, 2, 2, seg, block).transpose(2, 0, 1, 3, 4, 5)
        swapped_whole = swapped(whole)

        def part(left):
            return dot(pick(left, core, 0), near_weight) + dot(pick(left, 1 - core, 0), far_weight)

        return (lambda: part(whole), lambda *earlier: part(after(swapped_whole, *earlier))), row_scale()

    lined = depth == 2 * block and vocab == 4
    parts, scale = line_parts() if lined else gathered_parts()
    kept, sends = [], []
    for part in parts:
        whole = (part(*(sends[-1] if sends else ())) * SHRINK).reshape(2, 2, 2, seg, width)
        low, high = whole[..., : width // 2], whole[..., width // 2 :]
        kept.append((pick(low, x, 2), pick(high, y, 1)))
        sends.append(
            (pick(low, 1 - x, 2).astype(SUM_TYPE), pick(high, 1 - y, 1).astype(SUM_TYPE))
        )
    halfway, more_sends = [], []
    for i in range(2):
        away_x = lax.ppermute(sends[i][0], "batch", X_SWAP)
        away_y = lax.ppermute(sends[i][1], "batch", Y_SWAP)
        if i == 0:
            away_x, away_y = after(away_x, *sends[1]), after(away_y, *sends[1])
        sum_x = kept[i][0] + away_x.astype(jnp.float32)
        sum_y = kept[i][1] + away_y.astype(jnp.float32)
        halfway.append((pick(sum_x, y, 1), pick(sum_y, x, 1)))
        more_sends.append(
            (pick(sum_x, 1 - y, 1).astype(SUM_TYPE), pick(sum_y, 1 - x, 1).astype(SUM_TYPE))
        )
    mine, theirs = [], []
    for i in range(2):
        next_y = lax.ppermute(more_sends[i][0], "batch", Y_SWAP)
        next_x = lax.ppermute(more_sends[i][1], "batch", X_SWAP)
        if i == 0:
            next_y, next_x = after(next_y, *more_sends[1]), after(next_x, *more_sends[1])
        sums = jnp.concatenate(
            [
                halfway[i][0] + next_y.astype(jnp.float32),
                halfway[i][1] + next_x.astype(jnp.float32),
            ],
            axis=-1,
        ).astype(SUM_TYPE)
        mine.append(pick(sums, core, 0))
        theirs.append(swapped(pick(sums, 1 - core, 0)))

    def scores(own, other, got_own, got_other, gain):
        low = jnp.where(core == 0, own, got_own)
        high = jnp.where(core == 0, got_other, other)
        return jnp.concatenate([low, high], axis=1).astype(jnp.float32) * gain[:, None]

    cond = scores(mine[0], mine[1], theirs[0], theirs[1], scale[0])
    uncond = scores(mine[1], mine[0], theirs[1], theirs[0], scale[1])
    guided = GUIDE * cond + (1.0 - GUIDE) * uncond

    def stats(values):
        peak = jnp.max(values, axis=1)
        return peak, jnp.sum(jnp.exp(values - peak[:, None]), axis=1)

    peak_c, sum_c = stats(cond)
    peak_g, sum_g = stats(guided)
    own = jnp.stack([peak_c, peak_g, sum_c, sum_g])
    every = jnp.stack(
        [own]
        + [
            shifted(own, k) for k in range(1, vocab)
        ]
    )
    top = jnp.max(every[:, :2], axis=0)
    total = jnp.sum(every[:, 2:] * jnp.exp(every[:, :2] - top[None]), axis=0)
    norm = top + jnp.log(total)
    return (guided - norm[1][:, None], cond - norm[0][:, None])


def solution(mesh):
    in_specs = (P("pair", "batch", "vocab"), P("vocab"), P(("pair", "batch"), "vocab"))
    out_specs = (P(("pair", "batch"), "vocab"), P(("pair", "batch"), "vocab"))
    return jax.shard_map(
        on_device, mesh=mesh, in_specs=in_specs, out_specs=out_specs, check_vma=False
    )
```

```python
import functools

import jax
import jax.numpy as jnp
from jax import lax
from jax.sharding import PartitionSpec as P

EPS = 1e-05
GUIDE = 1.5
SHRINK = 1.0 / 32.0
SUM_TYPE = jnp.float16
CHUNKS = 2

X_SWAP = [(0, 1), (1, 0), (2, 3), (3, 2)]
Y_SWAP = [(0, 2), (2, 0), (1, 3), (3, 1)]
CORE_SWAP = [(0, 1), (1, 0)]


def pick(array, index, axis):
    return lax.dynamic_index_in_dim(array, index, axis, keepdims=False)


def after(value, *others):
    return lax.optimization_barrier((value, *others))[0]


def on_device(hidden, norm_gain, head_weight):
    core = lax.axis_index("pair")
    place = lax.axis_index("batch")
    level = lax.axis_index("vocab")
    vocab = lax.axis_size("vocab")
    y, x = place // 2, place % 2
    rows = hidden[0]
    seg = rows.shape[0] // 2
    depth = rows.shape[1]
    block, columns = head_weight.shape
    width = columns // 2
    model = depth * vocab
    step = seg // CHUNKS

    wide = rows.astype(jnp.float32)
    gained = (wide * norm_gain.astype(jnp.float32)[None, :]).astype(jnp.bfloat16)
    gained = gained.reshape(2, CHUNKS, step, depth).transpose(1, 0, 2, 3)

    take = lax.ppermute(head_weight, "pair", CORE_SWAP)

    def shifted(value, k):
        return lax.ppermute(value, "vocab", [(i, (i + k) % vocab) for i in range(vocab)])

    def paired(value, reach):
        return lax.ppermute(value, "vocab", [(i, i ^ reach) for i in range(vocab)])

    squares = jnp.sum(wide * wide, axis=1)
    if vocab == 4:
        squares += sum(shifted(squares, k) for k in range(1, vocab))
    else:
        reach = 1
        while reach < vocab:
            squares += paired(squares, reach)
            reach *= 2
    squares = squares.reshape(2, seg)

    def row_scale(*earlier):
        sent = [
            lax.ppermute(
                pick(after(squares, *earlier), core ^ k, 0),
                ("pair", "batch"),
                [(4 * s + b, 2 * b + (s ^ k)) for s in range(2) for b in range(4)],
            )
            for k in range(2)
        ]
        total = jnp.stack([jnp.where(x == 0, sent[0], sent[1]), jnp.where(x == 0, sent[1], sent[0])])
        return lax.rsqrt(total / model + EPS) / SHRINK

    def by_y(mine, other, axis):
        return jnp.stack([jnp.where(y == 0, mine, other), jnp.where(y == 0, other, mine)], axis)

    def swapped(value):
        return lax.ppermute(value, "pair", CORE_SWAP)

    def half_columns(weight, *earlier):
        return lax.dynamic_slice_in_dim(weight, after(core, *earlier) * width, width, 1)

    def dot(left, weight):
        return jnp.dot(left.reshape(-1, block), weight, preferred_element_type=jnp.float32)

    def line_parts():
        mine = lax.dynamic_slice_in_dim(gained, x * block, block, 3)
        other = lax.ppermute(
            lax.dynamic_slice_in_dim(gained, (1 - x) * block, block, 3), "batch", X_SWAP
        )
        own = jnp.stack([jnp.where(x == 0, mine, other), jnp.where(x == 0, other, mine)], axis=1)
        own = after(own, squares)

        def up(value, k):
            return lax.ppermute(value, "vocab", [(z, z + 1) for z in range(k - 1, vocab - 1)])

        def down(value, k):
            return lax.ppermute(value, "vocab", [(z + 1, z) for z in range(vocab - k)])

        below, above = [own, up(own, 1)], [own, down(own, 1)]

        def quarter(place, reach):
            part = own
            for k in range(1, reach + 1):
                part = jnp.where(level - place == k, below[k], part)
                part = jnp.where(place - level == k, above[k], part)
            return part

        first = level // 2
        scale = row_scale(own)
        below[1], above[1] = after(below[1], scale), after(above[1], scale)
        near_sent = quarter(1 - y + 2 * first, 1)
        got_near = lax.ppermute(near_sent, "batch", Y_SWAP)
        below.append(up(below[1], 2))
        above.append(down(above[1], 2))
        keep_near = (core ^ first) == 0
        kept, taken = half_columns(head_weight, near_sent), half_columns(take, near_sent)
        near_weight, far_weight = lax.optimization_barrier(
            (jnp.where(keep_near, kept, taken), jnp.where(keep_near, taken, kept))
        )
        ready = (got_near, near_weight, far_weight)
        below[2], above[2] = after(below[2], *ready), after(above[2], *ready)
        near = by_y(quarter(y + 2 * first, 1), after(got_near, below[2], above[2]), 1)
        swapped_near = swapped(near)

        far = 1 - y + 2 * (1 - first)
        pairs = [(b * vocab + z, (b ^ 2) * vocab + z) for b in range(4) for z in range(vocab)]
        lone = [b * vocab + (vocab - 1) * (b // 2) for b in range(4)]
        early = [pair for pair in pairs if pair[0] not in lone]
        far_sent = quarter(far, 2)
        got_early = [
            lax.ppermute(far_sent[c], ("batch", "vocab"), early) for c in range(CHUNKS)
        ]
        mine_early = lax.optimization_barrier(quarter(y + 2 * (1 - first), 2))
        is_late = (level == 0) & (y == 1) | (level == vocab - 1) & (y == 0)
        near_part = dot(near, near_weight).reshape(CHUNKS, -1, width)
        sent = after(own, below[2], above[2])
        ends = []
        for cross in (0, 2):
            moves = []
            for place in lone:
                b, z = divmod(place, vocab)
                moves.append(((b ^ cross) * vocab + z, b * vocab + vocab - 1 - z))
            ends.append(lax.ppermute(sent, ("batch", "vocab"), sorted(moves)))
        mine_late, got_late, got_early[0], _ = lax.optimization_barrier(
            (ends[0], ends[1], got_early[0], near_part)
        )

        def far_rows(c, *earlier):
            got = after(got_early[c], *earlier)
            return by_y(
                jnp.where(is_late, mine_late[c], mine_early[c]),
                jnp.where(is_late, got_late[c], got),
                0,
            )

        swapped_far = []

        def own_part(c, *earlier):
            rows = far_rows(c, *earlier)
            swapped_far.append(swapped(rows))
            return (near_part[c] + dot(rows, far_weight))[None]

        def other_part(*earlier):
            near_other = dot(swapped_near, near_weight).reshape(CHUNKS, -1, width)
            found = [
                near_other[c] + dot(after(swapped_far[c], *earlier), far_weight)
                for c in range(CHUNKS)
            ]
            return jnp.stack(found)

        own_parts = [functools.partial(own_part, c) for c in range(CHUNKS)]
        return (*own_parts, other_part), scale

    def gathered_parts():
        near_weight, far_weight = half_columns(head_weight), half_columns(take)
        whole = lax.all_gather(gained, "vocab", axis=3, tiled=True)
        whole = whole.reshape(CHUNKS, 2, step, 2, 4, block).transpose(4, 3, 0, 1, 2, 5)
        whole = lax.all_to_all(whole, "batch", split_axis=0, concat_axis=0)
        whole = whole.reshape(2, 2, 2, CHUNKS, 2, step, block).transpose(2, 3, 0, 1, 4, 5, 6)
        swapped_whole = swapped(whole)

        def part(left):
            near, far = pick(left, core, 0), pick(left, 1 - core, 0)
            found = dot(near, near_weight) + dot(far, far_weight)
            return found.reshape(near.shape[0], -1, width)

        def own_part(c, *earlier):
            return part(after(whole, *earlier)[:, c : c + 1])

        def other_part(*earlier):
            return part(after(swapped_whole, *earlier))

        own_parts = [functools.partial(own_part, c) for c in range(CHUNKS)]
        return (*own_parts, other_part), row_scale()

    lined = depth == 2 * block and vocab == 4
    parts, scale = line_parts() if lined else gathered_parts()
    groups = len(parts)
    kept, sends = [], []
    for part in parts:
        whole = part(*(sends[-1] if sends else ())) * SHRINK
        whole = whole.reshape(-1, 2, 2, 2, step, width)
        low, high = whole[..., : width // 2], whole[..., width // 2 :]
        kept.append((pick(low, x, 3), pick(high, y, 2)))
        sends.append(
            (pick(low, 1 - x, 3).astype(SUM_TYPE), pick(high, 1 - y, 2).astype(SUM_TYPE))
        )
    halfway, more_sends = [], []
    for i in range(groups):
        away_x = lax.ppermute(sends[i][0], "batch", X_SWAP)
        away_y = lax.ppermute(sends[i][1], "batch", Y_SWAP)
        if i + 1 < groups:
            away_x, away_y = after(away_x, *sends[i + 1]), after(away_y, *sends[i + 1])
        sum_x = kept[i][0] + away_x.astype(jnp.float32)
        sum_y = kept[i][1] + away_y.astype(jnp.float32)
        halfway.append((pick(sum_x, y, 2), pick(sum_y, x, 2)))
        more_sends.append(
            (pick(sum_x, 1 - y, 2).astype(SUM_TYPE), pick(sum_y, 1 - x, 2).astype(SUM_TYPE))
        )
    mine, theirs = [], []
    for i in range(groups):
        next_y = lax.ppermute(more_sends[i][0], "batch", Y_SWAP)
        next_x = lax.ppermute(more_sends[i][1], "batch", X_SWAP)
        if i + 1 < groups:
            next_y, next_x = after(next_y, *more_sends[i + 1]), after(next_x, *more_sends[i + 1])
        sums = jnp.concatenate(
            [
                halfway[i][0] + next_y.astype(jnp.float32),
                halfway[i][1] + next_x.astype(jnp.float32),
            ],
            axis=-1,
        ).astype(SUM_TYPE)
        mine.append(pick(sums, core, 1))
        theirs.append(swapped(pick(sums, 1 - core, 1)))

    def by_branch(found):
        own = jnp.concatenate(found[:-1]).reshape(seg, width)
        return own, found[-1].reshape(seg, width)

    mine, theirs = by_branch(mine), by_branch(theirs)

    def scores(own, other, got_own, got_other, gain):
        low = jnp.where(core == 0, own, got_own)
        high = jnp.where(core == 0, got_other, other)
        return jnp.concatenate([low, high], axis=1).astype(jnp.float32) * gain[:, None]

    cond = scores(mine[0], mine[1], theirs[0], theirs[1], scale[0])
    uncond = scores(mine[1], mine[0], theirs[1], theirs[0], scale[1])
    guided = GUIDE * cond + (1.0 - GUIDE) * uncond

    def stats(values):
        peak = jnp.max(values, axis=1)
        return peak, jnp.sum(jnp.exp(values - peak[:, None]), axis=1)

    peak_c, sum_c = stats(cond)
    peak_g, sum_g = stats(guided)
    own = jnp.stack([peak_c, peak_g, sum_c, sum_g])
    every = jnp.stack(
        [own]
        + [
            shifted(own, k) for k in range(1, vocab)
        ]
    )
    top = jnp.max(every[:, :2], axis=0)
    total = jnp.sum(every[:, 2:] * jnp.exp(every[:, :2] - top[None]), axis=0)
    norm = top + jnp.log(total)
    return (guided - norm[1][:, None], cond - norm[0][:, None])


def solution(mesh):
    in_specs = (P("pair", "batch", "vocab"), P("vocab"), P(("pair", "batch"), "vocab"))
    out_specs = (P(("pair", "batch"), "vocab"), P(("pair", "batch"), "vocab"))
    return jax.shard_map(
        on_device, mesh=mesh, in_specs=in_specs, out_specs=out_specs, check_vma=False
    )
```

```python
import jax
import jax.numpy as jnp
from jax import lax
from jax.sharding import PartitionSpec as P

EPS = 1e-05
GUIDE = 1.5
SHRINK = 1.0 / 32.0
SUM_TYPE = jnp.float16

X_SWAP = [(0, 1), (1, 0), (2, 3), (3, 2)]
Y_SWAP = [(0, 2), (2, 0), (1, 3), (3, 1)]
CORE_SWAP = [(0, 1), (1, 0)]


def pick(array, index, axis):
    return lax.dynamic_index_in_dim(array, index, axis, keepdims=False)


def after(value, *others):
    return lax.optimization_barrier((value, *others))[0]


def on_device(hidden, norm_gain, head_weight):
    core = lax.axis_index("pair")
    place = lax.axis_index("batch")
    level = lax.axis_index("vocab")
    vocab = lax.axis_size("vocab")
    y, x = place // 2, place % 2
    rows = hidden[0]
    seg = rows.shape[0] // 2
    depth = rows.shape[1]
    block, columns = head_weight.shape
    width = columns // 2
    model = depth * vocab

    wide = rows.astype(jnp.float32)
    gained = (wide * norm_gain.astype(jnp.float32)[None, :]).astype(jnp.bfloat16)
    gained = gained.reshape(2, seg, depth)

    take = lax.ppermute(head_weight, "pair", CORE_SWAP)

    def shifted(value, k):
        return lax.ppermute(value, "vocab", [(i, (i + k) % vocab) for i in range(vocab)])

    def paired(value, reach):
        return lax.ppermute(value, "vocab", [(i, i ^ reach) for i in range(vocab)])

    squares = jnp.sum(wide * wide, axis=1)
    if vocab == 4:
        squares += sum(shifted(squares, k) for k in range(1, vocab))
    else:
        reach = 1
        while reach < vocab:
            squares += paired(squares, reach)
            reach *= 2
    squares = squares.reshape(2, seg)

    def row_scale(*earlier):
        sent = [
            lax.ppermute(
                pick(after(squares, *earlier), core ^ k, 0),
                ("pair", "batch"),
                [(4 * s + b, 2 * b + (s ^ k)) for s in range(2) for b in range(4)],
            )
            for k in range(2)
        ]
        total = jnp.stack([jnp.where(x == 0, sent[0], sent[1]), jnp.where(x == 0, sent[1], sent[0])])
        return lax.rsqrt(total / model + EPS) / SHRINK

    def by_y(mine, other, axis):
        return jnp.stack([jnp.where(y == 0, mine, other), jnp.where(y == 0, other, mine)], axis)

    def swapped(value):
        return lax.ppermute(value, "pair", CORE_SWAP)

    def half_columns(weight, *earlier):
        return lax.dynamic_slice_in_dim(weight, after(core, *earlier) * width, width, 1)

    def dot(left, weight):
        return jnp.dot(left.reshape(-1, block), weight, preferred_element_type=jnp.float32)

    def line_parts():
        mine = lax.dynamic_slice_in_dim(gained, x * block, block, 2)
        other = lax.ppermute(
            lax.dynamic_slice_in_dim(gained, (1 - x) * block, block, 2), "batch", X_SWAP
        )
        own = jnp.stack([jnp.where(x == 0, mine, other), jnp.where(x == 0, other, mine)])
        own = after(own, squares)

        def up(value, k):
            return lax.ppermute(value, "vocab", [(z, z + 1) for z in range(k - 1, vocab - 1)])

        def down(value, k):
            return lax.ppermute(value, "vocab", [(z + 1, z) for z in range(vocab - k)])

        below, above = [own, up(own, 1)], [own, down(own, 1)]

        def quarter(place, reach):
            part = own
            for k in range(1, reach + 1):
                part = jnp.where(level - place == k, below[k], part)
                part = jnp.where(place - level == k, above[k], part)
            return part

        first = level // 2
        scale = row_scale(own)
        below[1], above[1] = after(below[1], scale), after(above[1], scale)
        near_sent = quarter(1 - y + 2 * first, 1)
        got_near = lax.ppermute(near_sent, "batch", Y_SWAP)
        below.append(up(below[1], 2))
        above.append(down(above[1], 2))
        keep_near = (core ^ first) == 0
        kept, taken = half_columns(head_weight, near_sent), half_columns(take, near_sent)
        near_weight, far_weight = lax.optimization_barrier(
            (jnp.where(keep_near, kept, taken), jnp.where(keep_near, taken, kept))
        )
        ready = (got_near, near_weight, far_weight)
        below[2], above[2] = after(below[2], *ready), after(above[2], *ready)
        near = by_y(quarter(y + 2 * first, 1), after(got_near, below[2], above[2]), 0)
        swapped_near = swapped(near)

        far = 1 - y + 2 * (1 - first)
        pairs = [(b * vocab + z, (b ^ 2) * vocab + z) for b in range(4) for z in range(vocab)]
        lone = [b * vocab + (vocab - 1) * (b // 2) for b in range(4)]
        early = [pair for pair in pairs if pair[0] not in lone]
        far_sent = quarter(far, 2)
        got_early = lax.ppermute(far_sent, ("batch", "vocab"), early)
        mine_early = lax.optimization_barrier(quarter(y + 2 * (1 - first), 2))
        is_late = (level == 0) & (y == 1) | (level == vocab - 1) & (y == 0)
        near_part = dot(near, near_weight)
        sent = after(own, below[2], above[2], far_sent)
        ends = []
        for cross in (0, 2):
            moves = []
            for place in lone:
                b, z = divmod(place, vocab)
                moves.append(((b ^ cross) * vocab + z, b * vocab + vocab - 1 - z))
            ends.append(lax.ppermute(sent, ("batch", "vocab"), sorted(moves)))
        got_early = after(got_early, near_part)
        mine_late, got_late = after(ends[0], got_early), after(ends[1], got_early)
        far = by_y(
            jnp.where(is_late, mine_late, mine_early), jnp.where(is_late, got_late, got_early), 0
        )
        swapped_far = swapped(far)

        def own_part():
            return near_part + dot(far, far_weight)

        def other_part(*earlier):
            left = after(swapped_far, *earlier)
            return dot(swapped_near, near_weight) + dot(left, far_weight)

        return (own_part, other_part), scale

    def gathered_parts():
        near_weight, far_weight = half_columns(head_weight), half_columns(take)
        whole = lax.all_gather(gained, "vocab", axis=2, tiled=True)
        whole = whole.reshape(2, seg, 2, 4, block).transpose(3, 2, 0, 1, 4)
        whole = lax.all_to_all(whole, "batch", split_axis=0, concat_axis=0)
        whole = whole.reshape(2, 2, 2, 2, seg, block).transpose(2, 0, 1, 3, 4, 5)
        swapped_whole = swapped(whole)

        def part(left):
            return dot(pick(left, core, 0), near_weight) + dot(pick(left, 1 - core, 0), far_weight)

        return (lambda: part(whole), lambda *earlier: part(after(swapped_whole, *earlier))), row_scale()

    lined = depth == 2 * block and vocab == 4
    parts, scale = line_parts() if lined else gathered_parts()
    kept, sends = [], []
    for part in parts:
        whole = (part(*(sends[-1] if sends else ())) * SHRINK).reshape(2, 2, 2, seg, width)
        low, high = whole[..., : width // 2], whole[..., width // 2 :]
        kept.append((pick(low, x, 2), pick(high, y, 1)))
        sends.append(
            (pick(low, 1 - x, 2).astype(SUM_TYPE), pick(high, 1 - y, 1).astype(SUM_TYPE))
        )
    halfway, more_sends = [], []
    for i in range(2):
        away_x = lax.ppermute(sends[i][0], "batch", X_SWAP)
        away_y = lax.ppermute(sends[i][1], "batch", Y_SWAP)
        if i == 0:
            away_x, away_y = after(away_x, *sends[1]), after(away_y, *sends[1])
        sum_x = kept[i][0] + away_x.astype(jnp.float32)
        sum_y = kept[i][1] + away_y.astype(jnp.float32)
        halfway.append((pick(sum_x, y, 1), pick(sum_y, x, 1)))
        more_sends.append(
            (pick(sum_x, 1 - y, 1).astype(SUM_TYPE), pick(sum_y, 1 - x, 1).astype(SUM_TYPE))
        )
    mine, theirs = [], []
    for i in range(2):
        next_y = lax.ppermute(more_sends[i][0], "batch", Y_SWAP)
        next_x = lax.ppermute(more_sends[i][1], "batch", X_SWAP)
        if i == 0:
            next_y, next_x = after(next_y, *more_sends[1]), after(next_x, *more_sends[1])
        sums = jnp.concatenate(
            [
                halfway[i][0] + next_y.astype(jnp.float32),
                halfway[i][1] + next_x.astype(jnp.float32),
            ],
            axis=-1,
        ).astype(SUM_TYPE)
        mine.append(pick(sums, core, 0))
        theirs.append(swapped(pick(sums, 1 - core, 0)))

    def scores(own, other, got_own, got_other, gain):
        low = jnp.where(core == 0, own, got_own)
        high = jnp.where(core == 0, got_other, other)
        return jnp.concatenate([low, high], axis=1).astype(jnp.float32) * gain[:, None]

    cond = scores(mine[0], mine[1], theirs[0], theirs[1], scale[0])
    uncond = scores(mine[1], mine[0], theirs[1], theirs[0], scale[1])
    guided = GUIDE * cond + (1.0 - GUIDE) * uncond

    def stats(values):
        peak = jnp.max(values, axis=1)
        return peak, jnp.sum(jnp.exp(values - peak[:, None]), axis=1)

    peak_c, sum_c = stats(cond)
    peak_g, sum_g = stats(guided)
    own = jnp.stack([peak_c, peak_g, sum_c, sum_g])
    every = jnp.stack(
        [own]
        + [
            shifted(own, k) for k in range(1, vocab)
        ]
    )
    top = jnp.max(every[:, :2], axis=0)
    total = jnp.sum(every[:, 2:] * jnp.exp(every[:, :2] - top[None]), axis=0)
    norm = top + jnp.log(total)
    return (guided - norm[1][:, None], cond - norm[0][:, None])


def solution(mesh):
    in_specs = (P("pair", "batch", "vocab"), P("vocab"), P(("pair", "batch"), "vocab"))
    out_specs = (P(("pair", "batch"), "vocab"), P(("pair", "batch"), "vocab"))
    return jax.shard_map(
        on_device, mesh=mesh, in_specs=in_specs, out_specs=out_specs, check_vma=False
    )
```

```python
import jax
import jax.numpy as jnp
from jax import lax
from jax.sharding import PartitionSpec as P

EPS = 1e-05
GUIDE = 1.5
SHRINK = 1.0 / 32.0
SUM_TYPE = jnp.float16

X_SWAP = [(0, 1), (1, 0), (2, 3), (3, 2)]
Y_SWAP = [(0, 2), (2, 0), (1, 3), (3, 1)]
CORE_SWAP = [(0, 1), (1, 0)]


def pick(array, index, axis):
    return lax.dynamic_index_in_dim(array, index, axis, keepdims=False)


def after(value, *others):
    return lax.optimization_barrier((value, *others))[0]


def on_device(hidden, norm_gain, head_weight):
    core = lax.axis_index("pair")
    place = lax.axis_index("batch")
    level = lax.axis_index("vocab")
    vocab = lax.axis_size("vocab")
    y, x = place // 2, place % 2
    rows = hidden[0]
    seg = rows.shape[0] // 2
    depth = rows.shape[1]
    block, columns = head_weight.shape
    width = columns // 2
    model = depth * vocab

    wide = rows.astype(jnp.float32)
    gained = (wide * norm_gain.astype(jnp.float32)[None, :]).astype(jnp.bfloat16)
    gained = gained.reshape(2, seg, depth)

    take = lax.ppermute(head_weight, "pair", CORE_SWAP)

    def shifted(value, k):
        return lax.ppermute(value, "vocab", [(i, (i + k) % vocab) for i in range(vocab)])

    def paired(value, reach):
        return lax.ppermute(value, "vocab", [(i, i ^ reach) for i in range(vocab)])

    squares = jnp.sum(wide * wide, axis=1).reshape(2, seg)

    def row_squares(*earlier):
        ending = [
            lax.ppermute(
                pick(after(squares, *earlier), core ^ k, 0),
                ("pair", "batch"),
                [(4 * s + b, 2 * b + (s ^ k)) for s in range(2) for b in range(4)],
            )
            for k in range(2)
        ]
        return jnp.stack(
            [jnp.where(x == 0, ending[0], ending[1]), jnp.where(x == 0, ending[1], ending[0])]
        )

    def row_scale(total):
        if vocab == 4:
            total += sum(shifted(total, k) for k in range(1, vocab))
        else:
            reach = 1
            while reach < vocab:
                total += paired(total, reach)
                reach *= 2
        return lax.rsqrt(total / model + EPS) / SHRINK

    def by_y(mine, other, axis):
        return jnp.stack([jnp.where(y == 0, mine, other), jnp.where(y == 0, other, mine)], axis)

    def swapped(value):
        return lax.ppermute(value, "pair", CORE_SWAP)

    def half_columns(weight, *earlier):
        return lax.dynamic_slice_in_dim(weight, after(core, *earlier) * width, width, 1)

    def dot(left, weight):
        return jnp.dot(left.reshape(-1, block), weight, preferred_element_type=jnp.float32)

    def line_parts():
        mine = lax.dynamic_slice_in_dim(gained, x * block, block, 2)
        other = lax.ppermute(
            lax.dynamic_slice_in_dim(gained, (1 - x) * block, block, 2), "batch", X_SWAP
        )
        own = jnp.stack([jnp.where(x == 0, mine, other), jnp.where(x == 0, other, mine)])

        def up(value, k):
            return lax.ppermute(value, "vocab", [(z, z + 1) for z in range(k - 1, vocab - 1)])

        def down(value, k):
            return lax.ppermute(value, "vocab", [(z + 1, z) for z in range(vocab - k)])

        below, above = [own, up(own, 1)], [own, down(own, 1)]

        def quarter(place, reach):
            part = own
            for k in range(1, reach + 1):
                part = jnp.where(level - place == k, below[k], part)
                part = jnp.where(place - level == k, above[k], part)
            return part

        first = level // 2
        ending = row_squares(own)
        below[1], above[1] = after(below[1], ending), after(above[1], ending)
        near_sent = quarter(1 - y + 2 * first, 1)
        got_near = lax.ppermute(near_sent, "batch", Y_SWAP)
        below.append(up(below[1], 2))
        above.append(down(above[1], 2))
        keep_near = (core ^ first) == 0
        kept, taken = half_columns(head_weight, near_sent), half_columns(take, near_sent)
        near_weight, far_weight = lax.optimization_barrier(
            (jnp.where(keep_near, kept, taken), jnp.where(keep_near, taken, kept))
        )
        ready = (near_weight, far_weight)
        below[2], above[2] = after(below[2], *ready), after(above[2], *ready)
        near = by_y(quarter(y + 2 * first, 1), after(got_near, below[2], above[2]), 0)
        swapped_near = swapped(near)

        far = 1 - y + 2 * (1 - first)
        pairs = [(b * vocab + z, (b ^ 2) * vocab + z) for b in range(4) for z in range(vocab)]
        lone = [b * vocab + (vocab - 1) * (b // 2) for b in range(4)]
        early = [pair for pair in pairs if pair[0] not in lone]
        far_sent = quarter(far, 2)
        got_early = lax.ppermute(far_sent, ("batch", "vocab"), early)
        mine_early = lax.optimization_barrier(quarter(y + 2 * (1 - first), 2))
        is_late = (level == 0) & (y == 1) | (level == vocab - 1) & (y == 0)
        near_part = dot(near, near_weight)
        sent = after(own, below[2], above[2])
        ends = []
        for cross in (0, 2):
            moves = []
            for place in lone:
                b, z = divmod(place, vocab)
                moves.append(((b ^ cross) * vocab + z, b * vocab + vocab - 1 - z))
            ends.append(lax.ppermute(sent, ("batch", "vocab"), sorted(moves)))
        scale = row_scale(after(ending, far_sent))
        mine_late, got_late, got_early, _, _ = lax.optimization_barrier(
            (ends[0], ends[1], got_early, near_part, scale)
        )
        far = by_y(
            jnp.where(is_late, mine_late, mine_early), jnp.where(is_late, got_late, got_early), 0
        )
        swapped_far = swapped(far)

        def own_part():
            return near_part + dot(far, far_weight)

        def other_part(*earlier):
            left = after(swapped_far, *earlier)
            return dot(swapped_near, near_weight) + dot(left, far_weight)

        return (own_part, other_part), scale

    def gathered_parts():
        near_weight, far_weight = half_columns(head_weight), half_columns(take)
        whole = lax.all_gather(gained, "vocab", axis=2, tiled=True)
        whole = whole.reshape(2, seg, 2, 4, block).transpose(3, 2, 0, 1, 4)
        whole = lax.all_to_all(whole, "batch", split_axis=0, concat_axis=0)
        whole = whole.reshape(2, 2, 2, 2, seg, block).transpose(2, 0, 1, 3, 4, 5)
        swapped_whole = swapped(whole)

        def part(left):
            return dot(pick(left, core, 0), near_weight) + dot(pick(left, 1 - core, 0), far_weight)

        return (lambda: part(whole), lambda *earlier: part(after(swapped_whole, *earlier))), row_scale(row_squares())

    lined = depth == 2 * block and vocab == 4
    parts, scale = line_parts() if lined else gathered_parts()
    kept, sends = [], []
    for part in parts:
        whole = (part(*(sends[-1] if sends else ())) * SHRINK).reshape(2, 2, 2, seg, width)
        low, high = whole[..., : width // 2], whole[..., width // 2 :]
        kept.append((pick(low, x, 2), pick(high, y, 1)))
        sends.append(
            (pick(low, 1 - x, 2).astype(SUM_TYPE), pick(high, 1 - y, 1).astype(SUM_TYPE))
        )
    halfway, more_sends = [], []
    for i in range(2):
        away_x = lax.ppermute(sends[i][0], "batch", X_SWAP)
        away_y = lax.ppermute(sends[i][1], "batch", Y_SWAP)
        if i == 0:
            away_x, away_y = after(away_x, *sends[1]), after(away_y, *sends[1])
        sum_x = kept[i][0] + away_x.astype(jnp.float32)
        sum_y = kept[i][1] + away_y.astype(jnp.float32)
        halfway.append((pick(sum_x, y, 1), pick(sum_y, x, 1)))
        more_sends.append(
            (pick(sum_x, 1 - y, 1).astype(SUM_TYPE), pick(sum_y, 1 - x, 1).astype(SUM_TYPE))
        )
    mine, theirs = [], []
    for i in range(2):
        next_y = lax.ppermute(more_sends[i][0], "batch", Y_SWAP)
        next_x = lax.ppermute(more_sends[i][1], "batch", X_SWAP)
        if i == 0:
            next_y, next_x = after(next_y, *more_sends[1]), after(next_x, *more_sends[1])
        sums = jnp.concatenate(
            [
                halfway[i][0] + next_y.astype(jnp.float32),
                halfway[i][1] + next_x.astype(jnp.float32),
            ],
            axis=-1,
        ).astype(SUM_TYPE)
        mine.append(pick(sums, core, 0))
        theirs.append(swapped(pick(sums, 1 - core, 0)))

    def scores(own, other, got_own, got_other, gain):
        low = jnp.where(core == 0, own, got_own)
        high = jnp.where(core == 0, got_other, other)
        return jnp.concatenate([low, high], axis=1).astype(jnp.float32) * gain[:, None]

    cond = scores(mine[0], mine[1], theirs[0], theirs[1], scale[0])
    uncond = scores(mine[1], mine[0], theirs[1], theirs[0], scale[1])
    guided = GUIDE * cond + (1.0 - GUIDE) * uncond

    def stats(values):
        peak = jnp.max(values, axis=1)
        return peak, jnp.sum(jnp.exp(values - peak[:, None]), axis=1)

    peak_c, sum_c = stats(cond)
    peak_g, sum_g = stats(guided)
    own = jnp.stack([peak_c, peak_g, sum_c, sum_g])
    every = jnp.stack(
        [own]
        + [
            shifted(own, k) for k in range(1, vocab)
        ]
    )
    top = jnp.max(every[:, :2], axis=0)
    total = jnp.sum(every[:, 2:] * jnp.exp(every[:, :2] - top[None]), axis=0)
    norm = top + jnp.log(total)
    return (guided - norm[1][:, None], cond - norm[0][:, None])


def solution(mesh):
    in_specs = (P("pair", "batch", "vocab"), P("vocab"), P(("pair", "batch"), "vocab"))
    out_specs = (P(("pair", "batch"), "vocab"), P(("pair", "batch"), "vocab"))
    return jax.shard_map(
        on_device, mesh=mesh, in_specs=in_specs, out_specs=out_specs, check_vma=False
    )
```

```python
import jax
import jax.numpy as jnp
from jax import lax
from jax.sharding import PartitionSpec as P

EPS = 1e-05
GUIDE = 1.5
SHRINK = 1.0 / 32.0
SUM_TYPE = jnp.float16

X_SWAP = [(0, 1), (1, 0), (2, 3), (3, 2)]
Y_SWAP = [(0, 2), (2, 0), (1, 3), (3, 1)]
CORE_SWAP = [(0, 1), (1, 0)]


def pick(array, index, axis):
    return lax.dynamic_index_in_dim(array, index, axis, keepdims=False)


def after(value, *others):
    return lax.optimization_barrier((value, *others))[0]


def on_device(hidden, norm_gain, head_weight):
    core = lax.axis_index("pair")
    place = lax.axis_index("batch")
    level = lax.axis_index("vocab")
    vocab = lax.axis_size("vocab")
    y, x = place // 2, place % 2
    rows = hidden[0]
    seg = rows.shape[0] // 2
    depth = rows.shape[1]
    block, columns = head_weight.shape
    width = columns // 2
    model = depth * vocab

    wide = rows.astype(jnp.float32)
    gained = (wide * norm_gain.astype(jnp.float32)[None, :]).astype(jnp.bfloat16)
    gained = gained.reshape(2, seg, depth)

    take = lax.ppermute(head_weight, "pair", CORE_SWAP)

    def shifted(value, k):
        return lax.ppermute(value, "vocab", [(i, (i + k) % vocab) for i in range(vocab)])

    def paired(value, reach):
        return lax.ppermute(value, "vocab", [(i, i ^ reach) for i in range(vocab)])

    squares = jnp.sum(wide * wide, axis=1)
    if vocab == 4:
        squares += sum(shifted(squares, k) for k in range(1, vocab))
    else:
        reach = 1
        while reach < vocab:
            squares += paired(squares, reach)
            reach *= 2
    squares = squares.reshape(2, seg)

    def row_scale(*earlier):
        sent = [
            lax.ppermute(
                pick(after(squares, *earlier), core ^ k, 0),
                ("pair", "batch"),
                [(4 * s + b, 2 * b + (s ^ k)) for s in range(2) for b in range(4)],
            )
            for k in range(2)
        ]
        total = jnp.stack([jnp.where(x == 0, sent[0], sent[1]), jnp.where(x == 0, sent[1], sent[0])])
        return lax.rsqrt(total / model + EPS) / SHRINK

    def by_y(mine, other, axis):
        return jnp.stack([jnp.where(y == 0, mine, other), jnp.where(y == 0, other, mine)], axis)

    def swapped(value):
        return lax.ppermute(value, "pair", CORE_SWAP)

    def half_columns(weight, *earlier):
        return lax.dynamic_slice_in_dim(weight, after(core, *earlier) * width, width, 1)

    def dot(left, weight):
        return jnp.dot(left.reshape(-1, block), weight, preferred_element_type=jnp.float32)

    def line_parts():
        mine = lax.dynamic_slice_in_dim(gained, x * block, block, 2)
        other = lax.ppermute(
            lax.dynamic_slice_in_dim(gained, (1 - x) * block, block, 2), "batch", X_SWAP
        )
        own = jnp.stack([jnp.where(x == 0, mine, other), jnp.where(x == 0, other, mine)])
        own = after(own, squares)

        def up(value, k):
            return lax.ppermute(value, "vocab", [(z, z + 1) for z in range(k - 1, vocab - 1)])

        def down(value, k):
            return lax.ppermute(value, "vocab", [(z + 1, z) for z in range(vocab - k)])

        below, above = [own, up(own, 1)], [own, down(own, 1)]

        def quarter(place, reach):
            part = own
            for k in range(1, reach + 1):
                part = jnp.where(level - place == k, below[k], part)
                part = jnp.where(place - level == k, above[k], part)
            return part

        first = level // 2
        scale = row_scale(own)
        below[1], above[1] = after(below[1], scale), after(above[1], scale)
        near_sent = quarter(1 - y + 2 * first, 1)
        got_near = lax.ppermute(near_sent, "batch", Y_SWAP)
        below.append(up(below[1], 2))
        above.append(down(above[1], 2))
        keep_near = (core ^ first) == 0
        kept, taken = half_columns(head_weight, near_sent), half_columns(take, near_sent)
        near_weight, far_weight = lax.optimization_barrier(
            (jnp.where(keep_near, kept, taken), jnp.where(keep_near, taken, kept))
        )
        ready = (got_near, near_weight, far_weight)
        below[2], above[2] = after(below[2], *ready), after(above[2], *ready)
        near = by_y(quarter(y + 2 * first, 1), after(got_near, below[2], above[2]), 0)
        swapped_near = swapped(near)

        far = 1 - y + 2 * (1 - first)
        pairs = [(b * vocab + z, (b ^ 2) * vocab + z) for b in range(4) for z in range(vocab)]
        lone = [b * vocab + (vocab - 1) * (b // 2) for b in range(4)]
        early = [pair for pair in pairs if pair[0] not in lone]
        got_early = lax.ppermute(quarter(far, 2), ("batch", "vocab"), early)
        mine_early = lax.optimization_barrier(quarter(y + 2 * (1 - first), 2))
        is_late = (level == 0) & (y == 1) | (level == vocab - 1) & (y == 0)
        near_part = dot(near, near_weight)
        sent = after(own, below[2], above[2])
        ends = []
        for cross in (0, 2):
            moves = []
            for place in lone:
                b, z = divmod(place, vocab)
                moves.append(((b ^ cross) * vocab + z, b * vocab + vocab - 1 - z))
            ends.append(lax.ppermute(sent, ("batch", "vocab"), sorted(moves)))
        mine_late, got_late, got_early, _ = lax.optimization_barrier(
            (ends[0], ends[1], got_early, near_part)
        )
        far = by_y(
            jnp.where(is_late, mine_late, mine_early), jnp.where(is_late, got_late, got_early), 0
        )
        swapped_far = swapped(far)

        def halves(near, left):
            return [
                near[:, low : low + width // 2] + dot(left, far_weight[:, low : low + width // 2])
                for low in (0, width // 2)
            ]

        def own_part():
            return halves(near_part, far)

        def other_part(*earlier):
            left = after(swapped_far, *earlier)
            return halves(dot(swapped_near, near_weight), left)

        return (own_part, other_part), scale

    def gathered_parts():
        near_weight, far_weight = half_columns(head_weight), half_columns(take)
        whole = lax.all_gather(gained, "vocab", axis=2, tiled=True)
        whole = whole.reshape(2, seg, 2, 4, block).transpose(3, 2, 0, 1, 4)
        whole = lax.all_to_all(whole, "batch", split_axis=0, concat_axis=0)
        whole = whole.reshape(2, 2, 2, 2, seg, block).transpose(2, 0, 1, 3, 4, 5)
        swapped_whole = swapped(whole)

        def part(left):
            near, far = pick(left, core, 0), pick(left, 1 - core, 0)
            found = dot(near, near_weight) + dot(far, far_weight)
            return found[:, : width // 2], found[:, width // 2 :]

        return (lambda: part(whole), lambda *earlier: part(after(swapped_whole, *earlier))), row_scale()

    lined = depth == 2 * block and vocab == 4
    parts, scale = line_parts() if lined else gathered_parts()
    kept, sends = [], []
    for part in parts:
        low, high = (
            (half * SHRINK).reshape(2, 2, 2, seg, width // 2)
            for half in part(*(sends[-1] if sends else ()))
        )
        kept.append((pick(low, x, 2), pick(high, y, 1)))
        sends.append(
            (pick(low, 1 - x, 2).astype(SUM_TYPE), pick(high, 1 - y, 1).astype(SUM_TYPE))
        )
    halfway, more_sends = [], []
    for i in range(2):
        away_x = lax.ppermute(sends[i][0], "batch", X_SWAP)
        away_y = lax.ppermute(sends[i][1], "batch", Y_SWAP)
        if i == 0:
            away_x, away_y = after(away_x, *sends[1]), after(away_y, *sends[1])
        sum_x = kept[i][0] + away_x.astype(jnp.float32)
        sum_y = kept[i][1] + away_y.astype(jnp.float32)
        halfway.append((pick(sum_x, y, 1), pick(sum_y, x, 1)))
        more_sends.append(
            (pick(sum_x, 1 - y, 1).astype(SUM_TYPE), pick(sum_y, 1 - x, 1).astype(SUM_TYPE))
        )
    mine, theirs = [], []
    for i in range(2):
        next_y = lax.ppermute(more_sends[i][0], "batch", Y_SWAP)
        next_x = lax.ppermute(more_sends[i][1], "batch", X_SWAP)
        if i == 0:
            next_y, next_x = after(next_y, *more_sends[1]), after(next_x, *more_sends[1])
        sums = jnp.concatenate(
            [
                halfway[i][0] + next_y.astype(jnp.float32),
                halfway[i][1] + next_x.astype(jnp.float32),
            ],
            axis=-1,
        ).astype(SUM_TYPE)
        mine.append(pick(sums, core, 0))
        theirs.append(swapped(pick(sums, 1 - core, 0)))

    def scores(own, other, got_own, got_other, gain):
        low = jnp.where(core == 0, own, got_own)
        high = jnp.where(core == 0, got_other, other)
        return jnp.concatenate([low, high], axis=1).astype(jnp.float32) * gain[:, None]

    cond = scores(mine[0], mine[1], theirs[0], theirs[1], scale[0])
    uncond = scores(mine[1], mine[0], theirs[1], theirs[0], scale[1])
    guided = GUIDE * cond + (1.0 - GUIDE) * uncond

    def stats(values):
        peak = jnp.max(values, axis=1)
        return peak, jnp.sum(jnp.exp(values - peak[:, None]), axis=1)

    peak_c, sum_c = stats(cond)
    peak_g, sum_g = stats(guided)
    own = jnp.stack([peak_c, peak_g, sum_c, sum_g])
    every = jnp.stack(
        [own]
        + [
            shifted(own, k) for k in range(1, vocab)
        ]
    )
    top = jnp.max(every[:, :2], axis=0)
    total = jnp.sum(every[:, 2:] * jnp.exp(every[:, :2] - top[None]), axis=0)
    norm = top + jnp.log(total)
    return (guided - norm[1][:, None], cond - norm[0][:, None])


def solution(mesh):
    in_specs = (P("pair", "batch", "vocab"), P("vocab"), P(("pair", "batch"), "vocab"))
    out_specs = (P(("pair", "batch"), "vocab"), P(("pair", "batch"), "vocab"))
    return jax.shard_map(
        on_device, mesh=mesh, in_specs=in_specs, out_specs=out_specs, check_vma=False
    )
```

```python
import jax
import jax.numpy as jnp
from jax import lax
from jax.sharding import PartitionSpec as P

EPS = 1e-05
GUIDE = 1.5
SHRINK = 1.0 / 32.0
SUM_TYPE = jnp.float16

X_SWAP = [(0, 1), (1, 0), (2, 3), (3, 2)]
Y_SWAP = [(0, 2), (2, 0), (1, 3), (3, 1)]
CORE_SWAP = [(0, 1), (1, 0)]


def pick(array, index, axis):
    return lax.dynamic_index_in_dim(array, index, axis, keepdims=False)


def after(value, *others):
    return lax.optimization_barrier((value, *others))[0]


def on_device(hidden, norm_gain, head_weight):
    core = lax.axis_index("pair")
    place = lax.axis_index("batch")
    level = lax.axis_index("vocab")
    vocab = lax.axis_size("vocab")
    y, x = place // 2, place % 2
    rows = hidden[0]
    seg = rows.shape[0] // 2
    depth = rows.shape[1]
    block, columns = head_weight.shape
    width = columns // 2
    model = depth * vocab

    wide = rows.astype(jnp.float32)
    gained = (wide * norm_gain.astype(jnp.float32)[None, :]).astype(jnp.bfloat16)
    gained = gained.reshape(2, seg, depth)

    take = lax.ppermute(head_weight, "pair", CORE_SWAP)

    def shifted(value, k):
        return lax.ppermute(value, "vocab", [(i, (i + k) % vocab) for i in range(vocab)])

    def paired(value, reach):
        return lax.ppermute(value, "vocab", [(i, i ^ reach) for i in range(vocab)])

    squares = jnp.sum(wide * wide, axis=1)
    if vocab == 4:
        squares += sum(shifted(squares, k) for k in range(1, vocab))
    else:
        reach = 1
        while reach < vocab:
            squares += paired(squares, reach)
            reach *= 2
    squares = squares.reshape(2, seg)

    def row_scale(*earlier):
        sent = [
            lax.ppermute(
                pick(after(squares, *earlier), core ^ k, 0),
                ("pair", "batch"),
                [(4 * s + b, 2 * b + (s ^ k)) for s in range(2) for b in range(4)],
            )
            for k in range(2)
        ]
        total = jnp.stack([jnp.where(x == 0, sent[0], sent[1]), jnp.where(x == 0, sent[1], sent[0])])
        return lax.rsqrt(total / model + EPS) / SHRINK

    def by_y(mine, other, axis):
        return jnp.stack([jnp.where(y == 0, mine, other), jnp.where(y == 0, other, mine)], axis)

    def swapped(value):
        return lax.ppermute(value, "pair", CORE_SWAP)

    def half_columns(weight, *earlier):
        return lax.dynamic_slice_in_dim(weight, after(core, *earlier) * width, width, 1)

    def dot(left, weight):
        return jnp.dot(left.reshape(-1, block), weight, preferred_element_type=jnp.float32)

    def line_parts():
        mine = lax.dynamic_slice_in_dim(gained, x * block, block, 2)
        other = lax.ppermute(
            lax.dynamic_slice_in_dim(gained, (1 - x) * block, block, 2), "batch", X_SWAP
        )
        own = jnp.stack([jnp.where(x == 0, mine, other), jnp.where(x == 0, other, mine)])
        own = after(own, squares)

        def up(value, k):
            return lax.ppermute(value, "vocab", [(z, z + 1) for z in range(k - 1, vocab - 1)])

        def down(value, k):
            return lax.ppermute(value, "vocab", [(z + 1, z) for z in range(vocab - k)])

        below, above = [own, up(own, 1)], [own, down(own, 1)]

        def quarter(place, reach, least=0):
            part = below[least]
            if least:
                part = jnp.where(level > place, part, above[least])
            for k in range(least + 1, reach + 1):
                part = jnp.where(level - place == k, below[k], part)
                part = jnp.where(place - level == k, above[k], part)
            return part

        first = level // 2
        scale = row_scale(own)
        below[1], above[1] = after(below[1], scale), after(above[1], scale)
        near_sent = quarter(1 - y + 2 * first, 1)
        got_near = lax.ppermute(near_sent, "batch", Y_SWAP)
        below.append(up(below[1], 2))
        above.append(down(above[1], 2))
        keep_near = (core ^ first) == 0
        kept, taken = half_columns(head_weight, near_sent), half_columns(take, near_sent)
        near_weight, far_weight = lax.optimization_barrier(
            (jnp.where(keep_near, kept, taken), jnp.where(keep_near, taken, kept))
        )
        ready = (got_near, near_weight, far_weight)
        below[2], above[2] = after(below[2], *ready), after(above[2], *ready)
        near = by_y(quarter(y + 2 * first, 1), after(got_near, below[2], above[2]), 0)
        swapped_near = swapped(near)

        far = 1 - y + 2 * (1 - first)
        pairs = [(b * vocab + z, (b ^ 2) * vocab + z) for b in range(4) for z in range(vocab)]
        lone = [b * vocab + (vocab - 1) * (b // 2) for b in range(4)]
        early = [pair for pair in pairs if pair[0] not in lone]
        got_early = lax.ppermute(quarter(far, 2, 1), ("batch", "vocab"), early)
        mine_early = lax.optimization_barrier(quarter(y + 2 * (1 - first), 2, 1))
        is_late = (level == 0) & (y == 1) | (level == vocab - 1) & (y == 0)
        near_part = dot(near, near_weight)
        sent = after(own, below[2], above[2])
        ends = []
        for cross in (0, 2):
            moves = []
            for place in lone:
                b, z = divmod(place, vocab)
                moves.append(((b ^ cross) * vocab + z, b * vocab + vocab - 1 - z))
            ends.append(lax.ppermute(sent, ("batch", "vocab"), sorted(moves)))
        mine_late, got_late, got_early, _ = lax.optimization_barrier(
            (ends[0], ends[1], got_early, near_part)
        )
        far = by_y(
            jnp.where(is_late, mine_late, mine_early), jnp.where(is_late, got_late, got_early), 0
        )
        swapped_far = swapped(far)

        def halves(near, left):
            return [
                near[:, low : low + width // 2] + dot(left, far_weight[:, low : low + width // 2])
                for low in (0, width // 2)
            ]

        def own_part():
            return halves(near_part, far)

        def other_part(*earlier):
            left = after(swapped_far, *earlier)
            return halves(dot(swapped_near, near_weight), left)

        return (own_part, other_part), scale

    def gathered_parts():
        near_weight, far_weight = half_columns(head_weight), half_columns(take)
        whole = lax.all_gather(gained, "vocab", axis=2, tiled=True)
        whole = whole.reshape(2, seg, 2, 4, block).transpose(3, 2, 0, 1, 4)
        whole = lax.all_to_all(whole, "batch", split_axis=0, concat_axis=0)
        whole = whole.reshape(2, 2, 2, 2, seg, block).transpose(2, 0, 1, 3, 4, 5)
        swapped_whole = swapped(whole)

        def part(left):
            near, far = pick(left, core, 0), pick(left, 1 - core, 0)
            found = dot(near, near_weight) + dot(far, far_weight)
            return found[:, : width // 2], found[:, width // 2 :]

        return (lambda: part(whole), lambda *earlier: part(after(swapped_whole, *earlier))), row_scale()

    lined = depth == 2 * block and vocab == 4
    parts, scale = line_parts() if lined else gathered_parts()
    kept, sends = [], []
    for part in parts:
        low, high = (
            (half * SHRINK).reshape(2, 2, 2, seg, width // 2)
            for half in part(*(sends[-1] if sends else ()))
        )
        kept.append((pick(low, x, 2), pick(high, y, 1)))
        sends.append(
            (pick(low, 1 - x, 2).astype(SUM_TYPE), pick(high, 1 - y, 1).astype(SUM_TYPE))
        )
    halfway, more_sends = [], []
    for i in range(2):
        away_x = lax.ppermute(sends[i][0], "batch", X_SWAP)
        away_y = lax.ppermute(sends[i][1], "batch", Y_SWAP)
        if i == 0:
            away_x, away_y = after(away_x, *sends[1]), after(away_y, *sends[1])
        sum_x = kept[i][0] + away_x.astype(jnp.float32)
        sum_y = kept[i][1] + away_y.astype(jnp.float32)
        halfway.append((pick(sum_x, y, 1), pick(sum_y, x, 1)))
        more_sends.append(
            (pick(sum_x, 1 - y, 1).astype(SUM_TYPE), pick(sum_y, 1 - x, 1).astype(SUM_TYPE))
        )
    mine, theirs = [], []
    for i in range(2):
        next_y = lax.ppermute(more_sends[i][0], "batch", Y_SWAP)
        next_x = lax.ppermute(more_sends[i][1], "batch", X_SWAP)
        if i == 0:
            next_y, next_x = after(next_y, *more_sends[1]), after(next_x, *more_sends[1])
        sums = jnp.concatenate(
            [
                halfway[i][0] + next_y.astype(jnp.float32),
                halfway[i][1] + next_x.astype(jnp.float32),
            ],
            axis=-1,
        ).astype(SUM_TYPE)
        mine.append(pick(sums, core, 0))
        theirs.append(swapped(pick(sums, 1 - core, 0)))

    def scores(own, other, got_own, got_other, gain):
        low = jnp.where(core == 0, own, got_own)
        high = jnp.where(core == 0, got_other, other)
        return jnp.concatenate([low, high], axis=1).astype(jnp.float32) * gain[:, None]

    cond = scores(mine[0], mine[1], theirs[0], theirs[1], scale[0])
    uncond = scores(mine[1], mine[0], theirs[1], theirs[0], scale[1])
    guided = GUIDE * cond + (1.0 - GUIDE) * uncond

    def stats(values):
        peak = jnp.max(values, axis=1)
        return peak, jnp.sum(jnp.exp(values - peak[:, None]), axis=1)

    peak_c, sum_c = stats(cond)
    peak_g, sum_g = stats(guided)
    own = jnp.stack([peak_c, peak_g, sum_c, sum_g])
    every = jnp.stack(
        [own]
        + [
            shifted(own, k) for k in range(1, vocab)
        ]
    )
    top = jnp.max(every[:, :2], axis=0)
    total = jnp.sum(every[:, 2:] * jnp.exp(every[:, :2] - top[None]), axis=0)
    norm = top + jnp.log(total)
    return (guided - norm[1][:, None], cond - norm[0][:, None])


def solution(mesh):
    in_specs = (P("pair", "batch", "vocab"), P("vocab"), P(("pair", "batch"), "vocab"))
    out_specs = (P(("pair", "batch"), "vocab"), P(("pair", "batch"), "vocab"))
    return jax.shard_map(
        on_device, mesh=mesh, in_specs=in_specs, out_specs=out_specs, check_vma=False
    )
```

```python
import jax
import jax.numpy as jnp
from jax import lax
from jax.sharding import PartitionSpec as P

EPS = 1e-05
GUIDE = 1.5
SHRINK = 1.0 / 32.0
SUM_TYPE = jnp.float16

X_SWAP = [(0, 1), (1, 0), (2, 3), (3, 2)]
Y_SWAP = [(0, 2), (2, 0), (1, 3), (3, 1)]
CORE_SWAP = [(0, 1), (1, 0)]


def pick(array, index, axis):
    return lax.dynamic_index_in_dim(array, index, axis, keepdims=False)


def after(value, *others):
    return lax.optimization_barrier((value, *others))[0]


def on_device(hidden, norm_gain, head_weight):
    core = lax.axis_index("pair")
    place = lax.axis_index("batch")
    level = lax.axis_index("vocab")
    vocab = lax.axis_size("vocab")
    y, x = place // 2, place % 2
    rows = hidden[0]
    seg = rows.shape[0] // 2
    depth = rows.shape[1]
    block, columns = head_weight.shape
    width = columns // 2
    model = depth * vocab

    wide = rows.astype(jnp.float32)
    gained = (wide * norm_gain.astype(jnp.float32)[None, :]).astype(jnp.bfloat16)
    gained = gained.reshape(2, seg, depth)

    take = lax.ppermute(head_weight, "pair", CORE_SWAP)

    def shifted(value, k):
        return lax.ppermute(value, "vocab", [(i, (i + k) % vocab) for i in range(vocab)])

    def paired(value, reach):
        return lax.ppermute(value, "vocab", [(i, i ^ reach) for i in range(vocab)])

    squares = jnp.sum(wide * wide, axis=1)
    if vocab == 4:
        squares += sum(shifted(squares, k) for k in range(1, vocab))
    else:
        reach = 1
        while reach < vocab:
            squares += paired(squares, reach)
            reach *= 2
    squares = squares.reshape(2, seg)

    def row_scale(*earlier):
        sent = [
            lax.ppermute(
                pick(after(squares, *earlier), core ^ k, 0),
                ("pair", "batch"),
                [(4 * s + b, 2 * b + (s ^ k)) for s in range(2) for b in range(4)],
            )
            for k in range(2)
        ]
        total = jnp.stack([jnp.where(x == 0, sent[0], sent[1]), jnp.where(x == 0, sent[1], sent[0])])
        return lax.rsqrt(total / model + EPS) / SHRINK

    def by_y(mine, other, axis):
        return jnp.stack([jnp.where(y == 0, mine, other), jnp.where(y == 0, other, mine)], axis)

    def swapped(value):
        return lax.ppermute(value, "pair", CORE_SWAP)

    def half_columns(weight, *earlier):
        return lax.dynamic_slice_in_dim(weight, after(core, *earlier) * width, width, 1)

    def dot(left, weight):
        return jnp.dot(left.reshape(-1, block), weight, preferred_element_type=jnp.float32)

    def line_parts():
        mine = lax.dynamic_slice_in_dim(gained, x * block, block, 2)
        other = lax.ppermute(
            lax.dynamic_slice_in_dim(gained, (1 - x) * block, block, 2), "batch", X_SWAP
        )
        own = jnp.stack([jnp.where(x == 0, mine, other), jnp.where(x == 0, other, mine)])
        own = after(own, squares)

        def up(value, k):
            return lax.ppermute(value, "vocab", [(z, z + 1) for z in range(k - 1, vocab - 1)])

        def down(value, k):
            return lax.ppermute(value, "vocab", [(z + 1, z) for z in range(vocab - k)])

        below, above = [own, up(own, 1)], [own, down(own, 1)]

        def quarter(place, reach, least=0):
            part = below[least]
            if least:
                part = jnp.where(level > place, part, above[least])
            for k in range(least + 1, reach + 1):
                part = jnp.where(level - place == k, below[k], part)
                part = jnp.where(place - level == k, above[k], part)
            return part

        first = level // 2
        scale = row_scale(own)
        below[1], above[1] = after(below[1], scale), after(above[1], scale)
        near_sent = quarter(1 - y + 2 * first, 1)
        got_near = lax.ppermute(near_sent, "batch", Y_SWAP)
        below.append(up(below[1], 2))
        above.append(down(above[1], 2))
        keep_near = (core ^ first) == 0
        kept, taken = half_columns(head_weight, near_sent), half_columns(take, near_sent)
        near_weight, far_weight = lax.optimization_barrier(
            (jnp.where(keep_near, kept, taken), jnp.where(keep_near, taken, kept))
        )
        ready = (got_near, near_weight, far_weight)
        below[2], above[2] = after(below[2], *ready), after(above[2], *ready)
        near = by_y(quarter(y + 2 * first, 1), after(got_near, below[2], above[2]), 0)
        swapped_near = swapped(near)

        far = 1 - y + 2 * (1 - first)
        pairs = [(b * vocab + z, (b ^ 2) * vocab + z) for b in range(4) for z in range(vocab)]
        lone = [b * vocab + (vocab - 1) * (b // 2) for b in range(4)]
        early = [pair for pair in pairs if pair[0] not in lone]
        got_early = lax.ppermute(quarter(far, 2, 1), ("batch", "vocab"), early)
        mine_early = lax.optimization_barrier(quarter(y + 2 * (1 - first), 2, 1))
        is_late = (level == 0) & (y == 1) | (level == vocab - 1) & (y == 0)
        near_part = dot(near, near_weight)
        sent = after(own, below[2], above[2])
        ends = []
        for cross in (0, 2):
            moves = []
            for place in lone:
                b, z = divmod(place, vocab)
                moves.append(((b ^ cross) * vocab + z, b * vocab + vocab - 1 - z))
            ends.append(lax.ppermute(sent, ("batch", "vocab"), sorted(moves)))
        mine_late, got_late, got_early, _ = lax.optimization_barrier(
            (ends[0], ends[1], got_early, near_part)
        )
        far = by_y(
            jnp.where(is_late, mine_late, mine_early), jnp.where(is_late, got_late, got_early), 0
        )
        swapped_far = swapped(far)

        def halves(near, left):
            middle = width // 2
            high = near[:, middle:] + dot(left, far_weight[:, middle:])
            low = near[:, :middle] + dot(after(left, high), far_weight[:, :middle])
            return low, high

        def own_part():
            return halves(near_part, far)

        def other_part(*earlier):
            left = after(swapped_far, *earlier)
            return halves(dot(swapped_near, near_weight), left)

        return (own_part, other_part), scale

    def gathered_parts():
        near_weight, far_weight = half_columns(head_weight), half_columns(take)
        whole = lax.all_gather(gained, "vocab", axis=2, tiled=True)
        whole = whole.reshape(2, seg, 2, 4, block).transpose(3, 2, 0, 1, 4)
        whole = lax.all_to_all(whole, "batch", split_axis=0, concat_axis=0)
        whole = whole.reshape(2, 2, 2, 2, seg, block).transpose(2, 0, 1, 3, 4, 5)
        swapped_whole = swapped(whole)

        def part(left):
            near, far = pick(left, core, 0), pick(left, 1 - core, 0)
            found = dot(near, near_weight) + dot(far, far_weight)
            return found[:, : width // 2], found[:, width // 2 :]

        return (lambda: part(whole), lambda *earlier: part(after(swapped_whole, *earlier))), row_scale()

    lined = depth == 2 * block and vocab == 4
    parts, scale = line_parts() if lined else gathered_parts()
    kept, sends = [], []
    for part in parts:
        low, high = (
            (half * SHRINK).reshape(2, 2, 2, seg, width // 2)
            for half in part(*(sends[-1] if sends else ()))
        )
        kept.append((pick(low, x, 2), pick(high, y, 1)))
        sends.append(
            (pick(low, 1 - x, 2).astype(SUM_TYPE), pick(high, 1 - y, 1).astype(SUM_TYPE))
        )
    halfway, more_sends = [], []
    for i in range(2):
        away_x = lax.ppermute(sends[i][0], "batch", X_SWAP)
        away_y = lax.ppermute(sends[i][1], "batch", Y_SWAP)
        if i == 0:
            away_x, away_y = after(away_x, *sends[1]), after(away_y, *sends[1])
        sum_x = kept[i][0] + away_x.astype(jnp.float32)
        sum_y = kept[i][1] + away_y.astype(jnp.float32)
        halfway.append((pick(sum_x, y, 1), pick(sum_y, x, 1)))
        more_sends.append(
            (pick(sum_x, 1 - y, 1).astype(SUM_TYPE), pick(sum_y, 1 - x, 1).astype(SUM_TYPE))
        )
    mine, theirs = [], []
    for i in range(2):
        next_y = lax.ppermute(more_sends[i][0], "batch", Y_SWAP)
        next_x = lax.ppermute(more_sends[i][1], "batch", X_SWAP)
        if i == 0:
            next_y, next_x = after(next_y, *more_sends[1]), after(next_x, *more_sends[1])
        sums = jnp.concatenate(
            [
                halfway[i][0] + next_y.astype(jnp.float32),
                halfway[i][1] + next_x.astype(jnp.float32),
            ],
            axis=-1,
        ).astype(SUM_TYPE)
        mine.append(pick(sums, core, 0))
        theirs.append(swapped(pick(sums, 1 - core, 0)))

    def scores(own, other, got_own, got_other, gain):
        low = jnp.where(core == 0, own, got_own)
        high = jnp.where(core == 0, got_other, other)
        return jnp.concatenate([low, high], axis=1).astype(jnp.float32) * gain[:, None]

    cond = scores(mine[0], mine[1], theirs[0], theirs[1], scale[0])
    uncond = scores(mine[1], mine[0], theirs[1], theirs[0], scale[1])
    guided = GUIDE * cond + (1.0 - GUIDE) * uncond

    def stats(values):
        peak = jnp.max(values, axis=1)
        return peak, jnp.sum(jnp.exp(values - peak[:, None]), axis=1)

    peak_c, sum_c = stats(cond)
    peak_g, sum_g = stats(guided)
    own = jnp.stack([peak_c, peak_g, sum_c, sum_g])
    every = jnp.stack(
        [own]
        + [
            shifted(own, k) for k in range(1, vocab)
        ]
    )
    top = jnp.max(every[:, :2], axis=0)
    total = jnp.sum(every[:, 2:] * jnp.exp(every[:, :2] - top[None]), axis=0)
    norm = top + jnp.log(total)
    return (guided - norm[1][:, None], cond - norm[0][:, None])


def solution(mesh):
    in_specs = (P("pair", "batch", "vocab"), P("vocab"), P(("pair", "batch"), "vocab"))
    out_specs = (P(("pair", "batch"), "vocab"), P(("pair", "batch"), "vocab"))
    return jax.shard_map(
        on_device, mesh=mesh, in_specs=in_specs, out_specs=out_specs, check_vma=False
    )
```
